32 devices in a mesh: dp: 16 (over z, y, x), head: 2 (over core).
Axes of the slice: x: 2, y: 2, z: 4, core: 2. Of those that a mesh axis runs over, the one named last changes fastest.
Arguments:
- source_copy: bfloat16 [128, 512, 512], P('dp', 'head'), may hold values from -6 to 6
- target_embed: bfloat16 [128, 512, 512], P('dp', 'head'), may hold values from -6 to 6
- memory: bfloat16 [128, 512, 512], P('dp', 'head'), may hold values from -6 to 6
- tgt_segments: int32 [128, 512], P('dp'), may hold values from 0 to 15, never falling along the last dimension, each value on 1 to 128 neighbouring positions
- src_segments: int32 [128, 512], P('dp'), may hold values from 0 to 15, never falling along the last dimension, each value on 1 to 128 neighbouring positions
- hamming: int32 [128, 16], P('dp'), may hold values from 0 to 64
- priority: int32 [128, 512], P('dp'), may hold values from 0 to 63
- cotangent: bfloat16 [128, 512, 512], P('dp', 'head'), may hold values from -6 to 6
- self_qkv: bfloat16 [3, 512, 512], P(None, None, 'head'), may hold values from -0.25 to 0.25
- self_out: bfloat16 [512, 512], P('head'), may hold values from -1.5 to 1.5
- cross_q: bfloat16 [512, 512], P(None, 'head'), may hold values from -0.25 to 0.25
- cross_kv: bfloat16 [2, 512, 512], P(None, None, 'head'), may hold values from -0.25 to 0.25
- cross_out: bfloat16 [512, 512], P('head'), may hold values from -1.5 to 1.5
- ffn_in: bfloat16 [512, 2048], P(None, 'head'), may hold values from -0.25 to 0.25
- ffn_out: bfloat16 [2048, 512], P('head'), may hold values from -0.125 to 0.125
- head_bias: bfloat16 [4, 512], P(None, 'head'), may hold values from -1.75 to 1.75
- ffn_bias: bfloat16 [2048], P('head'), may hold values from -1.75 to 1.75
- out_bias: bfloat16 [3, 512], replicated, may hold values from -1.75 to 1.75
- norm_gain: bfloat16 [3, 512], replicated, may hold values from 0.5 to 1.5
- norm_shift: bfloat16 [3, 512], replicated, may hold values from -1.75 to 1.75
Outputs:
- first_out: bfloat16 [128, 512, 512], P('dp', 'head')
- second_out: bfloat16 [128, 512, 512], P('dp', 'head')
- input_grad: bfloat16 [128, 512, 512], P('dp', 'head')
- memory_grad: bfloat16 [128, 512, 512], P('dp', 'head')
- self_qkv_grad: float32 [3, 512, 512], P(None, None, 'head')
- self_out_grad: float32 [512, 512], P('head')
- cross_q_grad: float32 [512, 512], P(None, 'head')
- cross_kv_grad: float32 [2, 512, 512], P(None, None, 'head')
- cross_out_grad: float32 [512, 512], P('head')
- ffn_in_grad: float32 [512, 2048], P(None, 'head')
- ffn_out_grad: float32 [2048, 512], P('head')
- head_bias_grad: float32 [4, 512], P(None, 'head')
- ffn_bias_grad: float32 [2048], P('head')
- out_bias_grad: float32 [3, 512], replicated
- gain_grad: float32 [3, 512], replicated
- shift_grad: float32 [3, 512], replicated
The draws below stay inside these ranges and needn't reach their ends.
Inputs may be any that keep to these rules, and one draw needn't show every extreme that they name: `hamming`: one count for each sentence number of a row; a position is glanced when its priority level is below its sentence's count. A priority level of each target position, drawn independently, ties allowed.
All inputs are finite; a program needn't handle non-finite values.
Results may differ from the reference program's by a relative error of at most 0.034.
Values may be sent and summed in bfloat16 or wider, within the bound.
A program may use at most 256 MiB of HBM per device.

```python
import math
import jax
import jax.numpy as jnp
import numpy as np
from jax import lax

D = 512
HEADS = 8
HEAD_DIM = 64
FF = 2048
LEN = 512
SEGS = 16
SEG_MOST = 128
PRIORITY = 64
BATCH = 128


def touch_ends(values, own_key, least, top_value):
    longest = values.shape.index(max(values.shape))
    spots = []
    for shift in (0, 1):
        where = [jax.random.randint(jax.random.fold_in(own_key, axis), (), 0, length) for axis, length in enumerate(values.shape)]
        where[longest] = (where[longest] + shift) % values.shape[longest]
        spots.append(tuple(where))
    return values.at[spots[0]].set(least).at[spots[1]].set(top_value)


def levels(stream_key, dims, split, smallest, top_value):
    loudness, own = 1.0, jax.random.fold_in(stream_key, 6)
    for position, blocks in split:
        steps = jnp.exp(jax.random.uniform(jax.random.fold_in(own, position), (blocks,), jnp.float32, smallest / len(split), top_value / len(split)))
        loudness = loudness * jnp.repeat(steps, dims[position] // blocks).reshape([-1 if axis == position else 1 for axis in range(len(dims))])
    return loudness


def profile(number_of, total, most, slope):
    portions = [(1 << 20) // math.isqrt(standing ** slope) + 1 for standing in range(2, number_of + 1)]
    spare, holding = total - most - (number_of - 1), [1] * (number_of - 1)
    while spare > 0:
        candidates = [i for i in range(number_of - 1) if holding[i] < most]
        mass, remaining = sum([portions[i] for i in candidates]), spare
        for i in candidates:
            extra = min(most - holding[i], max(1, remaining * portions[i] // mass), spare)
            holding[i] = holding[i] + extra
            spare = spare - extra
    return np.array([most] + holding)


def uneven(own_key, number_of, total, limit, slope):
    if number_of == 2:
        one = jax.random.randint(own_key, (), max(1, total - limit), min(limit, total - 1) + 1)
        return jnp.stack([one, total - one])
    lengths = jnp.asarray(profile(number_of, total, limit, slope), jnp.int32)
    twos = (number_of - 1) // 2
    donor, receiver = lengths[1:1 + 2 * twos:2], lengths[2:2 + 2 * twos:2]
    room = jnp.minimum(donor - 1, limit - receiver)
    moved = jax.random.randint(jax.random.fold_in(own_key, 1), (twos,), 0, 1 << 20) % (room + 1)
    lengths = lengths.at[1:1 + 2 * twos:2].set(donor - moved).at[2:2 + 2 * twos:2].set(receiver + moved)
    return lengths[jax.random.permutation(jax.random.fold_in(own_key, 2), number_of)]


def noise(own_key, dims, scale, limit, cuts=(), kind=jnp.bfloat16):
    result = jax.random.normal(own_key, dims, jnp.float32) * scale
    if len(cuts) > 0:
        result = levels(own_key, dims, cuts, -0.22, 0.18) * result
    return jnp.clip(result, min=-limit, max=limit).astype(kind)


def setup_inputs(seed: int = 0) -> dict:
    arg_keys = jax.random.split(jax.random.key(seed), 21)
    return {
        "source_copy": noise(arg_keys[0], (BATCH, LEN, D), 1.0, 6.0, ((0, 16), (1, 2))),
        "target_embed": noise(arg_keys[1], (BATCH, LEN, D), 1.0, 6.0, ((0, 16), (1, 2))),
        "memory": noise(arg_keys[2], (BATCH, LEN, D), 1.0, 6.0, ((0, 16), (1, 2))),
        "tgt_segments": jax.vmap(lambda own: jnp.searchsorted(jnp.cumsum(uneven(own, SEGS, LEN, SEG_MOST, 0)), jnp.arange(LEN), side="right"))(jax.random.split(arg_keys[3], BATCH)).reshape((BATCH, LEN)).astype(jnp.int32),
        "src_segments": jax.vmap(lambda own: jnp.searchsorted(jnp.cumsum(uneven(own, SEGS, LEN, SEG_MOST, 0)), jnp.arange(LEN), side="right"))(jax.random.split(arg_keys[4], BATCH)).reshape((BATCH, LEN)).astype(jnp.int32),
        "hamming": touch_ends(jax.random.randint(arg_keys[5], (BATCH, SEGS), 0, PRIORITY + 1), jax.random.fold_in(arg_keys[5], 1), 0, PRIORITY).astype(jnp.int32),
        "priority": touch_ends(jax.random.randint(arg_keys[6], (BATCH, LEN), 0, PRIORITY), jax.random.fold_in(arg_keys[6], 1), 0, PRIORITY - 1).astype(jnp.int32),
        "cotangent": noise(arg_keys[7], (BATCH, LEN, D), 1.0, 6.0, ((0, 16), (1, 2))),
        "self_qkv": noise(arg_keys[8], (3, D, D), D ** -0.5, 0.25, ((2, 2),)),
        "self_out": noise(arg_keys[9], (D, D), (max(D // 32, 1)) ** -0.5, 1.5, ((0, 2),)),
        "cross_q": noise(arg_keys[10], (D, D), D ** -0.5, 0.25, ((1, 2),)),
        "cross_kv": noise(arg_keys[11], (2, D, D), D ** -0.5, 0.25, ((2, 2),)),
        "cross_out": noise(arg_keys[12], (D, D), (max(D // 32, 1)) ** -0.5, 1.5, ((0, 2),)),
        "ffn_in": noise(arg_keys[13], (D, FF), D ** -0.5, 0.25, ((1, 2),)),
        "ffn_out": noise(arg_keys[14], (FF, D), FF ** -0.5, 0.125, ((0, 2),)),
        "head_bias": noise(arg_keys[15], (4, D), 0.3, 1.75, ((1, 2),)),
        "ffn_bias": noise(arg_keys[16], (FF,), 0.3, 1.75, ((0, 2),)),
        "out_bias": noise(arg_keys[17], (3, D), 0.3, 1.75),
        "norm_gain": jnp.clip(1.0 + 0.1 * jax.random.normal(arg_keys[18], (3, D), jnp.float32), 0.5, 1.5).astype(jnp.bfloat16),
        "norm_shift": noise(arg_keys[19], (3, D), 0.3, 1.75),
    }


@jax.custom_vjp
def low(v):
    return lax.optimization_barrier(v.astype(jnp.bfloat16)).astype(jnp.float32)

@jax.custom_vjp
def low_back(v):
    return v

def low_keep(v):
    return (low(v), None)

def low_pass(kept, grad):
    return (grad,)

def back_keep(v):
    return (v, None)

def back_low(kept, grad):
    return (low(grad),)
low.defvjp(low_keep, low_pass)
low_back.defvjp(back_keep, back_low)
exact_mode = lax.Precision.HIGHEST

def product(left, right):
    return jnp.matmul(left, right, precision=exact_mode)

def norm_rows(sums, gain_row, shift_row):
    row_mean = lax.optimization_barrier(jnp.mean(sums, axis=-1, keepdims=True))
    centred = sums - row_mean
    spread = lax.optimization_barrier(jnp.mean(centred * centred, axis=-1, keepdims=True))
    return centred * lax.rsqrt(spread + 1e-05) * gain_row + shift_row

def attend_row(queries, key_rows, value_rows, query_seg, key_seg):
    factor = HEAD_DIM ** (-0.5)
    scores = jnp.einsum('qhd,khd->hqk', queries, key_rows, precision=exact_mode) * factor
    scores = low_back(scores)
    same_doc = query_seg[:, None] == key_seg[None, :]
    masked = jnp.where(same_doc[None], scores, -1e+30)
    log_total = jax.nn.logsumexp(masked, axis=-1, keepdims=True)
    probs_low = low(jnp.exp(masked - log_total))
    return jnp.einsum('hqk,khd->qhd', probs_low, value_rows, precision=exact_mode)

def split_heads(matrix):
    return matrix.reshape(matrix.shape[:-1] + (HEADS, HEAD_DIM))

def attend_all(queries, key_rows, value_rows, query_seg, key_seg):

    def one_row(row_items):
        return attend_row(row_items[0], row_items[1], row_items[2], row_items[3], row_items[4])
    heads_out = lax.map(jax.checkpoint(one_row), (split_heads(queries), split_heads(key_rows), split_heads(value_rows), query_seg, key_seg))
    return heads_out.reshape(queries.shape)

def layer(inputs, memory, tgt_seg, src_seg, params):
    self_qkv, self_out, cross_q, cross_kv, cross_out, ffn_in, ffn_out, head_bias, ffn_bias, out_bias, norm_gain, norm_shift = params
    queries = low_back(low(product(inputs, self_qkv[0]) + head_bias[0]))
    key_rows = low_back(low(product(inputs, self_qkv[1])))
    value_rows = low_back(low(product(inputs, self_qkv[2]) + head_bias[1]))
    context = low_back(low(attend_all(queries, key_rows, value_rows, tgt_seg, tgt_seg)))
    attended = low_back(product(context, self_out) + out_bias[0])
    first_norm = norm_rows(inputs + attended, norm_gain[0], norm_shift[0])
    first_low = low(first_norm)
    cross_queries = low_back(low(product(first_low, cross_q) + head_bias[2]))
    cross_keys = low_back(low(product(memory, cross_kv[0])))
    cross_values = low_back(low(product(memory, cross_kv[1]) + head_bias[3]))
    cross_context = low_back(low(attend_all(cross_queries, cross_keys, cross_values, tgt_seg, src_seg)))
    crossed = low_back(product(cross_context, cross_out) + out_bias[1])
    second_norm = norm_rows(first_norm + crossed, norm_gain[1], norm_shift[1])
    second_low = low(second_norm)
    hidden_pre = low_back(product(second_low, ffn_in) + ffn_bias)
    hidden = low_back(low(jax.nn.gelu(hidden_pre, approximate=False)))
    fed = low_back(product(hidden, ffn_out) + out_bias[2])
    return norm_rows(second_norm + fed, norm_gain[2], norm_shift[2])

def reference(source_copy, target_embed, memory, tgt_segments, src_segments, hamming, priority, cotangent, self_qkv, self_out, cross_q, cross_kv, cross_out, ffn_in, ffn_out, head_bias, ffn_bias, out_bias, norm_gain, norm_shift):
    limits = jnp.take_along_axis(hamming, tgt_segments, axis=1)
    mixed = jnp.where((priority < limits)[:, :, None], target_embed, source_copy)
    params = tuple((weight.astype(jnp.float32) for weight in (self_qkv, self_out, cross_q, cross_kv, cross_out, ffn_in, ffn_out, head_bias, ffn_bias, out_bias, norm_gain, norm_shift)))
    group_rows = 4 if BATCH % 4 == 0 else 1
    step_count = BATCH // group_rows

    def split_rows(array):
        return array.reshape((step_count, group_rows) + array.shape[1:])

    def one_step(totals, step_items):
        source_rows, mixed_rows, memory_rows, tgt_rows, src_rows, cot_rows = step_items
        memory_float = memory_rows.astype(jnp.float32)
        first = layer(source_rows.astype(jnp.float32), memory_float, tgt_rows, src_rows, params)

        def second_pass(inputs, memory_in, weights):
            return layer(inputs, memory_in, tgt_rows, src_rows, weights)
        second, pull = jax.vjp(second_pass, mixed_rows.astype(jnp.float32), memory_float, params)
        input_grad, memory_grad, weight_grads = pull(cot_rows.astype(jnp.float32))
        totals = jax.tree.map(lambda left, right: left + right, totals, weight_grads)
        return (totals, (first.astype(jnp.bfloat16), second.astype(jnp.bfloat16), input_grad.astype(jnp.bfloat16), memory_grad.astype(jnp.bfloat16)))
    zeros = jax.tree.map(jnp.zeros_like, params)
    totals, stacked = lax.scan(one_step, zeros, (split_rows(source_copy), split_rows(mixed), split_rows(memory), split_rows(tgt_segments), split_rows(src_segments), split_rows(cotangent)))

    def join_rows(array):
        return array.reshape((BATCH,) + array.shape[2:])
    return (join_rows(stacked[0]), join_rows(stacked[1]), join_rows(stacked[2]), join_rows(stacked[3]), totals[0], totals[1], totals[2], totals[3], totals[4], totals[5], totals[6], totals[7], totals[8], totals[9], totals[10], totals[11])
```

```python
import functools

import jax
import jax.numpy as jnp
import numpy as np
from jax import lax
from jax.experimental import pallas as pl
from jax.experimental.pallas import tpu as pltpu
from jax.sharding import PartitionSpec as P

HEAD_DIM = 64
PAIR = 2 * HEAD_DIM
TILE = 128
WINDOW = 256
FAR = -1e30
F32 = jnp.float32
BF16 = jnp.bfloat16
VMEM_BYTES = 60 * 1024 * 1024


def dot_nn(left, right):
    return lax.dot_general(left, right, (((1,), (0,)), ((), ())), preferred_element_type=F32)


def dot_nt(left, right):
    return lax.dot_general(left, right, (((1,), (1,)), ((), ())), preferred_element_type=F32)


def norm_stats(sums):
    row_mean = jnp.mean(sums, axis=-1, keepdims=True)
    centred = sums - row_mean
    spread = jnp.mean(centred * centred, axis=-1, keepdims=True)
    inverse = lax.rsqrt(spread + 1e-05)
    return centred * inverse, inverse


def norm_back(sums, gain_row, incoming):
    normed, inverse = norm_stats(sums)
    scaled = incoming * gain_row
    mean_one = jnp.mean(scaled, axis=-1, keepdims=True)
    mean_two = jnp.mean(scaled * normed, axis=-1, keepdims=True)
    grad = (scaled - mean_one - normed * mean_two) * inverse
    gain_part = jnp.sum(incoming * normed, axis=0, keepdims=True)
    shift_part = jnp.sum(incoming, axis=0, keepdims=True)
    return grad, gain_part, shift_part


def gelu_parts(pre):
    size = jnp.abs(pre) * 0.7071067811865476
    ratio = 1.0 / (1.0 + 0.3275911 * size)
    series = ratio * (
        0.254829592
        + ratio
        * (-0.284496736 + ratio * (1.421413741 + ratio * (-1.453152027 + ratio * 1.061405429)))
    )
    bell = jnp.exp(-(size * size))
    tail = 0.5 * series * bell
    phi = jnp.where(pre >= 0, 1.0 - tail, tail)
    return phi, bell * 0.3989422804014327


def each_tile(count, step):
    def one(index, carry):
        step(index)
        return carry

    lax.fori_loop(0, count, one, 0)


def window_loop(starts_ref, base, tiles, length, step):
    def one(tile):
        start = starts_ref[base + tile]

        @pl.when(start >= 0)
        def near():
            step(tile, pl.multiple_of(start, 16), min(WINDOW, length))

        if length > WINDOW:

            @pl.when(start < 0)
            def whole():
                step(tile, 0, length)

    each_tile(tiles, one)


def attend(q_ref, k_ref, v_ref, far_ref, near_ref, sides_ref, ctx_ref, lse_ref, starts_ref, base):
    length, width = q_ref.shape
    pairs = width // PAIR
    left, right = sides_ref[0], sides_ref[1]

    def step(tile, start, window):
        rows = pl.ds(pl.multiple_of(tile * TILE, TILE), TILE)
        keys = pl.ds(start, window)
        query_marks = far_ref[rows, :]
        key_marks = near_ref[keys, :]
        for pair in range(pairs):
            lanes = slice(pair * PAIR, (pair + 1) * PAIR)
            queries = q_ref[rows, lanes]
            stacked = jnp.concatenate(
                [
                    jnp.concatenate([queries * left, query_marks], axis=1),
                    jnp.concatenate([queries * right, query_marks], axis=1),
                ],
                axis=0,
            )
            key_side = jnp.concatenate([k_ref[keys, lanes], key_marks], axis=1)
            scores = dot_nt(key_side, stacked)
            peak = jnp.max(scores, axis=0, keepdims=True)
            weights = jnp.exp(scores - peak)
            total = jnp.sum(weights, axis=0, keepdims=True)
            mixed = dot_nn(v_ref[keys, lanes].T, weights.astype(BF16))
            share = 1.0 / total
            context = jnp.concatenate(
                [
                    mixed[:HEAD_DIM, :TILE] * share[:, :TILE],
                    mixed[HEAD_DIM:, TILE:] * share[:, TILE:],
                ],
                axis=0,
            )
            ctx_ref[rows, lanes] = context.T.astype(BF16)
            if lse_ref is not None:
                log_total = peak + jnp.log(total)
                lse_ref[tile, pl.ds(2 * pair, 1), :] = log_total[:, :TILE]
                lse_ref[tile, pl.ds(2 * pair + 1, 1), :] = log_total[:, TILE:]

    window_loop(starts_ref, base, length // TILE, length, step)


def three_parts(values):
    high = values.astype(BF16).astype(F32)
    rest = values - high
    middle = rest.astype(BF16).astype(F32)
    return high, middle, rest - middle


def attend_back(
    q_ref,
    k_ref,
    v_ref,
    far_ref,
    near_ref,
    sides_ref,
    own_ref,
    spread_ref,
    lse_ref,
    ctx_ref,
    dctx_ref,
    dq_ref,
    dk_ref,
    dv_ref,
    starts_ref,
    base,
):
    length, width = q_ref.shape
    pairs = width // PAIR
    heads = width // HEAD_DIM
    left, right = sides_ref[0], sides_ref[1]
    dk_ref[...] = jnp.zeros_like(dk_ref)
    dv_ref[...] = jnp.zeros_like(dv_ref)

    def step(tile, start, window):
        rows = pl.ds(pl.multiple_of(tile * TILE, TILE), TILE)
        keys = pl.ds(start, window)
        key_marks = near_ref[keys, :]
        high, middle, low = three_parts(-lse_ref[tile])
        stats = jnp.concatenate(
            [
                jnp.zeros((16, TILE), F32),
                high,
                middle,
                low,
                jnp.zeros((TILE - 16 - 3 * heads, TILE), F32),
            ],
            axis=0,
        )
        query_marks = far_ref[rows, :] + stats.T.astype(BF16)
        product = dctx_ref[rows, :].astype(F32) * ctx_ref[rows, :].astype(F32)
        product_high = product.astype(BF16)
        product_low = (product - product_high.astype(F32)).astype(BF16)
        delta = -(dot_nn(product_high, spread_ref[...]) + dot_nn(product_low, spread_ref[...]))
        high, middle, low = three_parts(delta)
        lane = lax.broadcasted_iota(jnp.int32, delta.shape, 1)
        grad_marks = jnp.where(
            lane < 16 + heads, high, jnp.where(lane < 16 + 2 * heads, middle, low)
        ).astype(BF16)
        for pair in range(pairs):
            lanes = slice(pair * PAIR, (pair + 1) * PAIR)
            queries = q_ref[rows, lanes]
            grads = dctx_ref[rows, lanes]
            key_rows = k_ref[keys, lanes]
            query_stack = jnp.concatenate([queries * left, queries * right], axis=0)
            grad_stack = jnp.concatenate([grads * left, grads * right], axis=0)
            own = (own_ref[2 * pair], own_ref[2 * pair + 1])
            query_side = jnp.concatenate(
                [
                    query_stack,
                    jnp.concatenate([query_marks * own[0], query_marks * own[1]], axis=0),
                ],
                axis=1,
            )
            grad_side = jnp.concatenate(
                [
                    grad_stack,
                    jnp.concatenate([grad_marks * own[0], grad_marks * own[1]], axis=0),
                ],
                axis=1,
            )
            probs = jnp.exp(dot_nt(jnp.concatenate([key_rows, key_marks], axis=1), query_side))
            probs_grad = dot_nt(
                jnp.concatenate([v_ref[keys, lanes], key_marks], axis=1), grad_side
            )
            scores_grad = (probs * probs_grad).astype(BF16)
            dk_ref[keys, lanes] += dot_nn(scores_grad, query_stack)
            dv_ref[keys, lanes] += dot_nn(probs.astype(BF16), grad_stack)
            turned = dot_nn(key_rows.T, scores_grad)
            turned = jnp.concatenate(
                [turned[:HEAD_DIM, :TILE], turned[HEAD_DIM:, TILE:]], axis=0
            )
            dq_ref[rows, lanes] = (turned.T * (HEAD_DIM**-0.5)).astype(BF16)

    window_loop(starts_ref, base, length // TILE, length, step)


def attention_kernel(
    starts_ref,
    x_ref,
    memory_ref,
    far_ref,
    near_self_ref,
    near_cross_ref,
    sides_ref,
    self_qkv_ref,
    self_out_ref,
    cross_q_ref,
    cross_kv_ref,
    cross_out_ref,
    head_bias_ref,
    out_bias_ref,
    gain_ref,
    shift_ref,
    q_ref,
    k_ref,
    v_ref,
    ctx_ref,
    lse_ref,
    r1_ref,
    a1_ref,
    q2_ref,
    k2_ref,
    v2_ref,
    ctx2_ref,
    lse2_ref,
    r2_ref,
    work_ref,
):
    row = pl.program_id(0)
    tiles = x_ref.shape[0] // TILE
    self_part(
        starts_ref,
        row,
        x_ref,
        far_ref,
        near_self_ref,
        sides_ref,
        self_qkv_ref,
        self_out_ref,
        head_bias_ref,
        out_bias_ref,
        gain_ref,
        shift_ref,
        q_ref,
        k_ref,
        v_ref,
        ctx_ref,
        lse_ref,
        r1_ref,
        a1_ref,
        work_ref,
    )
    k2_ref[...] = dot_nn(memory_ref[...], cross_kv_ref[0]).astype(BF16)
    v2_ref[...] = (dot_nn(memory_ref[...], cross_kv_ref[1]) + head_bias_ref[3:4, :]).astype(BF16)
    cross_part(
        starts_ref,
        pl.num_programs(0) * tiles + row * tiles,
        far_ref,
        near_cross_ref,
        sides_ref,
        cross_q_ref,
        cross_out_ref,
        head_bias_ref,
        out_bias_ref,
        a1_ref,
        q2_ref,
        k2_ref,
        v2_ref,
        ctx2_ref,
        lse2_ref,
        r2_ref,
        work_ref,
    )


def self_part(
    starts_ref,
    row,
    x_ref,
    far_ref,
    near_ref,
    sides_ref,
    self_qkv_ref,
    self_out_ref,
    head_bias_ref,
    out_bias_ref,
    gain_ref,
    shift_ref,
    q_ref,
    k_ref,
    v_ref,
    ctx_ref,
    lse_ref,
    r1_ref,
    a1_ref,
    work_ref,
):
    tiles = x_ref.shape[0] // TILE
    inputs = x_ref[...]
    queries = (dot_nn(inputs, self_qkv_ref[0]) + head_bias_ref[0:1, :]).astype(BF16)
    q_ref[...] = queries * jnp.asarray(HEAD_DIM**-0.5, BF16)
    k_ref[...] = dot_nn(inputs, self_qkv_ref[1]).astype(BF16)
    v_ref[...] = (dot_nn(inputs, self_qkv_ref[2]) + head_bias_ref[1:2, :]).astype(BF16)
    attend(
        q_ref, k_ref, v_ref, far_ref, near_ref, sides_ref, ctx_ref, lse_ref, starts_ref, row * tiles
    )
    work_ref[...] = dot_nn(ctx_ref[...], self_out_ref[...])

    def step(tile):
        rows = pl.ds(pl.multiple_of(tile * TILE, TILE), TILE)
        sums = x_ref[rows, :].astype(F32) + (work_ref[rows, :] + out_bias_ref[0:1, :])
        if r1_ref is not None:
            r1_ref[rows, :] = sums
        normed = norm_stats(sums)[0] * gain_ref[0:1, :] + shift_ref[0:1, :]
        work_ref[rows, :] = normed
        a1_ref[rows, :] = normed.astype(BF16)

    each_tile(tiles, step)


def cross_part(
    starts_ref,
    base,
    far_ref,
    near_ref,
    sides_ref,
    cross_q_ref,
    cross_out_ref,
    head_bias_ref,
    out_bias_ref,
    a1_ref,
    q2_ref,
    k2_ref,
    v2_ref,
    ctx2_ref,
    lse2_ref,
    r2_ref,
    work_ref,
):
    queries = (dot_nn(a1_ref[...], cross_q_ref[...]) + head_bias_ref[2:3, :]).astype(BF16)
    q2_ref[...] = queries * jnp.asarray(HEAD_DIM**-0.5, BF16)
    attend(
        q2_ref, k2_ref, v2_ref, far_ref, near_ref, sides_ref, ctx2_ref, lse2_ref, starts_ref, base
    )
    r2_ref[...] = work_ref[...] + (
        dot_nn(ctx2_ref[...], cross_out_ref[...]) + out_bias_ref[1:2, :]
    )


def feed_part(r2_ref, a2_ref, work_ref, ffn_in_ref, ffn_out_ref, ffn_bias_ref, gain_ref, shift_ref, keep):
    length = r2_ref.shape[0]
    hidden = ffn_in_ref.shape[1]

    def step(tile):
        rows = pl.ds(pl.multiple_of(tile * TILE, TILE), TILE)
        normed = norm_stats(r2_ref[rows, :])[0] * gain_ref[1:2, :] + shift_ref[1:2, :]
        work_ref[rows, :] = normed
        a2_ref[rows, :] = normed.astype(BF16)

    each_tile(length // TILE, step)
    chunk = 256
    for first in range(0, hidden, chunk):
        units = slice(first, first + chunk)
        pre = dot_nn(a2_ref[...], ffn_in_ref[:, units]) + ffn_bias_ref[:, units]
        phi, bell = gelu_parts(pre)
        active = (pre * phi).astype(BF16)
        if keep is not None:
            keep[0][:, units] = active
            keep[1][:, units] = (phi + pre * bell).astype(BF16)
        work_ref[...] += dot_nn(active, ffn_out_ref[units, :])


def feed_kernel(
    r2_ref,
    cot_ref,
    ffn_in_ref,
    ffn_out_ref,
    ffn_bias_ref,
    out_bias_ref,
    gain_ref,
    shift_ref,
    out_ref,
    a2_ref,
    g_ref,
    df_ref,
    du_ref,
    dr2_ref,
    do2_ref,
    small_ref,
    ffn_bias_grad_ref,
    slope_ref,
    work_ref,
):
    length = r2_ref.shape[0]
    hidden = ffn_in_ref.shape[1]
    feed_part(
        r2_ref,
        a2_ref,
        work_ref,
        ffn_in_ref,
        ffn_out_ref,
        ffn_bias_ref,
        gain_ref,
        shift_ref,
        (g_ref, slope_ref),
    )
    small_ref[...] = jnp.zeros_like(small_ref)

    def last_norm(tile):
        rows = pl.ds(pl.multiple_of(tile * TILE, TILE), TILE)
        sums = work_ref[rows, :] + out_bias_ref[2:3, :]
        normed, inverse = norm_stats(sums)
        out_ref[rows, :] = (normed * gain_ref[2:3, :] + shift_ref[2:3, :]).astype(BF16)
        grad, gain_part, shift_part = norm_back(
            sums, gain_ref[2:3, :], cot_ref[rows, :].astype(F32)
        )
        work_ref[rows, :] = grad
        low = grad.astype(BF16)
        df_ref[rows, :] = low
        small_ref[0:1, :] += gain_part
        small_ref[1:2, :] += shift_part
        small_ref[2:3, :] += jnp.sum(low.astype(F32), axis=0, keepdims=True)

    each_tile(length // TILE, last_norm)
    chunk = 256
    for first in range(0, hidden, chunk):
        units = slice(first, first + chunk)
        hidden_grad = dot_nt(df_ref[...], ffn_out_ref[units, :]).astype(BF16).astype(F32)
        pre_grad = (hidden_grad * slope_ref[:, units].astype(F32)).astype(BF16)
        du_ref[:, units] = pre_grad
        ffn_bias_grad_ref[0:1, units] = jnp.sum(pre_grad.astype(F32), axis=0, keepdims=True)
        work_ref[...] += dot_nt(pre_grad, ffn_in_ref[:, units])

    def middle_norm(tile):
        rows = pl.ds(pl.multiple_of(tile * TILE, TILE), TILE)
        grad, gain_part, shift_part = norm_back(
            r2_ref[rows, :], gain_ref[1:2, :], work_ref[rows, :]
        )
        dr2_ref[rows, :] = grad
        low = grad.astype(BF16)
        do2_ref[rows, :] = low
        small_ref[3:4, :] += gain_part
        small_ref[4:5, :] += shift_part
        small_ref[5:6, :] += jnp.sum(low.astype(F32), axis=0, keepdims=True)

    each_tile(length // TILE, middle_norm)


def cross_back_kernel(
    starts_ref,
    dr2_ref,
    do2_ref,
    q2_ref,
    k2_ref,
    v2_ref,
    ctx2_ref,
    lse2_ref,
    r1_ref,
    far_ref,
    near_ref,
    sides_ref,
    own_ref,
    spread_ref,
    cross_q_ref,
    cross_kv_ref,
    cross_out_ref,
    gain_ref,
    dq_ref,
    dk_low_ref,
    dv_low_ref,
    memory_grad_ref,
    dr1_ref,
    do_ref,
    small_ref,
    dctx_ref,
    dk_ref,
    dv_ref,
    work_ref,
):
    tiles = dr2_ref.shape[0] // TILE
    base = pl.num_programs(0) * tiles + pl.program_id(0) * tiles
    dctx_ref[...] = dot_nt(do2_ref[...], cross_out_ref[...]).astype(BF16)
    attend_back(
        q2_ref,
        k2_ref,
        v2_ref,
        far_ref,
        near_ref,
        sides_ref,
        own_ref,
        spread_ref,
        lse2_ref,
        ctx2_ref,
        dctx_ref,
        dq_ref,
        dk_ref,
        dv_ref,
        starts_ref,
        base,
    )
    dk_low_ref[...] = dk_ref[...].astype(BF16)
    dv_low_ref[...] = dv_ref[...].astype(BF16)
    memory_grad_ref[...] = (
        dot_nt(dk_low_ref[...], cross_kv_ref[0]) + dot_nt(dv_low_ref[...], cross_kv_ref[1])
    ).astype(BF16)
    work_ref[...] = dr2_ref[...] + dot_nt(dq_ref[...], cross_q_ref[...])
    small_ref[...] = jnp.zeros_like(small_ref)

    def first_norm(tile):
        rows = pl.ds(pl.multiple_of(tile * TILE, TILE), TILE)
        grad, gain_part, shift_part = norm_back(
            r1_ref[rows, :], gain_ref[0:1, :], work_ref[rows, :]
        )
        dr1_ref[rows, :] = grad
        low = grad.astype(BF16)
        do_ref[rows, :] = low
        small_ref[0:1, :] += gain_part
        small_ref[1:2, :] += shift_part
        small_ref[2:3, :] += jnp.sum(low.astype(F32), axis=0, keepdims=True)
        small_ref[3:4, :] += jnp.sum(dq_ref[rows, :].astype(F32), axis=0, keepdims=True)
        small_ref[4:5, :] += jnp.sum(dv_low_ref[rows, :].astype(F32), axis=0, keepdims=True)

    each_tile(tiles, first_norm)


def self_back_kernel(
    starts_ref,
    dr1_ref,
    do_ref,
    q_ref,
    k_ref,
    v_ref,
    ctx_ref,
    lse_ref,
    far_ref,
    near_ref,
    sides_ref,
    own_ref,
    spread_ref,
    self_qkv_ref,
    self_out_ref,
    dq_ref,
    dk_low_ref,
    dv_low_ref,
    input_grad_ref,
    small_ref,
    dctx_ref,
    dk_ref,
    dv_ref,
):
    tiles = dr1_ref.shape[0] // TILE
    dctx_ref[...] = dot_nt(do_ref[...], self_out_ref[...]).astype(BF16)
    attend_back(
        q_ref,
        k_ref,
        v_ref,
        far_ref,
        near_ref,
        sides_ref,
        own_ref,
        spread_ref,
        lse_ref,
        ctx_ref,
        dctx_ref,
        dq_ref,
        dk_ref,
        dv_ref,
        starts_ref,
        pl.program_id(0) * tiles,
    )
    dk_low_ref[...] = dk_ref[...].astype(BF16)
    dv_low_ref[...] = dv_ref[...].astype(BF16)
    input_grad_ref[...] = (
        dr1_ref[...]
        + (dot_nt(dq_ref[...], self_qkv_ref[0]) + dot_nt(dk_low_ref[...], self_qkv_ref[1]))
        + dot_nt(dv_low_ref[...], self_qkv_ref[2])
    ).astype(BF16)
    small_ref[...] = jnp.zeros_like(small_ref)

    def totals(tile):
        rows = pl.ds(pl.multiple_of(tile * TILE, TILE), TILE)
        small_ref[0:1, :] += jnp.sum(dq_ref[rows, :].astype(F32), axis=0, keepdims=True)
        small_ref[1:2, :] += jnp.sum(dv_low_ref[rows, :].astype(F32), axis=0, keepdims=True)

    each_tile(tiles, totals)


def first_pass_kernel(
    starts_ref,
    x_ref,
    k2_ref,
    v2_ref,
    far_ref,
    near_self_ref,
    near_cross_ref,
    sides_ref,
    self_qkv_ref,
    self_out_ref,
    cross_q_ref,
    cross_out_ref,
    ffn_in_ref,
    ffn_out_ref,
    head_bias_ref,
    ffn_bias_ref,
    out_bias_ref,
    gain_ref,
    shift_ref,
    out_ref,
    q_ref,
    k_ref,
    v_ref,
    ctx_ref,
    low_ref,
    r2_ref,
    work_ref,
):
    row = pl.program_id(0)
    tiles = x_ref.shape[0] // TILE
    self_part(
        starts_ref,
        row,
        x_ref,
        far_ref,
        near_self_ref,
        sides_ref,
        self_qkv_ref,
        self_out_ref,
        head_bias_ref,
        out_bias_ref,
        gain_ref,
        shift_ref,
        q_ref,
        k_ref,
        v_ref,
        ctx_ref,
        None,
        None,
        low_ref,
        work_ref,
    )
    cross_part(
        starts_ref,
        pl.num_programs(0) * tiles + row * tiles,
        far_ref,
        near_cross_ref,
        sides_ref,
        cross_q_ref,
        cross_out_ref,
        head_bias_ref,
        out_bias_ref,
        low_ref,
        q_ref,
        k2_ref,
        v2_ref,
        ctx_ref,
        None,
        r2_ref,
        work_ref,
    )
    feed_part(
        r2_ref,
        low_ref,
        work_ref,
        ffn_in_ref,
        ffn_out_ref,
        ffn_bias_ref,
        gain_ref,
        shift_ref,
        None,
    )

    def last_norm(tile):
        rows = pl.ds(pl.multiple_of(tile * TILE, TILE), TILE)
        sums = work_ref[rows, :] + out_bias_ref[2:3, :]
        out_ref[rows, :] = (
            norm_stats(sums)[0] * gain_ref[2:3, :] + shift_ref[2:3, :]
        ).astype(BF16)

    each_tile(tiles, last_norm)


def per_row(array):
    block = (None,) + array.shape[1:]
    zeros = (0,) * (len(array.shape) - 1)
    return pl.BlockSpec(block, lambda row, *_: (row,) + zeros)


def whole(array):
    zeros = (0,) * len(array.shape)
    return pl.BlockSpec(array.shape, lambda row, *_: zeros, pipeline_mode=pl.Buffered(1))


def call_rows(kernel, name, rows, scalars, row_args, fixed_args, outs, scratch, flops, order=None):
    args = tuple(row_args) + tuple(fixed_args)
    specs = [per_row(a) for a in row_args] + [whole(a) for a in fixed_args]
    if order is not None:
        args = tuple(args[i] for i in order)
        specs = [specs[i] for i in order]
    out_shapes = tuple(jax.ShapeDtypeStruct(shape, kind) for shape, kind in outs)
    moved = sum(a.size * a.dtype.itemsize for a in args)
    moved += sum(int(np.prod(s.shape)) * s.dtype.itemsize for s in out_shapes)
    return pl.pallas_call(
        kernel,
        grid_spec=pltpu.PrefetchScalarGridSpec(
            num_scalar_prefetch=len(scalars),
            grid=(rows,),
            in_specs=specs,
            out_specs=tuple(per_row(s) for s in out_shapes),
            scratch_shapes=[pltpu.VMEM(shape, kind) for shape, kind in scratch],
        ),
        out_shape=out_shapes,
        compiler_params=pltpu.CompilerParams(
            dimension_semantics=("arbitrary",), vmem_limit_bytes=VMEM_BYTES
        ),
        cost_estimate=pl.CostEstimate(flops=flops, bytes_accessed=moved, transcendentals=0),
        name=name,
    )(*scalars, *args)


def shifted(values, axis, size, step):
    return lax.ppermute(values, axis, [(i, (i + step) % size) for i in range(size)])


def by_origin(parts, me):
    count = len(parts)
    if count == 1:
        return parts
    if count == 2:
        return [
            jnp.where(me == 0, parts[0], parts[1]),
            jnp.where(me == 0, parts[1], parts[0]),
        ]
    stacked = jnp.stack(parts)
    return [
        lax.dynamic_index_in_dim(stacked, (me - origin) % count, 0, keepdims=False)
        for origin in range(count)
    ]


def gather_parts(values, axis, me, size):
    parts = [values] + [shifted(values, "head", size, step) for step in range(1, size)]
    return jnp.concatenate(by_origin(parts, me), axis=axis)


def trade_parts(values, split_axis, join_axis, me, size):
    share = values.shape[split_axis] // size
    parts = []
    for step in range(size):
        target = (me + step) % size
        part = lax.dynamic_slice_in_dim(values, target * share, share, split_axis)
        parts.append(part if step == 0 else shifted(part, "head", size, step))
    return jnp.concatenate(by_origin(parts, me), axis=join_axis)


def head_share(values, axis, me, size):
    share = values.shape[axis] // size
    total = None
    for step in range(size):
        target = (me + step) % size
        part = lax.dynamic_slice_in_dim(values, target * share, share, axis)
        if step > 0:
            part = shifted(part, "head", size, step)
        total = part.astype(F32) if total is None else total + part.astype(F32)
    return total.astype(BF16)


def dp_stages(dp_size, swapped):
    bits = dp_size.bit_length() - 1
    first = [(1 << b, 2) for b in range(min(2, bits))]
    if swapped:
        first = first[::-1]
    if bits > 2:
        first.append((4, 1 << (bits - 2)))
    return first


def dp_permute(values, dp_size, stride, count, step):
    def place(i):
        digit = (i // stride) % count
        return i + (((digit ^ step) - digit) * stride)

    return lax.ppermute(values, "dp", [(i, place(i)) for i in range(dp_size)])


def dp_total(values, dp_size, spot, swapped):
    stages = dp_stages(dp_size, swapped)
    for stride, count in stages:
        digit = (spot // stride) % count
        share = values.shape[0] // count
        total = lax.dynamic_slice_in_dim(values, digit * share, share, 0).astype(F32)
        for step in range(1, count):
            part = lax.dynamic_slice_in_dim(values, (digit ^ step) * share, share, 0)
            total = total + dp_permute(part, dp_size, stride, count, step).astype(F32)
        values = total.astype(BF16)
    for stride, count in stages[::-1]:
        digit = (spot // stride) % count
        share = values.shape[0]
        grown = jnp.zeros((share * count,) + values.shape[1:], values.dtype)
        grown = lax.dynamic_update_slice_in_dim(grown, values, digit * share, 0)
        for step in range(1, count):
            part = dp_permute(values, dp_size, stride, count, step)
            grown = lax.dynamic_update_slice_in_dim(grown, part, (digit ^ step) * share, 0)
        values = grown
    return values


def small_total(values, dp_size, head_size):
    stride = 1
    while stride < dp_size:
        values = values + dp_permute(values, dp_size, stride, 2, 1)
        stride *= 2
    total = values
    for step in range(1, head_size):
        total = total + shifted(values, "head", head_size, step)
    return total


def window_starts(query_segments, key_segments, window):
    rows, length = query_segments.shape
    tiles = query_segments.reshape(rows, length // TILE, TILE)
    first, last = tiles[:, :, 0], tiles[:, :, -1]
    before = jnp.sum(key_segments[:, None, :] < first[:, :, None], axis=2).astype(jnp.int32)
    after = jnp.sum(key_segments[:, None, :] <= last[:, :, None], axis=2).astype(jnp.int32)
    start = jnp.minimum((before // 16) * 16, key_segments.shape[1] - window)
    return jnp.where(after - start <= window, start, -1).reshape(-1)


def token_grad(left, right):
    return lax.dot_general(
        left, right, (((0, 1), (0, 1)), ((), ())), preferred_element_type=F32
    ).astype(BF16)


def constants(width, levels):
    heads = width // HEAD_DIM
    lane = np.arange(PAIR)
    sides = np.stack([lane < HEAD_DIM, lane >= HEAD_DIM])
    own = np.stack(
        [(lane < levels) | ((lane >= 16) & (lane < 16 + 3 * heads) & ((lane - 16) % heads == h)) for h in range(heads)]
    )
    feature = np.arange(width)
    spread = (
        (lane[None, :] >= 16)
        & (lane[None, :] < 16 + 3 * heads)
        & ((lane[None, :] - 16) % heads == feature[:, None] // HEAD_DIM)
    )
    widen = lambda a: np.broadcast_to(a[:, None, :], (a.shape[0], TILE, PAIR))
    ones = (lane >= 16) & (lane < 16 + 3 * heads)
    return (
        jnp.asarray(widen(sides), BF16),
        jnp.asarray(widen(own), BF16),
        jnp.asarray(spread, BF16),
        jnp.asarray(ones, BF16),
    )


def segment_marks(segments, levels, ones):
    lane = jnp.arange(PAIR, dtype=jnp.int32)
    same = segments[:, :, None] == lane[None, None, :]
    far = jnp.where(same | (lane >= levels)[None, None, :], 0.0, FAR).astype(BF16)
    near = jnp.where(same, 1.0, 0.0).astype(BF16)
    return far, near + ones[None, None, :]


def local_layer(source, mixed, memory, cotangent, tgt_segments, src_segments, levels, weights):
    (
        self_qkv,
        self_out,
        cross_q,
        cross_kv,
        cross_out,
        ffn_in,
        ffn_out,
        head_bias,
        ffn_bias,
        out_bias,
        gain,
        shift,
    ) = weights
    rows, length, width = mixed.shape
    hidden = ffn_in.shape[1]
    heads = width // HEAD_DIM
    tiles = length // TILE
    window = min(WINDOW, length)
    sides, own, spread, ones = constants(width, levels)
    far, near_self = segment_marks(tgt_segments, levels, ones)
    near_cross = segment_marks(src_segments, levels, ones)[1]
    starts = jnp.concatenate(
        [
            window_starts(tgt_segments, tgt_segments, window),
            window_starts(tgt_segments, src_segments, window),
        ]
    )
    wide_low = ((rows, length, width), BF16)
    wide = ((rows, length, width), F32)
    stats = ((rows, tiles, heads, TILE), F32)
    small = ((rows, 8, width), F32)
    square = 2 * rows * length * width * width
    scores = 2 * rows * length * window * width
    one_low = ((length, width), BF16)
    one = ((length, width), F32)
    (
        queries,
        key_rows,
        value_rows,
        context,
        totals,
        first_sum,
        first_low,
        cross_queries,
        cross_keys,
        cross_values,
        cross_context,
        cross_totals,
        second_sum,
    ) = call_rows(
        attention_kernel,
        "attention",
        rows,
        (starts,),
        (mixed, memory, far, near_self, near_cross),
        (
            sides,
            self_qkv,
            self_out,
            cross_q,
            cross_kv,
            cross_out,
            head_bias,
            out_bias,
            gain,
            shift,
        ),
        (
            wide_low,
            wide_low,
            wide_low,
            wide_low,
            stats,
            wide,
            wide_low,
            wide_low,
            wide_low,
            wide_low,
            wide_low,
            stats,
            wide,
        ),
        (one,),
        8 * square + 8 * scores,
    )
    (
        second_out,
        second_low,
        hidden_rows,
        fed_grad,
        pre_grad,
        second_in,
        crossed_grad,
        feed_small,
        ffn_bias_part,
    ) = call_rows(
        feed_kernel,
        "feed",
        rows,
        (),
        (second_sum, cotangent),
        (ffn_in, ffn_out, ffn_bias, out_bias, gain, shift),
        (
            wide_low,
            wide_low,
            ((rows, length, hidden), BF16),
            wide_low,
            ((rows, length, hidden), BF16),
            wide,
            wide_low,
            small,
            ((rows, 8, hidden), F32),
        ),
        (((length, hidden), BF16), one),
        4 * square * hidden // width,
    )
    ffn_in_grad = token_grad(second_low, pre_grad)
    ffn_out_grad = token_grad(hidden_rows, fed_grad)
    (
        cross_query_grad,
        cross_key_grad,
        cross_value_grad,
        memory_grad,
        first_in,
        attended_grad,
        cross_small,
    ) = call_rows(
        cross_back_kernel,
        "cross_back",
        rows,
        (starts,),
        (
            second_in,
            crossed_grad,
            cross_queries,
            cross_keys,
            cross_values,
            cross_context,
            cross_totals,
            first_sum,
            far,
            near_cross,
        ),
        (sides, own, spread, cross_q, cross_kv, cross_out, gain),
        (wide_low, wide_low, wide_low, wide_low, wide, wide_low, small),
        (one_low, one, one, one),
        4 * square + 10 * scores,
    )
    cross_q_grad = token_grad(first_low, cross_query_grad)
    cross_k_grad = token_grad(memory, cross_key_grad)
    cross_v_grad = token_grad(memory, cross_value_grad)
    cross_out_grad = token_grad(cross_context, crossed_grad)
    query_grad, key_grad, value_grad, input_grad, self_small = call_rows(
        self_back_kernel,
        "self_back",
        rows,
        (starts,),
        (
            first_in,
            attended_grad,
            queries,
            key_rows,
            value_rows,
            context,
            totals,
            far,
            near_self,
        ),
        (sides, own, spread, self_qkv, self_out),
        (wide_low, wide_low, wide_low, wide_low, small),
        (one_low, one, one),
        4 * square + 10 * scores,
    )
    q_grad = token_grad(mixed, query_grad)
    k_grad = token_grad(mixed, key_grad)
    v_grad = token_grad(mixed, value_grad)
    self_out_grad = token_grad(context, attended_grad)
    source, input_grad = lax.optimization_barrier((source, input_grad))
    (first_out,) = call_rows(
        first_pass_kernel,
        "first_pass",
        rows,
        (starts,),
        (source, cross_keys, cross_values, far, near_self, near_cross),
        (
            sides,
            self_qkv,
            self_out,
            cross_q,
            cross_out,
            ffn_in,
            ffn_out,
            head_bias,
            ffn_bias,
            out_bias,
            gain,
            shift,
        ),
        (wide_low,),
        (one_low, one_low, one_low, one_low, one_low, one, one),
        6 * square + 2 * square * hidden // width + 8 * scores,
    )
    feed_sums = jnp.sum(feed_small, axis=0)
    cross_sums = jnp.sum(cross_small, axis=0)
    self_sums = jnp.sum(self_small, axis=0)
    bias_sums = jnp.sum(ffn_bias_part[:, 0, :], axis=0).reshape(hidden // width, width)
    small_sums = jnp.concatenate(
        [
            self_sums[0:2],
            cross_sums[3:5],
            cross_sums[2:3],
            feed_sums[5:6],
            feed_sums[2:3],
            cross_sums[0:1],
            feed_sums[3:4],
            feed_sums[0:1],
            cross_sums[1:2],
            feed_sums[4:5],
            feed_sums[1:2],
            bias_sums,
        ],
        axis=0,
    )
    return (
        first_out,
        second_out,
        input_grad,
        memory_grad,
        (ffn_in_grad, ffn_out_grad),
        (cross_q_grad, cross_k_grad, cross_v_grad, cross_out_grad),
        (q_grad, k_grad, v_grad, self_out_grad),
        small_sums,
    )


def body(
    dp_size,
    head_size,
    source_copy,
    target_embed,
    memory,
    tgt_segments,
    src_segments,
    hamming,
    priority,
    cotangent,
    self_qkv,
    self_out,
    cross_q,
    cross_kv,
    cross_out,
    ffn_in,
    ffn_out,
    head_bias,
    ffn_bias,
    out_bias,
    norm_gain,
    norm_shift,
):
    me = lax.axis_index("head")
    spot = lax.axis_index("dp")
    levels = hamming.shape[1]
    held, share, width = source_copy.shape
    rows = held // head_size

    def own_positions(array):
        return lax.dynamic_slice_in_dim(array, me * share, share, 1)

    def own_rows(array):
        return lax.dynamic_slice_in_dim(array, me * rows, rows, 0)

    level = jnp.arange(levels, dtype=jnp.int32)
    chosen = own_positions(tgt_segments)[:, :, None] == level[None, None, :]
    limits = jnp.sum(jnp.where(chosen, hamming[:, None, :], 0), axis=2)
    glanced = own_positions(priority) < limits
    mixed_part = jnp.where(glanced[:, :, None], target_embed, source_copy)

    gather = functools.partial(gather_parts, me=me, size=head_size)
    trade = functools.partial(trade_parts, me=me, size=head_size)
    mixed = trade(mixed_part, 0, 1)
    self_qkv = gather(self_qkv, 2)
    self_out = gather(self_out, 0)
    memory_rows = trade(memory, 0, 1)
    cross_q = gather(cross_q, 1)
    cross_kv = gather(cross_kv, 2)
    cross_out = gather(cross_out, 0)
    head_bias = gather(head_bias, 1).astype(F32)
    ffn_bias = gather(ffn_bias[None, :], 1).astype(F32)
    ffn_in = gather(ffn_in, 1)
    ffn_out = gather(ffn_out, 0)
    cot_rows = trade(cotangent, 0, 1)
    source = trade(source_copy, 0, 1)
    (
        first_out,
        second_out,
        input_grad,
        memory_grad,
        feed_grads,
        cross_grads,
        self_grads,
        small_sums,
    ) = local_layer(
        source,
        mixed,
        memory_rows,
        cot_rows,
        own_rows(tgt_segments),
        own_rows(src_segments),
        levels,
        (
            self_qkv,
            self_out,
            cross_q,
            cross_kv,
            cross_out,
            ffn_in,
            ffn_out,
            head_bias,
            ffn_bias,
            out_bias.astype(F32),
            norm_gain.astype(F32),
            norm_shift.astype(F32),
        ),
    )

    def total(values, axis, swapped):
        return dp_total(head_share(values, axis, me, head_size), dp_size, spot, swapped).astype(F32)

    ffn_in_grad = total(feed_grads[0], 1, False)
    ffn_out_grad = total(feed_grads[1], 0, True)
    cross_q_grad = total(cross_grads[0], 1, False)
    cross_kv_grad = jnp.stack([total(cross_grads[1], 1, False), total(cross_grads[2], 1, True)])
    cross_out_grad = total(cross_grads[3], 0, True)
    self_qkv_grad = jnp.stack(
        [
            total(self_grads[0], 1, False),
            total(self_grads[1], 1, True),
            total(self_grads[2], 1, False),
        ]
    )
    self_out_grad = total(self_grads[3], 0, True)
    sums = small_total(small_sums, dp_size, head_size)
    part = width // head_size
    head_bias_grad = lax.dynamic_slice_in_dim(sums[0:4], me * part, part, 1)
    hidden = ffn_in.shape[1] // head_size
    ffn_bias_grad = lax.dynamic_slice_in_dim(sums[13:].reshape(-1), me * hidden, hidden, 0)

    def back(array):
        return trade(array, 1, 0)

    return (
        back(first_out),
        back(second_out),
        back(input_grad),
        back(memory_grad),
        self_qkv_grad,
        self_out_grad,
        cross_q_grad,
        cross_kv_grad,
        cross_out_grad,
        ffn_in_grad,
        ffn_out_grad,
        head_bias_grad,
        ffn_bias_grad,
        sums[4:7],
        sums[7:10],
        sums[10:13],
    )


def solution(mesh):
    return jax.shard_map(
        functools.partial(body, mesh.shape["dp"], mesh.shape["head"]),
        mesh=mesh,
        in_specs=(
            P("dp", "head", None),
            P("dp", "head", None),
            P("dp", "head", None),
            P("dp", None),
            P("dp", None),
            P("dp", None),
            P("dp", None),
            P("dp", "head", None),
            P(None, None, "head"),
            P("head", None),
            P(None, "head"),
            P(None, None, "head"),
            P("head", None),
            P(None, "head"),
            P("head", None),
            P(None, "head"),
            P("head"),
            P(),
            P(),
            P(),
        ),
        out_specs=(
            P("dp", "head", None),
            P("dp", "head", None),
            P("dp", "head", None),
            P("dp", "head", None),
            P(None, None, "head"),
            P("head", None),
            P(None, "head"),
            P(None, None, "head"),
            P("head", None),
            P(None, "head"),
            P("head", None),
            P(None, "head"),
            P("head"),
            P(),
            P(),
            P(),
        ),
        check_vma=False,
    )
```

```python
import functools

import jax
import jax.numpy as jnp
import numpy as np
from jax import lax
from jax.experimental import pallas as pl
from jax.experimental.pallas import tpu as pltpu
from jax.sharding import PartitionSpec as P

HEAD_DIM = 64
PAIR = 2 * HEAD_DIM
TILE = 128
WINDOW = 256
FAR = -1e30
F32 = jnp.float32
BF16 = jnp.bfloat16
VMEM_BYTES = 60 * 1024 * 1024


def dot_nn(left, right):
    return lax.dot_general(left, right, (((1,), (0,)), ((), ())), preferred_element_type=F32)


def dot_nt(left, right):
    return lax.dot_general(left, right, (((1,), (1,)), ((), ())), preferred_element_type=F32)


def norm_stats(sums):
    row_mean = jnp.mean(sums, axis=-1, keepdims=True)
    centred = sums - row_mean
    spread = jnp.mean(centred * centred, axis=-1, keepdims=True)
    inverse = lax.rsqrt(spread + 1e-05)
    return centred * inverse, inverse


def norm_back(normed, inverse, gain_row, incoming):
    scaled = incoming * gain_row
    mean_one = jnp.mean(scaled, axis=-1, keepdims=True)
    mean_two = jnp.mean(scaled * normed, axis=-1, keepdims=True)
    grad = (scaled - mean_one - normed * mean_two) * inverse
    gain_part = jnp.sum(incoming * normed, axis=0, keepdims=True)
    shift_part = jnp.sum(incoming, axis=0, keepdims=True)
    return grad, gain_part, shift_part


def gelu_parts(pre):
    ratio = pltpu.reciprocal(1.0 + 0.23164189015488 * jnp.abs(pre), approx=True)
    series = ratio * (
        0.127414796
        + ratio
        * (-0.142248368 + ratio * (0.7107068705 + ratio * (-0.7265760135 + ratio * 0.5307027145)))
    )
    bell = jnp.exp(-0.5 * (pre * pre))
    tail = series * bell
    return jnp.where(pre >= 0, 1.0 - tail, tail), bell


def each_tile(count, step):
    def one(index, carry):
        step(index)
        return carry

    lax.fori_loop(0, count, one, 0)


def tile_rows(tile):
    start = tile * TILE
    return pl.ds(start if isinstance(start, int) else pl.multiple_of(start, TILE), TILE)


def window_loop(starts_ref, base, tiles, length, step):
    starts = [starts_ref[base + tile] for tile in range(tiles)]
    least = functools.reduce(jnp.minimum, starts)
    window = min(WINDOW, length)

    @pl.when(least >= 0)
    def straight():
        for tile in range(tiles):
            step(tile, pl.multiple_of(starts[tile], 16), window)

    if length > WINDOW:

        @pl.when(least < 0)
        def mixed():
            def one(tile):
                start = starts_ref[base + tile]

                @pl.when(start >= 0)
                def near():
                    step(tile, pl.multiple_of(start, 16), window)

                @pl.when(start < 0)
                def whole():
                    step(tile, 0, length)

            each_tile(tiles, one)


def make_marks(segment_row, levels, heads):
    shape = (PAIR, segment_row.shape[1])
    level = lax.broadcasted_iota(jnp.int32, shape, 0)
    same = level == segment_row
    near = jnp.where(same | ((level >= 16) & (level < 16 + 3 * heads)), 1.0, 0.0)
    far = jnp.where(same | (level >= levels), 0.0, FAR)
    return far.T.astype(BF16), near.T.astype(BF16)


def attend(q_ref, k_ref, v_ref, far_ref, near_ref, sides_ref, ctx_ref, lse_ref, starts_ref, base):
    length, width = q_ref.shape
    pairs = range(width // PAIR)
    lanes = [slice(p * PAIR, (p + 1) * PAIR) for p in pairs]

    def step(tile, start, window):
        rows = tile_rows(tile)
        keys = pl.ds(start, window)
        left, right = sides_ref[0], sides_ref[1]
        query_marks = far_ref[rows, :]
        key_marks = near_ref[keys, :]
        stacked = []
        for p in pairs:
            queries = q_ref[rows, lanes[p]]
            stacked.append(
                jnp.concatenate(
                    [
                        jnp.concatenate([queries * left, query_marks], axis=1),
                        jnp.concatenate([queries * right, query_marks], axis=1),
                    ],
                    axis=0,
                )
            )
        scores = [
            dot_nt(jnp.concatenate([k_ref[keys, lanes[p]], key_marks], axis=1), stacked[p])
            for p in pairs
        ]
        peaks = [jnp.max(s, axis=0, keepdims=True) for s in scores]
        weights = [jnp.exp(s - m) for s, m in zip(scores, peaks)]
        totals = [jnp.sum(w, axis=0, keepdims=True) for w in weights]
        low = [w.astype(BF16) for w in weights]
        turned = [v_ref[keys, lanes[p]].T for p in pairs]
        mixed = [dot_nn(turned[p], low[p]) for p in pairs]
        shares = [pltpu.reciprocal(t, approx=True) for t in totals]
        context = [
            jnp.concatenate(
                [
                    mixed[p][:HEAD_DIM, :TILE] * shares[p][:, :TILE],
                    mixed[p][HEAD_DIM:, TILE:] * shares[p][:, TILE:],
                ],
                axis=0,
            )
            for p in pairs
        ]
        for p in pairs:
            ctx_ref[rows, lanes[p]] = context[p].T.astype(BF16)
        if lse_ref is not None:
            for p in pairs:
                log_total = peaks[p] + jnp.log(totals[p])
                lse_ref[tile, pl.ds(2 * p, 1), :] = log_total[:, :TILE]
                lse_ref[tile, pl.ds(2 * p + 1, 1), :] = log_total[:, TILE:]

    window_loop(starts_ref, base, length // TILE, length, step)


def three_parts(values):
    high = values.astype(BF16).astype(F32)
    rest = values - high
    middle = rest.astype(BF16).astype(F32)
    return high, middle, rest - middle


def attend_back(
    q_ref,
    k_ref,
    v_ref,
    far_ref,
    near_ref,
    sides_ref,
    own_ref,
    spread_ref,
    lse_ref,
    ctx_ref,
    dctx_ref,
    dq_ref,
    dk_ref,
    dv_ref,
    starts_ref,
    base,
):
    length, width = q_ref.shape
    pairs = range(width // PAIR)
    heads = width // HEAD_DIM
    lanes = [slice(p * PAIR, (p + 1) * PAIR) for p in pairs]
    dk_ref[...] = jnp.zeros_like(dk_ref)
    dv_ref[...] = jnp.zeros_like(dv_ref)

    def step(tile, start, window):
        rows = tile_rows(tile)
        keys = pl.ds(start, window)
        left, right = sides_ref[0], sides_ref[1]
        key_marks = near_ref[keys, :]
        high, middle, rest = three_parts(-lse_ref[tile])
        stats = jnp.concatenate(
            [
                jnp.zeros((16, TILE), F32),
                high,
                middle,
                rest,
                jnp.zeros((TILE - 16 - 3 * heads, TILE), F32),
            ],
            axis=0,
        )
        query_marks = far_ref[rows, :] + stats.T.astype(BF16)
        product = dctx_ref[rows, :].astype(F32) * ctx_ref[rows, :].astype(F32)
        product_high = product.astype(BF16)
        product_rest = (product - product_high.astype(F32)).astype(BF16)
        delta = -(dot_nn(product_high, spread_ref[...]) + dot_nn(product_rest, spread_ref[...]))
        high, middle, rest = three_parts(delta)
        lane = lax.broadcasted_iota(jnp.int32, delta.shape, 1)
        grad_marks = jnp.where(
            lane < 16 + heads, high, jnp.where(lane < 16 + 2 * heads, middle, rest)
        ).astype(BF16)
        query_stack, grad_stack, query_side, grad_side, key_rows = [], [], [], [], []
        for p in pairs:
            queries = q_ref[rows, lanes[p]]
            grads = dctx_ref[rows, lanes[p]]
            key_rows.append(k_ref[keys, lanes[p]])
            query_stack.append(jnp.concatenate([queries * left, queries * right], axis=0))
            grad_stack.append(jnp.concatenate([grads * left, grads * right], axis=0))
            one, two = own_ref[2 * p], own_ref[2 * p + 1]
            marks = jnp.concatenate([query_marks * one, query_marks * two], axis=0)
            query_side.append(jnp.concatenate([query_stack[p], marks], axis=1))
            marks = jnp.concatenate([grad_marks * one, grad_marks * two], axis=0)
            grad_side.append(jnp.concatenate([grad_stack[p], marks], axis=1))
        scores = [
            dot_nt(jnp.concatenate([key_rows[p], key_marks], axis=1), query_side[p]) for p in pairs
        ]
        probs_grad = [
            dot_nt(jnp.concatenate([v_ref[keys, lanes[p]], key_marks], axis=1), grad_side[p])
            for p in pairs
        ]
        probs = [jnp.exp(s) for s in scores]
        probs_low = [w.astype(BF16) for w in probs]
        scores_grad = [(probs[p] * probs_grad[p]).astype(BF16) for p in pairs]
        turned_keys = [key_rows[p].T for p in pairs]
        for p in pairs:
            dv_ref[keys, lanes[p]] += dot_nn(probs_low[p], grad_stack[p])
        for p in pairs:
            dk_ref[keys, lanes[p]] += dot_nn(scores_grad[p], query_stack[p])
        turned = [dot_nn(turned_keys[p], scores_grad[p]) for p in pairs]
        for p in pairs:
            both = jnp.concatenate(
                [turned[p][:HEAD_DIM, :TILE], turned[p][HEAD_DIM:, TILE:]], axis=0
            )
            dq_ref[rows, lanes[p]] = (both.T * (HEAD_DIM**-0.5)).astype(BF16)

    window_loop(starts_ref, base, length // TILE, length, step)


def self_part(
    r, x_ref, seg_ref, near_ref, far_ref, q_ref, k_ref, v_ref, ctx_ref, lse_ref, r1_ref, a1_ref, work_ref, levels
):
    tiles, width = x_ref.shape[0] // TILE, x_ref.shape[1]
    far, near = make_marks(seg_ref[...], levels, width // HEAD_DIM)
    far_ref[...] = far
    near_ref[...] = near
    bias = r.head_bias[...].astype(F32)
    inputs = x_ref[...]
    queries = (dot_nn(inputs, r.self_qkv[0]) + bias[0:1, :]).astype(BF16)
    q_ref[...] = queries * jnp.asarray(HEAD_DIM**-0.5, BF16)
    k_ref[...] = dot_nn(inputs, r.self_qkv[1]).astype(BF16)
    v_ref[...] = (dot_nn(inputs, r.self_qkv[2]) + bias[1:2, :]).astype(BF16)
    base = pl.program_id(0) * tiles
    attend(q_ref, k_ref, v_ref, far_ref, near_ref, r.sides, ctx_ref, lse_ref, r.starts, base)
    work_ref[...] = dot_nn(ctx_ref[...], r.self_out[...])
    out_bias = r.out_bias[0:1, :].astype(F32)
    gain, shift = r.gain[0:1, :].astype(F32), r.shift[0:1, :].astype(F32)

    def step(tile):
        rows = tile_rows(tile)
        sums = x_ref[rows, :].astype(F32) + (work_ref[rows, :] + out_bias)
        if r1_ref is not None:
            r1_ref[rows, :] = sums
        normed = norm_stats(sums)[0] * gain + shift
        work_ref[rows, :] = normed
        a1_ref[rows, :] = normed.astype(BF16)

    each_tile(tiles, step)


def cross_part(
    r, seg_ref, near_ref, far_ref, a1_ref, q2_ref, k2_ref, v2_ref, ctx2_ref, lse2_ref, r2_ref, work_ref, levels
):
    tiles, width = q2_ref.shape[0] // TILE, q2_ref.shape[1]
    near_ref[...] = make_marks(seg_ref[...], levels, width // HEAD_DIM)[1]
    bias = r.head_bias[...].astype(F32)
    queries = (dot_nn(a1_ref[...], r.cross_q[...]) + bias[2:3, :]).astype(BF16)
    q2_ref[...] = queries * jnp.asarray(HEAD_DIM**-0.5, BF16)
    base = (pl.num_programs(0) + pl.program_id(0)) * tiles
    attend(q2_ref, k2_ref, v2_ref, far_ref, near_ref, r.sides, ctx2_ref, lse2_ref, r.starts, base)
    r2_ref[...] = work_ref[...] + (
        dot_nn(ctx2_ref[...], r.cross_out[...]) + r.out_bias[1:2, :].astype(F32)
    )


def attention_kernel(levels, r):
    self_part(
        r, r.x, r.tgt, r.near, r.far, r.q, r.k, r.v, r.ctx, r.lse, r.r1, r.a1, r.work, levels
    )
    bias = r.head_bias[...].astype(F32)
    r.k2[...] = dot_nn(r.memory[...], r.cross_kv[0]).astype(BF16)
    r.v2[...] = (dot_nn(r.memory[...], r.cross_kv[1]) + bias[3:4, :]).astype(BF16)
    cross_part(
        r, r.src, r.near, r.far, r.a1, r.q2, r.k2, r.v2, r.ctx2, r.lse2, r.r2, r.work, levels
    )


def feed_part(r, r2_ref, a2_ref, work_ref, g_ref, slope_ref):
    length = r2_ref.shape[0]
    units = r.ffn_in[0].shape[1]
    chunk = min(256, units)
    gain, shift = r.gain[1:2, :].astype(F32), r.shift[1:2, :].astype(F32)

    def step(tile):
        rows = tile_rows(tile)
        normed = norm_stats(r2_ref[rows, :])[0] * gain + shift
        work_ref[rows, :] = normed
        a2_ref[rows, :] = normed.astype(BF16)

    each_tile(length // TILE, step)
    spots = [(j, first) for j in range(len(r.ffn_in)) for first in range(0, units, chunk)]

    def product(spot):
        j, first = spot
        cut = slice(first, first + chunk)
        return dot_nn(a2_ref[...], r.ffn_in[j][:, cut]) + r.ffn_bias[j][:, cut].astype(F32)

    following = product(spots[0])
    for index, (j, first) in enumerate(spots):
        pre = following
        if index + 1 < len(spots):
            following = product(spots[index + 1])
        phi, bell = gelu_parts(pre)
        cut = slice(j * units + first, j * units + first + chunk)
        g_ref[:, cut] = (pre * phi).astype(BF16)
        if slope_ref is not None:
            slope_ref[:, cut] = (phi + (pre * bell) * 0.3989422804014327).astype(BF16)
    fed = r.out_bias[2:3, :].astype(F32)
    for j in range(len(r.ffn_out)):
        fed = fed + dot_nn(g_ref[:, j * units : (j + 1) * units], r.ffn_out[j][...])
    work_ref[...] += fed


def add_grad(total_ref, left, right):
    total_ref[...] += dot_nn(left, right)


def start_totals(refs):
    @pl.when(pl.program_id(0) == 0)
    def clear():
        for ref in refs:
            ref[...] = jnp.zeros_like(ref)


def end_totals(pairs):
    @pl.when(pl.program_id(0) == pl.num_programs(0) - 1)
    def write():
        for total_ref, out_ref in pairs:
            share = out_ref.shape[2]
            for j in range(out_ref.shape[0]):
                out_ref[j] = total_ref[:, j * share : (j + 1) * share].astype(BF16)


def column_total(values):
    return jnp.sum(values.astype(F32), axis=0, keepdims=True)


def add_share(share_ref, row, values):
    share = share_ref.shape[2]
    for j in range(share_ref.shape[0]):
        share_ref[j, row : row + 1, :] += values[:, j * share : (j + 1) * share]


def feed_kernel(levels, r):
    length = r.r2.shape[0]
    units = r.ffn_in[0].shape[1]
    chunk = min(256, units)
    start_totals([r.in_total, r.out_total, r.common, r.shares])
    feed_part(r, r.r2, r.a2, r.work, r.g, r.slope)
    gain, shift = r.gain[...].astype(F32), r.shift[...].astype(F32)

    def last_norm(tile):
        rows = tile_rows(tile)
        normed, inverse = norm_stats(r.work[rows, :])
        r.second[rows, :] = (normed * gain[2:3, :] + shift[2:3, :]).astype(BF16)
        grad, gain_part, shift_part = norm_back(
            normed, inverse, gain[2:3, :], r.cot[rows, :].astype(F32)
        )
        r.work[rows, :] = grad
        low = grad.astype(BF16)
        r.df[rows, :] = low
        r.common[2:3, :] += column_total(low)
        r.common[5:6, :] += gain_part
        r.common[8:9, :] += shift_part

    each_tile(length // TILE, last_norm)
    spots = [(j, first) for j in range(len(r.ffn_in)) for first in range(0, units, chunk)]

    def product(spot):
        j, first = spot
        return dot_nt(r.df[...], r.ffn_out[j][first : first + chunk, :])

    share = r.shares.shape[2]
    following = product(spots[0])
    for index, (j, first) in enumerate(spots):
        hidden_grad = following.astype(BF16)
        if index + 1 < len(spots):
            following = product(spots[index + 1])
        cut = slice(j * units + first, j * units + first + chunk)
        pre_grad = (hidden_grad.astype(F32) * r.slope[:, cut].astype(F32)).astype(BF16)
        r.du[:, cut] = pre_grad
        sums = column_total(pre_grad)
        for piece in range(0, chunk, share):
            row = 4 + (first + piece) // share
            r.shares[j, row : row + 1, :] += sums[:, piece : piece + share]
    back = r.work[...]
    for j in range(len(r.ffn_in)):
        back = back + dot_nt(r.du[:, j * units : (j + 1) * units], r.ffn_in[j][...])
    r.work[...] = back

    def middle_norm(tile):
        rows = tile_rows(tile)
        normed, inverse = norm_stats(r.r2[rows, :])
        grad, gain_part, shift_part = norm_back(normed, inverse, gain[1:2, :], r.work[rows, :])
        r.dr2[rows, :] = grad
        low = grad.astype(BF16)
        r.common[1:2, :] += column_total(low)
        r.common[4:5, :] += gain_part
        r.common[7:8, :] += shift_part

    each_tile(length // TILE, middle_norm)
    turned = r.a2[...].T
    hidden = r.du.shape[1]
    wide = min(512, hidden)
    for first in range(0, hidden, wide):
        cut = slice(first, first + wide)
        r.in_total[:, cut] += dot_nn(turned, r.du[:, cut])
    turned = r.df[...].T
    for first in range(0, hidden, wide):
        cut = slice(first, first + wide)
        r.out_total[:, cut] += dot_nn(turned, r.g[:, cut])
    end_totals([(r.in_total, r.ffn_in_grad), (r.out_total, r.ffn_out_grad)])


def cross_back_kernel(levels, r):
    tiles, width = r.dr2.shape[0] // TILE, r.dr2.shape[1]
    start_totals([r.total_q, r.total_k, r.total_v, r.total_o, r.common, r.shares])
    far, unused = make_marks(r.tgt[...], levels, width // HEAD_DIM)
    unused, near = make_marks(r.src[...], levels, width // HEAD_DIM)
    r.far[...] = far
    r.near[...] = near
    r.low[...] = r.dr2[...].astype(BF16)
    r.dctx[...] = dot_nt(r.low[...], r.cross_out[...]).astype(BF16)
    base = (pl.num_programs(0) + pl.program_id(0)) * tiles
    attend_back(
        r.q2,
        r.k2,
        r.v2,
        r.far,
        r.near,
        r.sides,
        r.own,
        r.spread,
        r.lse2,
        r.ctx2,
        r.dctx,
        r.dq,
        r.dk,
        r.dv,
        r.starts,
        base,
    )
    r.dk_low[...] = r.dk[...].astype(BF16)
    r.dv_low[...] = r.dv[...].astype(BF16)
    r.memory_grad[...] = (
        dot_nt(r.dk_low[...], r.cross_kv[0]) + dot_nt(r.dv_low[...], r.cross_kv[1])
    ).astype(BF16)
    r.work[...] = r.dr2[...] + dot_nt(r.dq[...], r.cross_q[...])
    add_grad(r.total_o, r.low[...].T, r.ctx2[...])
    turned = r.memory[...].T
    add_grad(r.total_k, turned, r.dk_low[...])
    add_grad(r.total_v, turned, r.dv_low[...])
    add_grad(r.total_q, r.a1[...].T, r.dq[...])
    add_share(r.shares, 2, column_total(r.dq[...]))
    add_share(r.shares, 3, column_total(r.dv_low[...]))
    gain = r.gain[0:1, :].astype(F32)

    def first_norm(tile):
        rows = tile_rows(tile)
        normed, inverse = norm_stats(r.r1[rows, :])
        grad, gain_part, shift_part = norm_back(normed, inverse, gain, r.work[rows, :])
        r.dr1[rows, :] = grad
        r.common[0:1, :] += column_total(grad.astype(BF16))
        r.common[3:4, :] += gain_part
        r.common[6:7, :] += shift_part

    each_tile(tiles, first_norm)
    end_totals(
        [
            (r.total_q, r.cross_q_grad),
            (r.total_k, r.cross_k_grad),
            (r.total_v, r.cross_v_grad),
            (r.total_o, r.cross_out_grad),
        ]
    )


def self_back_kernel(levels, r):
    tiles, width = r.dr1.shape[0] // TILE, r.dr1.shape[1]
    start_totals([r.total_q, r.total_k, r.total_v, r.total_o, r.shares])
    far, near = make_marks(r.tgt[...], levels, width // HEAD_DIM)
    r.far[...] = far
    r.near[...] = near
    r.low[...] = r.dr1[...].astype(BF16)
    r.dctx[...] = dot_nt(r.low[...], r.self_out[...]).astype(BF16)
    attend_back(
        r.q,
        r.k,
        r.v,
        r.far,
        r.near,
        r.sides,
        r.own,
        r.spread,
        r.lse,
        r.ctx,
        r.dctx,
        r.dq,
        r.dk,
        r.dv,
        r.starts,
        pl.program_id(0) * tiles,
    )
    r.dk_low[...] = r.dk[...].astype(BF16)
    r.dv_low[...] = r.dv[...].astype(BF16)
    r.input_grad[...] = (
        r.dr1[...]
        + (dot_nt(r.dq[...], r.self_qkv[0]) + dot_nt(r.dk_low[...], r.self_qkv[1]))
        + dot_nt(r.dv_low[...], r.self_qkv[2])
    ).astype(BF16)
    add_grad(r.total_o, r.low[...].T, r.ctx[...])
    turned = r.x[...].T
    add_grad(r.total_q, turned, r.dq[...])
    add_grad(r.total_k, turned, r.dk_low[...])
    add_grad(r.total_v, turned, r.dv_low[...])
    add_share(r.shares, 0, column_total(r.dq[...]))
    add_share(r.shares, 1, column_total(r.dv_low[...]))
    end_totals(
        [
            (r.total_q, r.self_q_grad),
            (r.total_k, r.self_k_grad),
            (r.total_v, r.self_v_grad),
            (r.total_o, r.self_out_grad),
        ]
    )


def first_pass_kernel(levels, r):
    tiles = r.x.shape[0] // TILE
    self_part(
        r, r.x, r.tgt, r.near, r.far, r.q, r.k, r.v, r.ctx, None, None, r.low, r.work, levels
    )
    cross_part(
        r, r.src, r.near, r.far, r.low, r.q, r.k2, r.v2, r.ctx, None, r.r2, r.work, levels
    )
    feed_part(r, r.r2, r.low, r.work, r.g, None)
    gain, shift = r.gain[2:3, :].astype(F32), r.shift[2:3, :].astype(F32)

    def last_norm(tile):
        rows = tile_rows(tile)
        r.first[rows, :] = (norm_stats(r.work[rows, :])[0] * gain + shift).astype(BF16)

    each_tile(tiles, last_norm)


class Refs:
    pass


def call_rows(kernel, name, rows, levels, scalars, row_args, fixed_args, row_outs, fixed_outs, scratch):
    names, args, specs = [], [], []

    def put(key, array, fixed):
        zeros = (0,) * (array.ndim if fixed else array.ndim - 1)
        names.append(key)
        args.append(array)
        if fixed:
            specs.append(
                pl.BlockSpec(array.shape, lambda row, *_: zeros, pipeline_mode=pl.Buffered(1))
            )
        else:
            specs.append(
                pl.BlockSpec((None,) + array.shape[1:], lambda row, *_: (row,) + zeros)
            )

    for group, fixed in ((row_args, False), (fixed_args, True)):
        for key, value in group.items():
            if isinstance(value, tuple):
                for index, array in enumerate(value):
                    put((key, index), array, fixed)
            else:
                put(key, value, fixed)
    out_names, out_shapes, out_specs = [], [], []
    for key, (shape, kind) in row_outs.items():
        tail = (0,) * (len(shape) - 1)
        out_names.append(key)
        out_shapes.append(jax.ShapeDtypeStruct(shape, kind))
        out_specs.append(
            pl.BlockSpec((None,) + shape[1:], lambda row, *_, tail=tail: (row,) + tail)
        )
    for key, (shape, kind) in fixed_outs.items():
        zeros = (0,) * len(shape)
        out_names.append(key)
        out_shapes.append(jax.ShapeDtypeStruct(shape, kind))
        out_specs.append(pl.BlockSpec(shape, lambda row, *_, zeros=zeros: zeros))
    all_names = list(scalars) + names + out_names + list(scratch)

    def run(*refs):
        found = Refs()
        for key, ref in zip(all_names, refs):
            if isinstance(key, tuple):
                if key[1] == 0:
                    setattr(found, key[0], [])
                getattr(found, key[0]).append(ref)
            else:
                setattr(found, key, ref)
        kernel(levels, found)

    outs = pl.pallas_call(
        run,
        grid_spec=pltpu.PrefetchScalarGridSpec(
            num_scalar_prefetch=len(scalars),
            grid=(rows,),
            in_specs=specs,
            out_specs=tuple(out_specs),
            scratch_shapes=[pltpu.VMEM(shape, kind) for shape, kind in scratch.values()],
        ),
        out_shape=tuple(out_shapes),
        compiler_params=pltpu.CompilerParams(
            dimension_semantics=("arbitrary",), vmem_limit_bytes=VMEM_BYTES
        ),
        cost_estimate=pl.CostEstimate(flops=1000, bytes_accessed=1000, transcendentals=0),
        name=name,
    )(*scalars.values(), *args)
    return dict(zip(out_names, outs))


def from_peer(values, size, step):
    return lax.ppermute(values, "head", [((i + step) % size, i) for i in range(size)])


def by_origin(parts, me):
    count = len(parts)
    if count == 1:
        return parts
    if count == 2:
        return [
            jnp.where(me == 0, parts[0], parts[1]),
            jnp.where(me == 0, parts[1], parts[0]),
        ]
    stacked = jnp.stack(parts)
    return [
        lax.dynamic_index_in_dim(stacked, (origin - me) % count, 0, keepdims=False)
        for origin in range(count)
    ]


def own_first(values, size):
    return tuple([values] + [from_peer(values, size, step) for step in range(1, size)])


def trade_parts(values, split_axis, join_axis, me, size):
    share = values.shape[split_axis] // size
    parts = []
    for step in range(size):
        target = (me - step) % size
        part = lax.dynamic_slice_in_dim(values, target * share, share, split_axis)
        parts.append(part if step == 0 else from_peer(part, size, step))
    return jnp.concatenate(by_origin(parts, me), axis=join_axis)


def head_share(parts, size):
    total = parts[0].astype(F32)
    for step in range(1, size):
        arrived = lax.ppermute(parts[step], "head", [(i, (i + step) % size) for i in range(size)])
        total = total + arrived.astype(F32)
    return total.astype(BF16)


def stage_orders(dp_size):
    bits = [1 << b for b in range(dp_size.bit_length() - 1)]
    return bits, bits[:2][::-1] + bits[2:]


def reduce_kernel(dp_size, head_size, count, *refs):
    grads = refs[:count]
    common_one, common_two, share_one, share_two, share_three = refs[count : count + 5]
    out_ref, small_out_ref = refs[count + 5 : count + 7]
    head_land, land, small_land, small_ref, sum_ref = refs[count + 7 : count + 12]
    (
        local_sem,
        head_send,
        head_recv,
        fold_send,
        fold_recv,
        grow_send,
        grow_recv,
        small_send,
        small_recv,
    ) = refs[count + 12 :]
    length = out_ref.shape[1]
    me, spot = lax.axis_index("head"), lax.axis_index("dp")
    orders = stage_orders(dp_size)
    depth = len(orders[0])

    def digit(stride):
        return (spot // stride) % 2

    def partner(stride):
        return spot + (1 - 2 * digit(stride)) * stride

    share = out_ref.shape[2]
    for j in range(head_size):
        small_ref[j, 0:16, :] = common_one[...] + common_two[...]
        small_ref[j, 16:24, 0:share] = share_one[j] + share_two[j] + share_three[j]
        if share < small_ref.shape[2]:
            small_ref[j, 16:24, share:] = jnp.zeros((8, small_ref.shape[2] - share), F32)
    peers = [(me + step) % head_size for step in range(1, head_size)]
    barrier = pltpu.get_barrier_semaphore()
    for peer in peers:
        pl.semaphore_signal(
            barrier, inc=1, device_id={"head": peer}, device_id_type=pl.DeviceIdType.MESH
        )
    for stride in orders[0]:
        pl.semaphore_signal(
            barrier, inc=1, device_id={"dp": partner(stride)}, device_id_type=pl.DeviceIdType.MESH
        )
    pl.semaphore_wait(barrier, len(peers) + depth)

    def remote(source, target, send, recv, where):
        return pltpu.make_async_remote_copy(
            src_ref=source,
            dst_ref=target,
            send_sem=send,
            recv_sem=recv,
            device_id=where,
            device_id_type=pl.DeviceIdType.MESH,
        )

    queue = [i for pair in zip(range(count // 2), range(count // 2, count)) for i in pair]
    small_head = [
        remote(
            small_ref.at[j + 1],
            small_land.at[j],
            small_send.at[j],
            small_recv.at[j],
            {"head": peer},
        )
        for j, peer in enumerate(peers)
    ]
    for copy in small_head:
        copy.start()
    locals_, heads_ = {}, {}
    for i in queue:
        locals_[i] = pltpu.make_async_copy(grads[i].at[0], sum_ref.at[i], local_sem.at[i])
        locals_[i].start()
        heads_[i] = [
            remote(
                grads[i].at[j + 1],
                head_land.at[j, i],
                head_send.at[j, i],
                head_recv.at[j, i],
                {"head": peer},
            )
            for j, peer in enumerate(peers)
        ]
        for copy in heads_[i]:
            copy.start()

    def places(i):
        order = orders[0] if i < count // 2 else orders[1]
        offset, size, result = 0, length, []
        for stride in order:
            size //= 2
            keep = offset + digit(stride) * size
            give = offset + (1 - digit(stride)) * size
            result.append((stride, size, pl.multiple_of(keep, 16), pl.multiple_of(give, 16)))
            offset = keep
        return result

    plan = {i: places(i) for i in range(count)}
    moving = {}

    def fold(i, stage):
        stride, size, keep, give = plan[i][stage]
        base = length - (length >> stage)
        copy = remote(
            sum_ref.at[i, pl.ds(give, size), :],
            land.at[i, pl.ds(base, size), :],
            fold_send.at[stage, i],
            fold_recv.at[stage, i],
            {"dp": partner(stride)},
        )
        copy.start()
        moving[i] = copy

    def grow(i, stage):
        stride, size, keep, give = plan[i][stage]
        rows = out_ref.at[i, pl.ds(keep, size), :]
        copy = remote(
            rows, rows, grow_send.at[stage, i], grow_recv.at[stage, i], {"dp": partner(stride)}
        )
        copy.start()
        moving[i] = copy

    def task(i, number):
        if number == 0:
            locals_[i].wait()
            total = sum_ref[i].astype(F32)
            for j, copy in enumerate(heads_[i]):
                copy.wait()
                total = total + head_land[j, i].astype(F32)
            sum_ref[i] = total.astype(BF16)
            fold(i, 0)
        elif number <= depth:
            moving[i].wait()
            stage = number - 1
            stride, size, keep, give = plan[i][stage]
            base = length - (length >> stage)
            rows = pl.ds(keep, size)
            total = (
                sum_ref[i, rows, :].astype(F32) + land[i, pl.ds(base, size), :].astype(F32)
            ).astype(BF16)
            if number < depth:
                sum_ref[i, rows, :] = total
                fold(i, number)
            else:
                out_ref[i, rows, :] = total
                grow(i, depth - 1)
        else:
            moving[i].wait()
            stage = 2 * depth - number
            if stage > 0:
                grow(i, stage - 1)

    steps = 2 * depth + 1
    small_moving = None
    for time in range(steps + count // 2 - 1):
        if time == 0:
            total = small_ref[0]
            for j, copy in enumerate(small_head):
                copy.wait()
                total = total + small_land[j]
            small_out_ref[...] = total
        elif time <= depth:
            small_moving.wait()
            small_out_ref[...] += small_land[len(peers) + time - 1]
        if time < depth:
            slot = len(peers) + time
            small_moving = remote(
                small_out_ref,
                small_land.at[slot],
                small_send.at[slot],
                small_recv.at[slot],
                {"dp": partner(orders[0][time])},
            )
            small_moving.start()
        for place, i in enumerate(queue):
            number = time - place // 2
            if 0 <= number < steps:
                task(i, number)


def reduce_grads(grads, common, shares, dp_size, head_size):
    count = len(grads)
    length, share = grads[0].shape[1:]
    depth = dp_size.bit_length() - 1
    peers = head_size - 1
    small = (24, common[0].shape[1])
    any_spec = pl.BlockSpec(memory_space=pl.ANY)
    vmem = pl.BlockSpec(memory_space=pltpu.VMEM)
    dma = pltpu.SemaphoreType.DMA
    return pl.pallas_call(
        functools.partial(reduce_kernel, dp_size, head_size, count),
        out_shape=(
            jax.ShapeDtypeStruct((count, length, share), BF16),
            jax.ShapeDtypeStruct(small, F32),
        ),
        in_specs=[any_spec] * count + [vmem] * 5,
        out_specs=(vmem, vmem),
        scratch_shapes=[
            pltpu.VMEM((peers, count, length, share), BF16),
            pltpu.VMEM((count, length, share), BF16),
            pltpu.VMEM((peers + depth,) + small, F32),
            pltpu.VMEM((head_size,) + small, F32),
            pltpu.VMEM((count, length, share), BF16),
            dma((count,)),
            dma((peers, count)),
            dma((peers, count)),
            dma((depth, count)),
            dma((depth, count)),
            dma((depth, count)),
            dma((depth, count)),
            dma((peers + depth,)),
            dma((peers + depth,)),
        ],
        compiler_params=pltpu.CompilerParams(
            collective_id=0, has_side_effects=True, vmem_limit_bytes=VMEM_BYTES
        ),
        name="reduce",
    )(*grads, *common, *shares)


def window_starts(query_segments, key_segments, window):
    rows, length = query_segments.shape
    tiles = query_segments.reshape(rows, length // TILE, TILE)
    first, last = tiles[:, :, 0], tiles[:, :, -1]
    before = jnp.sum(key_segments[:, None, :] < first[:, :, None], axis=2).astype(jnp.int32)
    after = jnp.sum(key_segments[:, None, :] <= last[:, :, None], axis=2).astype(jnp.int32)
    start = jnp.minimum((before // 16) * 16, key_segments.shape[1] - window)
    return jnp.where(after - start <= window, start, -1).reshape(-1)


def constants(width, levels):
    heads = width // HEAD_DIM
    lane = np.arange(PAIR)
    sides = np.stack([lane < HEAD_DIM, lane >= HEAD_DIM])
    kept = (lane >= 16) & (lane < 16 + 3 * heads)
    own = np.stack([(lane < levels) | (kept & ((lane - 16) % heads == h)) for h in range(heads)])
    spread = kept[None, :] & (
        (lane[None, :] - 16) % heads == np.arange(width)[:, None] // HEAD_DIM
    )

    def tall(rows):
        return jnp.asarray(np.broadcast_to(rows[:, None, :], (rows.shape[0], TILE, PAIR)), BF16)

    return {"sides": tall(sides), "own": tall(own), "spread": jnp.asarray(spread, BF16)}


def local_layer(
    source,
    mixed,
    memory,
    cotangent,
    tgt_segments,
    src_segments,
    levels,
    weights,
    head_size=1,
    feed_sums=lambda grads: grads,
):
    rows, length, width = mixed.shape
    hidden = sum(part.shape[1] for part in weights["ffn_in"])
    heads = width // HEAD_DIM
    tiles = length // TILE
    window = min(WINDOW, length)
    share = width // head_size
    marks = constants(width, levels)
    sides = {"sides": marks["sides"]}
    tgt, src = tgt_segments[:, None, :], src_segments[:, None, :]
    starts = {
        "starts": jnp.concatenate(
            [
                window_starts(tgt_segments, tgt_segments, window),
                window_starts(tgt_segments, src_segments, window),
            ]
        )
    }

    def pick(*keys):
        return {key: weights[key] for key in keys}

    wide_low = ((rows, length, width), BF16)
    wide = ((rows, length, width), F32)
    stats = ((rows, tiles, heads, TILE), F32)
    one_low, one = ((length, width), BF16), ((length, width), F32)
    mark = ((length, PAIR), BF16)
    square = ((width, width), F32)
    split = ((head_size, width, share), BF16)
    common, shares = ((16, width), F32), ((head_size, 8, share), F32)
    norms = pick("out_bias", "gain", "shift")
    attention = pick("self_qkv", "self_out", "cross_q", "cross_kv", "cross_out", "head_bias")
    feed = pick("ffn_in", "ffn_out", "ffn_bias")
    kept = call_rows(
        attention_kernel,
        "attention",
        rows,
        levels,
        starts,
        {"x": mixed, "memory": memory, "tgt": tgt, "src": src},
        sides | attention | norms,
        {key: wide_low for key in ("q", "k", "v", "ctx", "a1", "q2", "k2", "v2", "ctx2")}
        | {"lse": stats, "lse2": stats, "r1": wide, "r2": wide},
        {},
        {"work": one, "far": mark, "near": mark},
    )
    fed = call_rows(
        feed_kernel,
        "feed",
        rows,
        levels,
        {},
        {"r2": kept["r2"], "cot": cotangent},
        feed | norms,
        {"second": wide_low, "dr2": wide},
        {
            "ffn_in_grad": ((head_size, width, hidden // head_size), BF16),
            "ffn_out_grad": ((head_size, width, hidden // head_size), BF16),
            "common": common,
            "shares": shares,
        },
        {
            "a2": one_low,
            "df": one_low,
            "work": one,
            "g": ((length, hidden), BF16),
            "du": ((length, hidden), BF16),
            "slope": ((length, hidden), BF16),
            "in_total": ((width, hidden), F32),
            "out_total": ((width, hidden), F32),
        },
    )
    feed_grads = feed_sums((fed["ffn_in_grad"], fed["ffn_out_grad"]))
    dr2, feed_grads = lax.optimization_barrier((fed["dr2"], feed_grads))
    totals = {"total_" + key: square for key in "qkvo"}
    back_scratch = totals | {
        "far": mark,
        "near": mark,
        "dctx": one_low,
        "low": one_low,
        "dq": one_low,
        "dk_low": one_low,
        "dv_low": one_low,
        "dk": one,
        "dv": one,
    }
    crossed = call_rows(
        cross_back_kernel,
        "cross_back",
        rows,
        levels,
        starts,
        {key: kept[key] for key in ("q2", "k2", "v2", "ctx2", "lse2", "r1", "a1")}
        | {"dr2": dr2, "memory": memory, "tgt": tgt, "src": src},
        marks | pick("cross_q", "cross_kv", "cross_out", "gain"),
        {"memory_grad": wide_low, "dr1": wide},
        {key: split for key in ("cross_q_grad", "cross_k_grad", "cross_v_grad", "cross_out_grad")}
        | {"common": common, "shares": shares},
        back_scratch | {"work": one},
    )
    selfed = call_rows(
        self_back_kernel,
        "self_back",
        rows,
        levels,
        starts,
        {key: kept[key] for key in ("q", "k", "v", "ctx", "lse")}
        | {"dr1": crossed["dr1"], "x": mixed, "tgt": tgt},
        marks | pick("self_qkv", "self_out"),
        {"input_grad": wide_low},
        {key: split for key in ("self_q_grad", "self_k_grad", "self_v_grad", "self_out_grad")}
        | {"shares": shares},
        back_scratch,
    )
    source, input_grad = lax.optimization_barrier((source, selfed["input_grad"]))
    first = call_rows(
        first_pass_kernel,
        "first_pass",
        rows,
        levels,
        starts,
        {"x": source, "k2": kept["k2"], "v2": kept["v2"], "tgt": tgt, "src": src},
        sides
        | pick("self_qkv", "self_out", "cross_q", "cross_out", "head_bias")
        | feed
        | norms,
        {"first": wide_low},
        {},
        {
            "q": one_low,
            "k": one_low,
            "v": one_low,
            "ctx": one_low,
            "low": one_low,
            "r2": one,
            "work": one,
            "g": ((length, hidden), BF16),
            "far": mark,
            "near": mark,
        },
    )
    grads = tuple(
        crossed[key] for key in ("cross_q_grad", "cross_k_grad", "cross_v_grad", "cross_out_grad")
    ) + tuple(selfed[key] for key in ("self_q_grad", "self_k_grad", "self_v_grad", "self_out_grad"))
    return (
        first["first"],
        fed["second"],
        input_grad,
        crossed["memory_grad"],
        feed_grads,
        grads,
        (fed["common"], crossed["common"]),
        (fed["shares"], crossed["shares"], selfed["shares"]),
    )


def body(
    dp_size,
    head_size,
    source_copy,
    target_embed,
    memory,
    tgt_segments,
    src_segments,
    hamming,
    priority,
    cotangent,
    self_qkv,
    self_out,
    cross_q,
    cross_kv,
    cross_out,
    ffn_in,
    ffn_out,
    head_bias,
    ffn_bias,
    out_bias,
    norm_gain,
    norm_shift,
):
    me = lax.axis_index("head")
    levels = hamming.shape[1]
    held, share, width = source_copy.shape
    rows = held // head_size

    def own_positions(array):
        return lax.dynamic_slice_in_dim(array, me * share, share, 1)

    def own_rows(array):
        return lax.dynamic_slice_in_dim(array, me * rows, rows, 0)

    level = jnp.arange(levels, dtype=jnp.int32)
    chosen = own_positions(tgt_segments)[:, :, None] == level[None, None, :]
    limits = jnp.sum(jnp.where(chosen, hamming[:, None, :], 0), axis=2)
    glanced = own_positions(priority) < limits
    mixed_part = jnp.where(glanced[:, :, None], target_embed, source_copy)

    def gather(values, axis):
        return jnp.concatenate(own_first(values, head_size), axis=axis)

    trade = functools.partial(trade_parts, me=me, size=head_size)
    (
        first_out,
        second_out,
        input_grad,
        memory_grad,
        feed_grads,
        grads,
        common,
        shares,
    ) = local_layer(
        trade(source_copy, 0, 1),
        trade(mixed_part, 0, 1),
        trade(memory, 0, 1),
        trade(cotangent, 0, 1),
        own_rows(tgt_segments),
        own_rows(src_segments),
        levels,
        {
            "self_qkv": gather(self_qkv, 2),
            "self_out": gather(self_out, 0),
            "cross_q": gather(cross_q, 1),
            "cross_kv": gather(cross_kv, 2),
            "cross_out": gather(cross_out, 0),
            "head_bias": gather(head_bias, 1),
            "ffn_bias": own_first(ffn_bias[None, :], head_size),
            "ffn_in": own_first(ffn_in, head_size),
            "ffn_out": own_first(ffn_out, head_size),
            "out_bias": out_bias,
            "gain": norm_gain,
            "shift": norm_shift,
        },
        head_size,
        lambda pair: tuple(head_share(parts, head_size) for parts in pair),
    )
    ffn_in_grad, ffn_out_grad = lax.psum(feed_grads, "dp")
    first_out, ffn_in_grad, ffn_out_grad = lax.optimization_barrier(
        (first_out, ffn_in_grad, ffn_out_grad)
    )
    common = lax.optimization_barrier((common, first_out))[0]
    summed, sums = reduce_grads(grads, common, shares, dp_size, head_size)
    summed = summed.astype(F32)
    part = width // head_size

    def back(array):
        return trade(array, 1, 0)

    return (
        back(first_out),
        back(second_out),
        back(input_grad),
        back(memory_grad),
        summed[4:7],
        summed[7].T,
        summed[0],
        summed[1:3],
        summed[3].T,
        ffn_in_grad.astype(F32),
        ffn_out_grad.T.astype(F32),
        sums[16:20, :part],
        sums[20:24, :part].reshape(-1),
        sums[0:3],
        sums[3:6],
        sums[6:9],
    )


def solution(mesh):
    split = P("dp", "head", None)
    rows = P("dp", None)
    last, last_two, first = P(None, "head"), P(None, None, "head"), P("head", None)
    return jax.shard_map(
        functools.partial(body, mesh.shape["dp"], mesh.shape["head"]),
        mesh=mesh,
        in_specs=(split, split, split, rows, rows, rows, rows, split)
        + (last_two, first, last, last_two, first, last, first, last, P("head"), P(), P(), P()),
        out_specs=(split, split, split, split)
        + (last_two, first, last, last_two, first, last, first, last, P("head"), P(), P(), P()),
        check_vma=False,
    )
```

```python
import functools

import jax
import jax.numpy as jnp
import numpy as np
from jax import lax
from jax.experimental import pallas as pl
from jax.experimental.pallas import tpu as pltpu
from jax.sharding import PartitionSpec as P

HEAD_DIM = 64
PAIR = 2 * HEAD_DIM
TILE = 128
WINDOW = 256
FAR = -1e30
F32 = jnp.float32
BF16 = jnp.bfloat16
VMEM_BYTES = 60 * 1024 * 1024


def dot_nn(left, right):
    return lax.dot_general(left, right, (((1,), (0,)), ((), ())), preferred_element_type=F32)


def dot_nt(left, right):
    return lax.dot_general(left, right, (((1,), (1,)), ((), ())), preferred_element_type=F32)


def norm_stats(sums):
    row_mean = jnp.mean(sums, axis=-1, keepdims=True)
    centred = sums - row_mean
    spread = jnp.mean(centred * centred, axis=-1, keepdims=True)
    inverse = lax.rsqrt(spread + 1e-05)
    return centred * inverse, inverse


def norm_back(normed, inverse, gain_row, incoming):
    scaled = incoming * gain_row
    mean_one = jnp.mean(scaled, axis=-1, keepdims=True)
    mean_two = jnp.mean(scaled * normed, axis=-1, keepdims=True)
    grad = (scaled - mean_one - normed * mean_two) * inverse
    gain_part = jnp.sum(incoming * normed, axis=0, keepdims=True)
    shift_part = jnp.sum(incoming, axis=0, keepdims=True)
    return grad, gain_part, shift_part


def gelu_parts(pre):
    ratio = pltpu.reciprocal(1.0 + 0.23164189015488 * jnp.abs(pre), approx=True)
    series = ratio * (
        0.127414796
        + ratio
        * (-0.142248368 + ratio * (0.7107068705 + ratio * (-0.7265760135 + ratio * 0.5307027145)))
    )
    bell = jnp.exp(-0.5 * (pre * pre))
    tail = series * bell
    return jnp.where(pre >= 0, 1.0 - tail, tail), bell


def each_tile(count, step):
    for index in range(count):
        step(index)


def tile_rows(tile):
    start = tile * TILE
    return pl.ds(start if isinstance(start, int) else pl.multiple_of(start, TILE), TILE)


def window_loop(starts_ref, base, tiles, length, step):
    starts = [starts_ref[base + tile] for tile in range(tiles)]
    least = functools.reduce(jnp.minimum, starts)
    window = min(WINDOW, length)

    @pl.when(least >= 0)
    def straight():
        for tile in range(tiles):
            step(tile, pl.multiple_of(starts[tile], 16), window)

    if length > WINDOW:

        @pl.when(least < 0)
        def mixed():
            def one(tile, carry):
                start = starts_ref[base + tile]

                @pl.when(start >= 0)
                def near():
                    step(tile, pl.multiple_of(start, 16), window)

                @pl.when(start < 0)
                def whole():
                    step(tile, 0, length)

                return carry

            lax.fori_loop(0, tiles, one, 0)


def make_marks(segment_row, levels, heads):
    shape = (PAIR, segment_row.shape[1])
    level = lax.broadcasted_iota(jnp.int32, shape, 0)
    same = level == segment_row
    near = jnp.where(same | ((level >= 16) & (level < 16 + 3 * heads)), 1.0, 0.0)
    far = jnp.where(same | (level >= levels), 0.0, FAR)
    return far.T.astype(BF16), near.T.astype(BF16)


def attend(q_ref, k_ref, v_ref, far_ref, near_ref, sides_ref, ctx_ref, lse_ref, starts_ref, base):
    length, width = q_ref.shape
    pairs = range(width // PAIR)
    lanes = [slice(p * PAIR, (p + 1) * PAIR) for p in pairs]

    def step(tile, start, window):
        rows = tile_rows(tile)
        keys = pl.ds(start, window)
        left, right = sides_ref[0], sides_ref[1]
        query_marks = far_ref[rows, :]
        key_marks = near_ref[keys, :]
        stacked = []
        for p in pairs:
            queries = q_ref[rows, lanes[p]]
            stacked.append(
                jnp.concatenate(
                    [
                        jnp.concatenate([queries * left, query_marks], axis=1),
                        jnp.concatenate([queries * right, query_marks], axis=1),
                    ],
                    axis=0,
                )
            )
        scores = [
            dot_nt(jnp.concatenate([k_ref[keys, lanes[p]], key_marks], axis=1), stacked[p])
            for p in pairs
        ]
        peaks = [jnp.max(s, axis=0, keepdims=True) for s in scores]
        weights = [jnp.exp(s - m) for s, m in zip(scores, peaks)]
        totals = [jnp.sum(w, axis=0, keepdims=True) for w in weights]
        low = [w.astype(BF16) for w in weights]
        turned = [v_ref[keys, lanes[p]].T for p in pairs]
        mixed = [dot_nn(turned[p], low[p]) for p in pairs]
        shares = [pltpu.reciprocal(t, approx=True) for t in totals]
        context = [
            jnp.concatenate(
                [
                    mixed[p][:HEAD_DIM, :TILE] * shares[p][:, :TILE],
                    mixed[p][HEAD_DIM:, TILE:] * shares[p][:, TILE:],
                ],
                axis=0,
            )
            for p in pairs
        ]
        for p in pairs:
            ctx_ref[rows, lanes[p]] = context[p].T.astype(BF16)
        if lse_ref is not None:
            for p in pairs:
                log_total = peaks[p] + jnp.log(totals[p])
                lse_ref[tile, pl.ds(2 * p, 1), :] = log_total[:, :TILE]
                lse_ref[tile, pl.ds(2 * p + 1, 1), :] = log_total[:, TILE:]

    window_loop(starts_ref, base, length // TILE, length, step)


def three_parts(values):
    high = values.astype(BF16).astype(F32)
    rest = values - high
    middle = rest.astype(BF16).astype(F32)
    return high, middle, rest - middle


def attend_back(
    q_ref,
    k_ref,
    v_ref,
    far_ref,
    near_ref,
    sides_ref,
    own_ref,
    spread_ref,
    lse_ref,
    ctx_ref,
    dctx_ref,
    dq_ref,
    dk_ref,
    dv_ref,
    starts_ref,
    base,
):
    length, width = q_ref.shape
    pairs = range(width // PAIR)
    heads = width // HEAD_DIM
    lanes = [slice(p * PAIR, (p + 1) * PAIR) for p in pairs]
    dk_ref[...] = jnp.zeros_like(dk_ref)
    dv_ref[...] = jnp.zeros_like(dv_ref)

    def step(tile, start, window):
        rows = tile_rows(tile)
        keys = pl.ds(start, window)
        left, right = sides_ref[0], sides_ref[1]
        key_marks = near_ref[keys, :]
        high, middle, rest = three_parts(-lse_ref[tile])
        stats = jnp.concatenate(
            [
                jnp.zeros((16, TILE), F32),
                high,
                middle,
                rest,
                jnp.zeros((TILE - 16 - 3 * heads, TILE), F32),
            ],
            axis=0,
        )
        query_marks = far_ref[rows, :] + stats.T.astype(BF16)
        product = dctx_ref[rows, :].astype(F32) * ctx_ref[rows, :].astype(F32)
        product_high = product.astype(BF16)
        product_rest = (product - product_high.astype(F32)).astype(BF16)
        delta = -(dot_nn(product_high, spread_ref[...]) + dot_nn(product_rest, spread_ref[...]))
        high, middle, rest = three_parts(delta)
        lane = lax.broadcasted_iota(jnp.int32, delta.shape, 1)
        grad_marks = jnp.where(
            lane < 16 + heads, high, jnp.where(lane < 16 + 2 * heads, middle, rest)
        ).astype(BF16)
        query_stack, grad_stack, query_side, grad_side, key_rows = [], [], [], [], []
        for p in pairs:
            queries = q_ref[rows, lanes[p]]
            grads = dctx_ref[rows, lanes[p]]
            key_rows.append(k_ref[keys, lanes[p]])
            query_stack.append(jnp.concatenate([queries * left, queries * right], axis=0))
            grad_stack.append(jnp.concatenate([grads * left, grads * right], axis=0))
            one, two = own_ref[2 * p], own_ref[2 * p + 1]
            marks = jnp.concatenate([query_marks * one, query_marks * two], axis=0)
            query_side.append(jnp.concatenate([query_stack[p], marks], axis=1))
            marks = jnp.concatenate([grad_marks * one, grad_marks * two], axis=0)
            grad_side.append(jnp.concatenate([grad_stack[p], marks], axis=1))
        scores = [
            dot_nt(jnp.concatenate([key_rows[p], key_marks], axis=1), query_side[p]) for p in pairs
        ]
        probs_grad = [
            dot_nt(jnp.concatenate([v_ref[keys, lanes[p]], key_marks], axis=1), grad_side[p])
            for p in pairs
        ]
        probs = [jnp.exp(s) for s in scores]
        probs_low = [w.astype(BF16) for w in probs]
        scores_grad = [(probs[p] * probs_grad[p]).astype(BF16) for p in pairs]
        turned_keys = [key_rows[p].T for p in pairs]
        for p in pairs:
            dv_ref[keys, lanes[p]] += dot_nn(probs_low[p], grad_stack[p])
        for p in pairs:
            dk_ref[keys, lanes[p]] += dot_nn(scores_grad[p], query_stack[p])
        turned = [dot_nn(turned_keys[p], scores_grad[p]) for p in pairs]
        for p in pairs:
            both = jnp.concatenate(
                [turned[p][:HEAD_DIM, :TILE], turned[p][HEAD_DIM:, TILE:]], axis=0
            )
            dq_ref[rows, lanes[p]] = (both.T * (HEAD_DIM**-0.5)).astype(BF16)

    window_loop(starts_ref, base, length // TILE, length, step)


def join_positions(target_ref, parts, place):
    share = parts[0].shape[0]
    for j, part in enumerate(parts):
        start = ((place + j) % len(parts)) * share
        target_ref[pl.ds(pl.multiple_of(start, share), share), :] = part[...]


def join_weights(pairs):
    @pl.when(pl.program_id(0) == 0)
    def join():
        for target_ref, parts, axis in pairs:
            share = parts[0].shape[axis]
            for j, part in enumerate(parts):
                where = [slice(None)] * len(target_ref.shape)
                where[axis] = slice(j * share, (j + 1) * share)
                target_ref[tuple(where)] = part[...]


def joined(parts):
    return jnp.concatenate([part[...].astype(F32) for part in parts], axis=1)


def window_base(r, tiles, cross):
    rows = pl.num_programs(0)
    row = r.place[0] * rows + pl.program_id(0)
    held = r.starts.shape[0] // (2 * tiles)
    return (row + held * cross) * tiles


def self_part(
    r, x_ref, seg_ref, near_ref, far_ref, q_ref, k_ref, v_ref, ctx_ref, lse_ref, r1_ref, a1_ref, work_ref, levels
):
    tiles, width = x_ref.shape[0] // TILE, x_ref.shape[1]
    far, near = make_marks(seg_ref[...], levels, width // HEAD_DIM)
    far_ref[...] = far
    near_ref[...] = near
    bias = joined(r.head_bias)
    inputs = x_ref[...]
    queries = (dot_nn(inputs, r.self_qkv[0]) + bias[0:1, :]).astype(BF16)
    q_ref[...] = queries * jnp.asarray(HEAD_DIM**-0.5, BF16)
    k_ref[...] = dot_nn(inputs, r.self_qkv[1]).astype(BF16)
    v_ref[...] = (dot_nn(inputs, r.self_qkv[2]) + bias[1:2, :]).astype(BF16)
    base = window_base(r, tiles, 0)
    attend(q_ref, k_ref, v_ref, far_ref, near_ref, r.sides, ctx_ref, lse_ref, r.starts, base)
    work_ref[...] = dot_nn(ctx_ref[...], r.self_out[...])
    out_bias = r.out_bias[0:1, :].astype(F32)
    gain, shift = r.gain[0:1, :].astype(F32), r.shift[0:1, :].astype(F32)

    def step(tile):
        rows = tile_rows(tile)
        sums = x_ref[rows, :].astype(F32) + (work_ref[rows, :] + out_bias)
        if r1_ref is not None:
            r1_ref[rows, :] = sums
        normed = norm_stats(sums)[0] * gain + shift
        work_ref[rows, :] = normed
        a1_ref[rows, :] = normed.astype(BF16)

    each_tile(tiles, step)


def cross_part(
    r, seg_ref, near_ref, far_ref, a1_ref, q2_ref, k2_ref, v2_ref, ctx2_ref, lse2_ref, r2_ref, work_ref, levels
):
    tiles, width = q2_ref.shape[0] // TILE, q2_ref.shape[1]
    near_ref[...] = make_marks(seg_ref[...], levels, width // HEAD_DIM)[1]
    bias = joined(r.head_bias)
    queries = (dot_nn(a1_ref[...], r.cross_q[...]) + bias[2:3, :]).astype(BF16)
    q2_ref[...] = queries * jnp.asarray(HEAD_DIM**-0.5, BF16)
    base = window_base(r, tiles, 1)
    attend(q2_ref, k2_ref, v2_ref, far_ref, near_ref, r.sides, ctx2_ref, lse2_ref, r.starts, base)
    r2_ref[...] = work_ref[...] + (
        dot_nn(ctx2_ref[...], r.cross_out[...]) + r.out_bias[1:2, :].astype(F32)
    )


def attention_weights(r):
    return [
        (r.self_qkv, r.self_qkv_parts, 2),
        (r.self_out, r.self_out_parts, 0),
        (r.cross_q, r.cross_q_parts, 1),
        (r.cross_out, r.cross_out_parts, 0),
    ]


def attention_kernel(levels, r):
    join_weights(attention_weights(r) + [(r.cross_kv, r.cross_kv_parts, 2)])
    join_positions(r.x, r.x_parts, r.place[0])
    join_positions(r.memory, r.memory_parts, r.place[0])
    self_part(
        r, r.x, r.tgt, r.near, r.far, r.q, r.k, r.v, r.ctx, r.lse, r.r1, r.a1, r.work, levels
    )
    bias = joined(r.head_bias)
    r.k2[...] = dot_nn(r.memory[...], r.cross_kv[0]).astype(BF16)
    r.v2[...] = (dot_nn(r.memory[...], r.cross_kv[1]) + bias[3:4, :]).astype(BF16)
    cross_part(
        r, r.src, r.near, r.far, r.a1, r.q2, r.k2, r.v2, r.ctx2, r.lse2, r.r2, r.work, levels
    )


def feed_norm(r, r2_ref, a2_ref, work_ref):
    gain, shift = r.gain[1:2, :].astype(F32), r.shift[1:2, :].astype(F32)

    def step(tile):
        rows = tile_rows(tile)
        normed = norm_stats(r2_ref[rows, :])[0] * gain + shift
        work_ref[rows, :] = normed
        a2_ref[rows, :] = normed.astype(BF16)

    each_tile(r2_ref.shape[0] // TILE, step)


def feed_units(r, j, a2_ref, g_ref, slope_ref):
    units = r.ffn_in[j].shape[1]
    chunk = min(256, units)
    for first in range(0, units, chunk):
        cut = slice(first, first + chunk)
        pre = dot_nn(a2_ref[...], r.ffn_in[j][:, cut]) + r.ffn_bias[j][:, cut].astype(F32)
        phi, bell = gelu_parts(pre)
        cut = slice(j * units + first, j * units + first + chunk)
        g_ref[:, cut] = (pre * phi).astype(BF16)
        if slope_ref is not None:
            slope_ref[:, cut] = (phi + (pre * bell) * 0.3989422804014327).astype(BF16)


def feed_out(r, work_ref, g_ref):
    units = r.ffn_in[0].shape[1]
    fed = r.out_bias[2:3, :].astype(F32)
    for j in range(len(r.ffn_out)):
        fed = fed + dot_nn(g_ref[:, j * units : (j + 1) * units], r.ffn_out[j][...])
    work_ref[...] += fed


def add_grad(total_ref, left, right):
    total_ref[...] += dot_nn(left, right)


def start_totals(refs):
    @pl.when(pl.program_id(0) == 0)
    def clear():
        for ref in refs:
            ref[...] = jnp.zeros_like(ref)


def end_totals(pairs):
    @pl.when(pl.program_id(0) == pl.num_programs(0) - 1)
    def write():
        for total_ref, out_ref in pairs:
            share = out_ref.shape[2]
            for j in range(out_ref.shape[0]):
                out_ref[j] = total_ref[:, j * share : (j + 1) * share].astype(BF16)


def end_feed_totals(r):
    @pl.when(pl.program_id(0) == pl.num_programs(0) - 1)
    def write():
        share = r.own_grads.shape[2]
        for which, total_ref in enumerate((r.in_total, r.out_total)):
            r.own_grads[which] = total_ref[:, 0:share].astype(BF16)
            for j, out_ref in enumerate(r.sent_grads):
                out_ref[which] = total_ref[:, (j + 1) * share : (j + 2) * share].astype(BF16)


def column_total(values):
    return jnp.sum(values.astype(F32), axis=0, keepdims=True)


def add_share(share_ref, row, values):
    share = share_ref.shape[2]
    for j in range(share_ref.shape[0]):
        share_ref[j, row : row + 1, :] += values[:, j * share : (j + 1) * share]


def feed_kernel(levels, r):
    length = r.r2.shape[0]
    units = r.ffn_in[0].shape[1]
    chunk = min(256, units)
    start_totals([r.in_total, r.out_total, r.common, r.shares])
    join_positions(r.cot, r.cot_parts, r.place[0])
    feed_norm(r, r.r2, r.a2, r.work)
    for j in range(len(r.ffn_in)):
        feed_units(r, j, r.a2, r.g, r.slope)
    feed_out(r, r.work, r.g)
    gain, shift = r.gain[...].astype(F32), r.shift[...].astype(F32)

    def last_norm(tile):
        rows = tile_rows(tile)
        normed, inverse = norm_stats(r.work[rows, :])
        r.second[rows, :] = (normed * gain[2:3, :] + shift[2:3, :]).astype(BF16)
        grad, gain_part, shift_part = norm_back(
            normed, inverse, gain[2:3, :], r.cot[rows, :].astype(F32)
        )
        r.work[rows, :] = grad
        low = grad.astype(BF16)
        r.df[rows, :] = low
        r.common[2:3, :] += column_total(low)
        r.common[5:6, :] += gain_part
        r.common[8:9, :] += shift_part

    each_tile(length // TILE, last_norm)
    spots = [(j, first) for j in range(len(r.ffn_in)) for first in range(0, units, chunk)]

    def product(spot):
        j, first = spot
        return dot_nt(r.df[...], r.ffn_out[j][first : first + chunk, :])

    share = r.shares.shape[2]
    following = product(spots[0])
    for index, (j, first) in enumerate(spots):
        hidden_grad = following.astype(BF16)
        if index + 1 < len(spots):
            following = product(spots[index + 1])
        cut = slice(j * units + first, j * units + first + chunk)
        pre_grad = (hidden_grad.astype(F32) * r.slope[:, cut].astype(F32)).astype(BF16)
        r.du[:, cut] = pre_grad
        sums = column_total(pre_grad)
        for piece in range(0, chunk, share):
            row = 4 + (first + piece) // share
            r.shares[j, row : row + 1, :] += sums[:, piece : piece + share]
    back = r.work[...]
    for j in range(len(r.ffn_in)):
        back = back + dot_nt(r.du[:, j * units : (j + 1) * units], r.ffn_in[j][...])
    r.work[...] = back

    def middle_norm(tile):
        rows = tile_rows(tile)
        normed, inverse = norm_stats(r.r2[rows, :])
        grad, gain_part, shift_part = norm_back(normed, inverse, gain[1:2, :], r.work[rows, :])
        r.dr2[rows, :] = grad
        low = grad.astype(BF16)
        r.common[1:2, :] += column_total(low)
        r.common[4:5, :] += gain_part
        r.common[7:8, :] += shift_part

    each_tile(length // TILE, middle_norm)
    turned = r.a2[...].T
    hidden = r.du.shape[1]
    wide = min(512, hidden)
    for first in range(0, hidden, wide):
        cut = slice(first, first + wide)
        r.in_total[:, cut] += dot_nn(turned, r.du[:, cut])
    turned = r.df[...].T
    for first in range(0, hidden, wide):
        cut = slice(first, first + wide)
        r.out_total[:, cut] += dot_nn(turned, r.g[:, cut])
    end_feed_totals(r)


def cross_back_kernel(levels, r):
    tiles, width = r.dr2.shape[0] // TILE, r.dr2.shape[1]
    start_totals([r.total_q, r.total_k, r.total_v, r.total_o, r.common, r.shares])
    join_weights(
        [
            (r.cross_q, r.cross_q_parts, 1),
            (r.cross_kv, r.cross_kv_parts, 2),
            (r.cross_out, r.cross_out_parts, 0),
        ]
    )
    join_positions(r.memory, r.memory_parts, r.place[0])
    far, unused = make_marks(r.tgt[...], levels, width // HEAD_DIM)
    unused, near = make_marks(r.src[...], levels, width // HEAD_DIM)
    r.far[...] = far
    r.near[...] = near
    r.low[...] = r.dr2[...].astype(BF16)
    r.dctx[...] = dot_nt(r.low[...], r.cross_out[...]).astype(BF16)
    base = window_base(r, tiles, 1)
    attend_back(
        r.q2,
        r.k2,
        r.v2,
        r.far,
        r.near,
        r.sides,
        r.own,
        r.spread,
        r.lse2,
        r.ctx2,
        r.dctx,
        r.dq,
        r.dk,
        r.dv,
        r.starts,
        base,
    )
    r.dk_low[...] = r.dk[...].astype(BF16)
    r.dv_low[...] = r.dv[...].astype(BF16)
    r.memory_grad[...] = (
        dot_nt(r.dk_low[...], r.cross_kv[0]) + dot_nt(r.dv_low[...], r.cross_kv[1])
    ).astype(BF16)
    r.work[...] = r.dr2[...] + dot_nt(r.dq[...], r.cross_q[...])
    add_grad(r.total_o, r.low[...].T, r.ctx2[...])
    turned = r.memory[...].T
    add_grad(r.total_k, turned, r.dk_low[...])
    add_grad(r.total_v, turned, r.dv_low[...])
    add_grad(r.total_q, r.a1[...].T, r.dq[...])
    add_share(r.shares, 2, column_total(r.dq[...]))
    add_share(r.shares, 3, column_total(r.dv_low[...]))
    gain = r.gain[0:1, :].astype(F32)

    def first_norm(tile):
        rows = tile_rows(tile)
        normed, inverse = norm_stats(r.r1[rows, :])
        grad, gain_part, shift_part = norm_back(normed, inverse, gain, r.work[rows, :])
        r.dr1[rows, :] = grad
        r.common[0:1, :] += column_total(grad.astype(BF16))
        r.common[3:4, :] += gain_part
        r.common[6:7, :] += shift_part

    each_tile(tiles, first_norm)
    end_totals(
        [
            (r.total_q, r.cross_q_grad),
            (r.total_k, r.cross_k_grad),
            (r.total_v, r.cross_v_grad),
            (r.total_o, r.cross_out_grad),
        ]
    )


def self_back_kernel(levels, r):
    tiles, width = r.dr1.shape[0] // TILE, r.dr1.shape[1]
    start_totals([r.total_q, r.total_k, r.total_v, r.total_o, r.shares])
    join_weights([(r.self_qkv, r.self_qkv_parts, 2), (r.self_out, r.self_out_parts, 0)])
    join_positions(r.x, r.x_parts, r.place[0])
    far, near = make_marks(r.tgt[...], levels, width // HEAD_DIM)
    r.far[...] = far
    r.near[...] = near
    r.low[...] = r.dr1[...].astype(BF16)
    r.dctx[...] = dot_nt(r.low[...], r.self_out[...]).astype(BF16)
    attend_back(
        r.q,
        r.k,
        r.v,
        r.far,
        r.near,
        r.sides,
        r.own,
        r.spread,
        r.lse,
        r.ctx,
        r.dctx,
        r.dq,
        r.dk,
        r.dv,
        r.starts,
        window_base(r, tiles, 0),
    )
    r.dk_low[...] = r.dk[...].astype(BF16)
    r.dv_low[...] = r.dv[...].astype(BF16)
    r.input_grad[...] = (
        r.dr1[...]
        + (dot_nt(r.dq[...], r.self_qkv[0]) + dot_nt(r.dk_low[...], r.self_qkv[1]))
        + dot_nt(r.dv_low[...], r.self_qkv[2])
    ).astype(BF16)
    add_grad(r.total_o, r.low[...].T, r.ctx[...])
    turned = r.x[...].T
    add_grad(r.total_q, turned, r.dq[...])
    add_grad(r.total_k, turned, r.dk_low[...])
    add_grad(r.total_v, turned, r.dv_low[...])
    add_share(r.shares, 0, column_total(r.dq[...]))
    add_share(r.shares, 1, column_total(r.dv_low[...]))
    end_totals(
        [
            (r.total_q, r.self_q_grad),
            (r.total_k, r.self_k_grad),
            (r.total_v, r.self_v_grad),
            (r.total_o, r.self_out_grad),
        ]
    )


def first_pass_kernel(levels, r):
    join_weights(attention_weights(r))
    join_positions(r.x, r.x_parts, r.place[0])
    tiles = r.x.shape[0] // TILE
    self_part(
        r, r.x, r.tgt, r.near, r.far, r.q, r.k, r.v, r.ctx, None, None, r.low, r.work, levels
    )
    cross_part(
        r, r.src, r.near, r.far, r.low, r.q, r.k2, r.v2, r.ctx, None, r.r2, r.work, levels
    )


class Refs:
    pass


def call_rows(
    kernel, name, rows, levels, scalars, held_args, row_args, fixed_args, row_outs, fixed_outs, scratch
):
    names, args, specs = [], [], []

    def put(key, array, kind):
        names.append(key)
        args.append(array)
        zeros = (0,) * (array.ndim if kind == "fixed" else array.ndim - 1)
        block = (None,) + array.shape[1:]
        if kind == "fixed":
            spec = pl.BlockSpec(array.shape, lambda row, *_: zeros, pipeline_mode=pl.Buffered(1))
        elif kind == "row":
            spec = pl.BlockSpec(block, lambda row, *_: (row,) + zeros)
        else:
            spec = pl.BlockSpec(block, lambda row, place, *_: (place[0] * rows + row,) + zeros)
        specs.append(spec)

    for group, kind in ((held_args, "held"), (row_args, "row"), (fixed_args, "fixed")):
        for key, value in group.items():
            if isinstance(value, tuple):
                for index, array in enumerate(value):
                    put((key, index), array, kind)
            else:
                put(key, value, kind)
    out_names, out_shapes, out_specs = [], [], []
    for key, (shape, kind) in row_outs.items():
        tail = (0,) * (len(shape) - 1)
        out_names.append(key)
        out_shapes.append(jax.ShapeDtypeStruct(shape, kind))
        out_specs.append(
            pl.BlockSpec((None,) + shape[1:], lambda row, *_, tail=tail: (row,) + tail)
        )
    for key, (shape, kind) in fixed_outs.items():
        zeros = (0,) * len(shape)
        out_names.append(key)
        out_shapes.append(jax.ShapeDtypeStruct(shape, kind))
        out_specs.append(pl.BlockSpec(shape, lambda row, *_, zeros=zeros: zeros))
    all_names = list(scalars) + names + out_names + list(scratch)

    def run(*refs):
        found = Refs()
        for key, ref in zip(all_names, refs):
            if isinstance(key, tuple):
                if not hasattr(found, key[0]):
                    setattr(found, key[0], [])
                getattr(found, key[0]).append(ref)
            else:
                setattr(found, key, ref)
        kernel(levels, found)

    outs = pl.pallas_call(
        run,
        grid_spec=pltpu.PrefetchScalarGridSpec(
            num_scalar_prefetch=len(scalars),
            grid=(rows,),
            in_specs=specs,
            out_specs=tuple(out_specs),
            scratch_shapes=[pltpu.VMEM(shape, kind) for shape, kind in scratch.values()],
        ),
        out_shape=tuple(out_shapes),
        compiler_params=pltpu.CompilerParams(
            dimension_semantics=("arbitrary",), vmem_limit_bytes=VMEM_BYTES
        ),
        cost_estimate=pl.CostEstimate(flops=1000, bytes_accessed=1000, transcendentals=0),
        name=name,
    )(*scalars.values(), *args)
    return dict(zip(out_names, outs))


def from_peer(values, size, step):
    return lax.ppermute(values, "head", [((i + step) % size, i) for i in range(size)])


def own_first(values, size):
    return tuple([values] + [from_peer(values, size, step) for step in range(1, size)])


def row_shares(values, rows, me, size):
    shares = []
    for step in range(1, size):
        target = (me - step) % size
        part = lax.dynamic_slice_in_dim(values, target * rows, rows, 0)
        shares.append(from_peer(part, size, step))
    return tuple(shares)


def stage_orders(dp_size):
    bits = [1 << b for b in range(dp_size.bit_length() - 1)]
    return bits, bits[:2][::-1] + bits[2:]


def reduce_kernel(dp_size, head_size, count, results, *refs):
    refs = list(refs)

    def take(number):
        taken = refs[:number]
        del refs[:number]
        return taken

    grads = take(count)
    rows_in = take(results)
    sums_in, feed_in = take(1)[0], take(2 * head_size)
    r = Refs()
    r.out_bias, r.gain, r.shift, *r.ffn_bias = take(3 + head_size)
    common_one, common_two, share_one, share_two, share_three = take(5)
    out_ref, small_out_ref, first_ref = take(3)
    rows_out = take(results + 1)
    head_land, land, small_land, small_ref, sum_ref = take(5)
    sums_ref, ffn_in_ref, ffn_out_ref, low_ref, work_ref, g_ref = take(6)
    r.ffn_in = [ffn_in_ref.at[j] for j in range(head_size)]
    r.ffn_out = [ffn_out_ref.at[j] for j in range(head_size)]
    (
        local_sem,
        head_send,
        head_recv,
        fold_send,
        fold_recv,
        grow_send,
        grow_recv,
        small_send,
        small_recv,
        rows_send,
        rows_recv,
        feed_sem,
    ) = refs
    loads = [pltpu.make_async_copy(sums_in, sums_ref, feed_sem.at[0])] + [
        pltpu.make_async_copy(feed_in[i], (r.ffn_in + r.ffn_out)[i], feed_sem.at[i + 1])
        for i in range(2 * head_size)
    ]
    for copy in loads:
        copy.start()
    length = out_ref.shape[1]
    me, spot = lax.axis_index("head"), lax.axis_index("dp")
    orders = stage_orders(dp_size)
    depth = len(orders[0])

    def digit(stride):
        return (spot // stride) % 2

    def partner(stride):
        return spot + (1 - 2 * digit(stride)) * stride

    share = out_ref.shape[2]
    for j in range(head_size):
        small_ref[j, 0:16, :] = common_one[...] + common_two[...]
        small_ref[j, 16:24, 0:share] = share_one[j] + share_two[j] + share_three[j]
        if share < small_ref.shape[2]:
            small_ref[j, 16:24, share:] = jnp.zeros((8, small_ref.shape[2] - share), F32)
    peers = [(me + step) % head_size for step in range(1, head_size)]
    barrier = pltpu.get_barrier_semaphore()
    for peer in peers:
        pl.semaphore_signal(
            barrier, inc=1, device_id={"head": peer}, device_id_type=pl.DeviceIdType.MESH
        )
    for stride in orders[0]:
        pl.semaphore_signal(
            barrier, inc=1, device_id={"dp": partner(stride)}, device_id_type=pl.DeviceIdType.MESH
        )
    pl.semaphore_wait(barrier, len(peers) + depth)

    def remote(source, target, send, recv, where):
        return pltpu.make_async_remote_copy(
            src_ref=source,
            dst_ref=target,
            send_sem=send,
            recv_sem=recv,
            device_id=where,
            device_id_type=pl.DeviceIdType.MESH,
        )

    queue = [i for pair in zip(range(count // 2), range(count // 2, count)) for i in pair]
    small_head = [
        remote(
            small_ref.at[j + 1],
            small_land.at[j],
            small_send.at[j],
            small_recv.at[j],
            {"head": peer},
        )
        for j, peer in enumerate(peers)
    ]
    for copy in small_head:
        copy.start()
    locals_, heads_ = {}, {}
    for i in queue:
        locals_[i] = pltpu.make_async_copy(grads[i].at[0], sum_ref.at[i], local_sem.at[i])
        locals_[i].start()
        heads_[i] = [
            remote(
                grads[i].at[j + 1],
                head_land.at[j, i],
                head_send.at[j, i],
                head_recv.at[j, i],
                {"head": peer},
            )
            for j, peer in enumerate(peers)
        ]
        for copy in heads_[i]:
            copy.start()

    held, positions = rows_out[0].shape[0] // head_size, rows_out[0].shape[1]
    trades = []

    def trade(source, target, j, i):
        there = pl.ds(pl.multiple_of(peers[j] * positions, positions), positions)
        copy = remote(
            source.at[:, there, :], target, rows_send.at[j, i], rows_recv.at[j, i], {"head": peers[j]}
        )
        copy.start()
        trades.append(copy)

    for i in range(results):
        for j in range(len(peers)):
            trade(rows_in[i], rows_out[i + 1].at[pl.ds(me * held, held)], j, i)

    def feed_start(row):
        if row == 0:
            for copy in loads:
                copy.wait()
        feed_norm(r, sums_ref.at[row], low_ref, work_ref)
        feed_middle(range(0, head_size // 2))

    def feed_middle(parts):
        for j in parts:
            feed_units(r, j, low_ref, g_ref, None)

    def feed_end(row):
        feed_out(r, work_ref, g_ref)
        gain, shift = r.gain[2:3, :].astype(F32), r.shift[2:3, :].astype(F32)
        for tile in range(work_ref.shape[0] // TILE):
            rows = tile_rows(tile)
            normed = norm_stats(work_ref[rows, :])[0]
            first_ref[row, rows, :] = (normed * gain + shift).astype(BF16)
        for j in range(len(peers)):
            trade(
                first_ref.at[pl.ds(row, 1)],
                rows_out[0].at[pl.ds(me * held + row, 1)],
                j,
                results + row,
            )

    pieces = []
    for row in range(held):
        pieces.append(functools.partial(feed_start, row))
        pieces.append(functools.partial(feed_middle, range(head_size // 2, head_size)))
        pieces.append(functools.partial(feed_end, row))

    def places(i):
        order = orders[0] if i < count // 2 else orders[1]
        offset, size, result = 0, length, []
        for stride in order:
            size //= 2
            keep = offset + digit(stride) * size
            give = offset + (1 - digit(stride)) * size
            result.append((stride, size, pl.multiple_of(keep, 16), pl.multiple_of(give, 16)))
            offset = keep
        return result

    plan = {i: places(i) for i in range(count)}
    moving = {}

    def fold(i, stage):
        stride, size, keep, give = plan[i][stage]
        base = length - (length >> stage)
        copy = remote(
            sum_ref.at[i, pl.ds(give, size), :],
            land.at[i, pl.ds(base, size), :],
            fold_send.at[stage, i],
            fold_recv.at[stage, i],
            {"dp": partner(stride)},
        )
        copy.start()
        moving[i] = copy

    def grow(i, stage):
        stride, size, keep, give = plan[i][stage]
        rows = out_ref.at[i, pl.ds(keep, size), :]
        copy = remote(
            rows, rows, grow_send.at[stage, i], grow_recv.at[stage, i], {"dp": partner(stride)}
        )
        copy.start()
        moving[i] = copy

    def task(i, number):
        if number == 0:
            locals_[i].wait()
            total = sum_ref[i].astype(F32)
            for j, copy in enumerate(heads_[i]):
                copy.wait()
                total = total + head_land[j, i].astype(F32)
            sum_ref[i] = total.astype(BF16)
            fold(i, 0)
        elif number <= depth:
            moving[i].wait()
            stage = number - 1
            stride, size, keep, give = plan[i][stage]
            base = length - (length >> stage)
            rows = pl.ds(keep, size)
            total = (
                sum_ref[i, rows, :].astype(F32) + land[i, pl.ds(base, size), :].astype(F32)
            ).astype(BF16)
            if number < depth:
                sum_ref[i, rows, :] = total
                fold(i, number)
            else:
                out_ref[i, rows, :] = total
                grow(i, depth - 1)
        else:
            moving[i].wait()
            stage = 2 * depth - number
            if stage > 0:
                grow(i, stage - 1)

    steps = 2 * depth + 1
    small_moving = None
    times = steps + count // 2 - 1
    for time in range(times):
        if time == 0:
            total = small_ref[0]
            for j, copy in enumerate(small_head):
                copy.wait()
                total = total + small_land[j]
            small_out_ref[...] = total
        elif time <= depth:
            small_moving.wait()
            small_out_ref[...] += small_land[len(peers) + time - 1]
        if time < depth:
            slot = len(peers) + time
            small_moving = remote(
                small_out_ref,
                small_land.at[slot],
                small_send.at[slot],
                small_recv.at[slot],
                {"dp": partner(orders[0][time])},
            )
            small_moving.start()
        for place, i in enumerate(queue):
            number = time - place // 2
            if 0 <= number < steps:
                task(i, number)
        for piece in pieces[time * len(pieces) // times : (time + 1) * len(pieces) // times]:
            piece()
    for copy in trades:
        copy.wait()


def reduce_grads(grads, common, shares, arrays, first_sums, weights, dp_size, head_size):
    count, results = len(grads), len(arrays)
    rows, positions, width = arrays[0].shape
    traded = jax.ShapeDtypeStruct((rows * head_size, positions // head_size, width), BF16)
    length, share = grads[0].shape[1:]
    depth = dp_size.bit_length() - 1
    peers = head_size - 1
    small = (24, common[0].shape[1])
    any_spec = pl.BlockSpec(memory_space=pl.ANY)
    vmem = pl.BlockSpec(memory_space=pltpu.VMEM)
    dma = pltpu.SemaphoreType.DMA
    return pl.pallas_call(
        functools.partial(reduce_kernel, dp_size, head_size, count, results),
        out_shape=(
            jax.ShapeDtypeStruct((count, length, share), BF16),
            jax.ShapeDtypeStruct(small, F32),
            jax.ShapeDtypeStruct(arrays[0].shape, BF16),
        )
        + (traded,) * (results + 1),
        in_specs=[any_spec] * (count + results + 1 + 2 * head_size) + [vmem] * (8 + head_size),
        out_specs=(vmem, vmem, vmem) + (any_spec,) * (results + 1),
        scratch_shapes=[
            pltpu.VMEM((peers, count, length, share), BF16),
            pltpu.VMEM((count, length, share), BF16),
            pltpu.VMEM((peers + depth,) + small, F32),
            pltpu.VMEM((head_size,) + small, F32),
            pltpu.VMEM((count, length, share), BF16),
            pltpu.VMEM(first_sums.shape, F32),
            pltpu.VMEM((head_size,) + weights["ffn_in"][0].shape, BF16),
            pltpu.VMEM((head_size,) + weights["ffn_out"][0].shape, BF16),
            pltpu.VMEM((positions, width), BF16),
            pltpu.VMEM((positions, width), F32),
            pltpu.VMEM((positions, head_size * weights["ffn_in"][0].shape[1]), BF16),
            dma((count,)),
            dma((peers, count)),
            dma((peers, count)),
            dma((depth, count)),
            dma((depth, count)),
            dma((depth, count)),
            dma((depth, count)),
            dma((peers + depth,)),
            dma((peers + depth,)),
            dma((peers, results + rows)),
            dma((peers, results + rows)),
            dma((1 + 2 * head_size,)),
        ],
        compiler_params=pltpu.CompilerParams(
            collective_id=0, has_side_effects=True, vmem_limit_bytes=VMEM_BYTES
        ),
        name="reduce",
    )(
        *grads,
        *arrays,
        first_sums,
        *weights["ffn_in"],
        *weights["ffn_out"],
        weights["out_bias"],
        weights["gain"],
        weights["shift"],
        *weights["ffn_bias"],
        *common,
        *shares,
    )


def finish_kernel(results, *refs):
    place_ref, refs = refs[0], list(refs[1:])

    def take(number):
        taken = refs[:number]
        del refs[:number]
        return taken

    own, arrived = take(results), take(results)
    summed_ref, feed_in_ref, feed_out_ref = take(3)
    rows_out = take(results)
    qkv_ref, kv_ref, self_out_ref, cross_q_ref, cross_out_ref, ffn_in_ref, ffn_out_ref = take(7)
    step = pl.program_id(0)
    rows = pl.num_programs(0) // place_ref[1]
    mine = step // rows == place_ref[0]
    for i in range(results):
        rows_out[i][...] = jnp.where(mine, own[i][...], arrived[i][...])
    ffn_in_ref[...] = feed_in_ref[...].astype(F32)
    ffn_out_ref[...] = feed_out_ref[...].astype(F32).T

    def at(number, target_ref, turned):
        @pl.when(step == number)
        def write():
            values = summed_ref[...].astype(F32)
            target_ref[...] = values.T if turned else values

    for number, (target_ref, turned) in enumerate(
        [(cross_q_ref, False), (kv_ref, False), (kv_ref, False), (cross_out_ref, True)]
        + [(qkv_ref, False)] * 3
        + [(self_out_ref, True)]
    ):
        at(number, target_ref, turned)


def finish(place, arrays, arrived, summed, feed_grads, head_size):
    results = len(arrays)
    rows, length, width = arrays[0].shape
    held, positions = rows * head_size, length // head_size
    share, units = summed.shape[2], feed_grads.shape[2]
    steps = summed.shape[0]
    if held != steps:
        raise ValueError(held)
    pieces = max(1, min(steps, units // 128))
    tall, wide = width // steps, units // pieces

    def clip(step, low, high):
        return jnp.clip(step - low, 0, high)

    def own_row(step, place):
        return (jnp.clip(step - place[0] * rows, 0, rows - 1), place[0], 0)

    def arrived_row(step, place):
        other = ((place[0] + 1) % place[1]) * rows
        return (jnp.where(step // rows == place[0], other, step), 0, 0)

    block = (None, positions, width)
    return pl.pallas_call(
        functools.partial(finish_kernel, results),
        grid_spec=pltpu.PrefetchScalarGridSpec(
            num_scalar_prefetch=1,
            grid=(steps,),
            in_specs=[pl.BlockSpec(block, own_row)] * results
            + [pl.BlockSpec(block, arrived_row)] * results
            + [
                pl.BlockSpec((None, width, share), lambda step, _: (step, 0, 0)),
                pl.BlockSpec((None, tall, units), lambda step, _: (0, step, 0)),
                pl.BlockSpec(
                    (None, width, wide), lambda step, _: (1, 0, clip(step, 0, pieces - 1))
                ),
            ],
            out_specs=(pl.BlockSpec(block, lambda step, _: (step, 0, 0)),) * results
            + (
                pl.BlockSpec((None, width, share), lambda step, _: (clip(step, 4, 2), 0, 0)),
                pl.BlockSpec((None, width, share), lambda step, _: (clip(step, 1, 1), 0, 0)),
                pl.BlockSpec((share, width), lambda step, _: (0, 0)),
                pl.BlockSpec((width, share), lambda step, _: (0, 0)),
                pl.BlockSpec((share, width), lambda step, _: (0, 0)),
                pl.BlockSpec((tall, units), lambda step, _: (step, 0)),
                pl.BlockSpec((wide, width), lambda step, _: (clip(step, 0, pieces - 1), 0)),
            ),
        ),
        out_shape=(jax.ShapeDtypeStruct((held, positions, width), BF16),) * results
        + tuple(
            jax.ShapeDtypeStruct(shape, F32)
            for shape in (
                (3, width, share),
                (2, width, share),
                (share, width),
                (width, share),
                (share, width),
                (width, units),
                (units, width),
            )
        ),
        compiler_params=pltpu.CompilerParams(
            dimension_semantics=("arbitrary",), vmem_limit_bytes=VMEM_BYTES
        ),
        name="finish",
    )(place, *arrays, *arrived, summed, feed_grads, feed_grads)


def window_starts(query_segments, key_segments, window):
    rows, length = query_segments.shape
    tiles = query_segments.reshape(rows, length // TILE, TILE)
    first, last = tiles[:, :, 0], tiles[:, :, -1]
    before = jnp.sum(key_segments[:, None, :] < first[:, :, None], axis=2).astype(jnp.int32)
    after = jnp.sum(key_segments[:, None, :] <= last[:, :, None], axis=2).astype(jnp.int32)
    start = jnp.minimum((before // 16) * 16, key_segments.shape[1] - window)
    return jnp.where(after - start <= window, start, -1).reshape(-1)


def constants(width, levels):
    heads = width // HEAD_DIM
    lane = np.arange(PAIR)
    sides = np.stack([lane < HEAD_DIM, lane >= HEAD_DIM])
    kept = (lane >= 16) & (lane < 16 + 3 * heads)
    own = np.stack([(lane < levels) | (kept & ((lane - 16) % heads == h)) for h in range(heads)])
    spread = kept[None, :] & (
        (lane[None, :] - 16) % heads == np.arange(width)[:, None] // HEAD_DIM
    )

    def tall(rows):
        return jnp.asarray(np.broadcast_to(rows[:, None, :], (rows.shape[0], TILE, PAIR)), BF16)

    return {"sides": tall(sides), "own": tall(own), "spread": jnp.asarray(spread, BF16)}


def local_layer(
    place,
    rows,
    source,
    mixed,
    memory,
    cotangent,
    tgt_segments,
    src_segments,
    levels,
    weights,
    feed_total=lambda own, sent: own,
):
    head_size = len(weights["ffn_in"])
    held, length = tgt_segments.shape
    width = mixed[0].shape[2]
    hidden = weights["ffn_in"][0].shape[1] * head_size
    heads = width // HEAD_DIM
    tiles = length // TILE
    window = min(WINDOW, length)
    share = width // head_size
    marks = constants(width, levels)
    sides = {"sides": marks["sides"]}
    alone = {"place": place}
    starts = alone | {
        "starts": jnp.concatenate(
            [
                window_starts(tgt_segments, tgt_segments, window),
                window_starts(tgt_segments, src_segments, window),
            ]
        )
    }
    tgt = {"tgt": tgt_segments[:, None, :]}
    src = {"src": src_segments[:, None, :]}

    def pick(*keys):
        return {key: weights[key] for key in keys}

    def parts_of(*keys):
        return {key + "_parts": weights[key] for key in keys}

    wide_low = ((rows, length, width), BF16)
    wide = ((rows, length, width), F32)
    stats = ((rows, tiles, heads, TILE), F32)
    one_low, one = ((length, width), BF16), ((length, width), F32)
    mark = ((length, PAIR), BF16)
    square, square_low = ((width, width), F32), ((width, width), BF16)
    split = ((head_size, width, share), BF16)
    common, shares = ((16, width), F32), ((head_size, 8, share), F32)
    norms = pick("out_bias", "gain", "shift")
    feed = pick("ffn_in", "ffn_out", "ffn_bias")
    self_qkv = {"self_qkv": ((3, width, width), BF16)}
    cross_kv = {"cross_kv": ((2, width, width), BF16)}
    marks_scratch = {"far": mark, "near": mark}
    half = ((2, width, hidden // head_size), BF16)
    kept = call_rows(
        attention_kernel,
        "attention",
        rows,
        levels,
        starts,
        {"x_parts": mixed[:1], "memory_parts": memory[:1]} | tgt | src,
        {("x_parts", j): part for j, part in enumerate(mixed[1:])}
        | {("memory_parts", j): part for j, part in enumerate(memory[1:])},
        sides
        | parts_of("self_qkv", "self_out", "cross_q", "cross_kv", "cross_out")
        | pick("head_bias")
        | norms,
        {key: wide_low for key in ("q", "k", "v", "ctx", "a1", "q2", "k2", "v2", "ctx2")}
        | {"lse": stats, "lse2": stats, "r1": wide, "r2": wide},
        {},
        {"work": one, "x": one_low, "memory": one_low}
        | {key: square_low for key in ("self_out", "cross_q", "cross_out")}
        | self_qkv
        | cross_kv
        | marks_scratch,
    )
    fed = call_rows(
        feed_kernel,
        "feed",
        rows,
        levels,
        alone,
        {"cot_parts": cotangent},
        {"r2": kept["r2"]},
        feed | norms,
        {"second": wide_low, "dr2": wide},
        {"own_grads": half, "common": common, "shares": shares}
        | {("sent_grads", j): half for j in range(1, head_size)},
        {
            "cot": one_low,
            "a2": one_low,
            "df": one_low,
            "work": one,
            "g": ((length, hidden), BF16),
            "du": ((length, hidden), BF16),
            "slope": ((length, hidden), BF16),
            "in_total": ((width, hidden), F32),
            "out_total": ((width, hidden), F32),
        },
    )
    sent = [fed[("sent_grads", j)] for j in range(1, head_size)]
    dr2, feed_grads = feed_total(fed["dr2"], fed["own_grads"], sent)
    totals = {"total_" + key: square for key in "qkvo"}
    back_scratch = (
        totals
        | marks_scratch
        | {key: one_low for key in ("dctx", "low", "dq", "dk_low", "dv_low")}
        | {"dk": one, "dv": one}
    )
    crossed = call_rows(
        cross_back_kernel,
        "cross_back",
        rows,
        levels,
        starts,
        {"memory_parts": memory[:1]} | tgt | src,
        {key: kept[key] for key in ("q2", "k2", "v2", "ctx2", "lse2", "r1", "a1")}
        | {"dr2": dr2}
        | {("memory_parts", j): part for j, part in enumerate(memory[1:])},
        marks | parts_of("cross_q", "cross_kv", "cross_out") | pick("gain"),
        {"memory_grad": wide_low, "dr1": wide},
        {key: split for key in ("cross_q_grad", "cross_k_grad", "cross_v_grad", "cross_out_grad")}
        | {"common": common, "shares": shares},
        back_scratch
        | cross_kv
        | {"work": one, "memory": one_low, "cross_q": square_low, "cross_out": square_low},
    )
    selfed = call_rows(
        self_back_kernel,
        "self_back",
        rows,
        levels,
        starts,
        {"x_parts": mixed[:1]} | tgt,
        {key: kept[key] for key in ("q", "k", "v", "ctx", "lse")}
        | {"dr1": crossed["dr1"]}
        | {("x_parts", j): part for j, part in enumerate(mixed[1:])},
        marks | parts_of("self_qkv", "self_out"),
        {"input_grad": wide_low},
        {key: split for key in ("self_q_grad", "self_k_grad", "self_v_grad", "self_out_grad")}
        | {"shares": shares},
        back_scratch | self_qkv | {"x": one_low, "self_out": square_low},
    )
    keys2, input_grad = lax.optimization_barrier((kept["k2"], selfed["input_grad"]))
    first = call_rows(
        first_pass_kernel,
        "first_pass",
        rows,
        levels,
        starts,
        {"x_parts": source} | tgt | src,
        {"k2": keys2, "v2": kept["v2"]},
        sides
        | parts_of("self_qkv", "self_out", "cross_q", "cross_out")
        | pick("head_bias")
        | norms,
        {"r2": wide},
        {},
        {key: one_low for key in ("x", "q", "k", "v", "ctx", "low")}
        | {"work": one}
        | {key: square_low for key in ("self_out", "cross_q", "cross_out")}
        | self_qkv
        | marks_scratch,
    )
    grads = tuple(
        crossed[key] for key in ("cross_q_grad", "cross_k_grad", "cross_v_grad", "cross_out_grad")
    ) + tuple(selfed[key] for key in ("self_q_grad", "self_k_grad", "self_v_grad", "self_out_grad"))
    return (
        first["r2"],
        (fed["second"], input_grad, crossed["memory_grad"]),
        feed_grads,
        grads,
        (fed["common"], crossed["common"]),
        (fed["shares"], crossed["shares"], selfed["shares"]),
    )


def body(
    dp_size,
    head_size,
    source_copy,
    target_embed,
    memory,
    tgt_segments,
    src_segments,
    hamming,
    priority,
    cotangent,
    self_qkv,
    self_out,
    cross_q,
    cross_kv,
    cross_out,
    ffn_in,
    ffn_out,
    head_bias,
    ffn_bias,
    out_bias,
    norm_gain,
    norm_shift,
):
    me = lax.axis_index("head")
    levels = hamming.shape[1]
    held, share, width = source_copy.shape
    rows = held // head_size

    def own_positions(array):
        return lax.dynamic_slice_in_dim(array, me * share, share, 1)

    level = jnp.arange(levels, dtype=jnp.int32)
    chosen = own_positions(tgt_segments)[:, :, None] == level[None, None, :]
    limits = jnp.sum(jnp.where(chosen, hamming[:, None, :], 0), axis=2)
    glanced = own_positions(priority) < limits
    mixed = jnp.where(glanced[:, :, None], target_embed, source_copy)
    weights = {
        "self_qkv": own_first(self_qkv, head_size),
        "self_out": own_first(self_out, head_size),
        "cross_q": own_first(cross_q, head_size),
        "cross_kv": own_first(cross_kv, head_size),
        "cross_out": own_first(cross_out, head_size),
        "head_bias": own_first(head_bias, head_size),
        "out_bias": out_bias,
        "gain": norm_gain,
        "shift": norm_shift,
    }
    memory_shares = row_shares(memory, rows, me, head_size)
    mixed_shares = row_shares(mixed, rows, me, head_size)
    ffn_bias, ffn_in, ffn_out, cotangent, source_copy, mixed_shares = lax.optimization_barrier(
        (ffn_bias, ffn_in, ffn_out, cotangent, source_copy, mixed_shares)
    )
    weights["ffn_bias"] = own_first(ffn_bias[None, :], head_size)
    weights["ffn_in"] = own_first(ffn_in, head_size)
    weights["ffn_out"] = own_first(ffn_out, head_size)

    def feed_total(later, own, sent):
        arrived = [
            lax.ppermute(part, "head", [(i, (i + j + 1) % head_size) for i in range(head_size)])
            for j, part in enumerate(sent)
        ]
        total = own.astype(F32)
        for part in arrived:
            total = total + part.astype(F32)
        later, total = lax.optimization_barrier((later, total.astype(BF16)))
        return later, lax.psum(total, "dp")

    first_sums, arrays, feed_grads, grads, common, shares = local_layer(
        me.astype(jnp.int32).reshape(1),
        rows,
        own_first(source_copy, head_size),
        (mixed,) + mixed_shares,
        (memory,) + memory_shares,
        own_first(cotangent, head_size),
        tgt_segments,
        src_segments,
        levels,
        weights,
        feed_total,
    )
    summed, sums, first, *arrived = reduce_grads(
        grads, common, shares, arrays, first_sums, weights, dp_size, head_size
    )
    place = jnp.stack([me.astype(jnp.int32), jnp.int32(head_size)])
    *outs, qkv, kv, self_out, cross_q, cross_out, ffn_in, ffn_out = finish(
        place, (first, *arrays), arrived, summed, feed_grads, head_size
    )
    part = width // head_size

    return (
        *outs,
        qkv,
        self_out,
        cross_q,
        kv,
        cross_out,
        ffn_in,
        ffn_out,
        sums[16:20, :part],
        sums[20:24, :part].reshape(-1),
        sums[0:3],
        sums[3:6],
        sums[6:9],
    )


def solution(mesh):
    split = P("dp", "head", None)
    rows = P("dp", None)
    last, last_two, first = P(None, "head"), P(None, None, "head"), P("head", None)
    return jax.shard_map(
        functools.partial(body, mesh.shape["dp"], mesh.shape["head"]),
        mesh=mesh,
        in_specs=(split, split, split, rows, rows, rows, rows, split)
        + (last_two, first, last, last_two, first, last, first, last, P("head"), P(), P(), P()),
        out_specs=(split, split, split, split)
        + (last_two, first, last, last_two, first, last, first, last, P("head"), P(), P(), P()),
        check_vma=False,
    )
```

```python
import functools

import jax
import jax.numpy as jnp
import numpy as np
from jax import lax
from jax.experimental import pallas as pl
from jax.experimental.pallas import tpu as pltpu
from jax.sharding import PartitionSpec as P

HEAD_DIM = 64
PAIR = 2 * HEAD_DIM
TILE = 128
WINDOW = 256
EARLY = 2
FAR = -1e30
F32 = jnp.float32
BF16 = jnp.bfloat16
VMEM_BYTES = 60 * 1024 * 1024


def dot_nn(left, right):
    return lax.dot_general(left, right, (((1,), (0,)), ((), ())), preferred_element_type=F32)


def dot_nt(left, right):
    return lax.dot_general(left, right, (((1,), (1,)), ((), ())), preferred_element_type=F32)


def norm_stats(sums):
    row_mean = jnp.mean(sums, axis=-1, keepdims=True)
    centred = sums - row_mean
    spread = jnp.mean(centred * centred, axis=-1, keepdims=True)
    inverse = lax.rsqrt(spread + 1e-05)
    return centred * inverse, inverse


def norm_back(normed, inverse, gain_row, incoming):
    scaled = incoming * gain_row
    mean_one = jnp.mean(scaled, axis=-1, keepdims=True)
    mean_two = jnp.mean(scaled * normed, axis=-1, keepdims=True)
    grad = (scaled - mean_one - normed * mean_two) * inverse
    gain_part = jnp.sum(incoming * normed, axis=0, keepdims=True)
    shift_part = jnp.sum(incoming, axis=0, keepdims=True)
    return grad, gain_part, shift_part


def gelu_parts(pre):
    ratio = pltpu.reciprocal(1.0 + 0.23164189015488 * jnp.abs(pre), approx=True)
    series = ratio * (
        0.127414796
        + ratio
        * (-0.142248368 + ratio * (0.7107068705 + ratio * (-0.7265760135 + ratio * 0.5307027145)))
    )
    bell = jnp.exp(-0.5 * (pre * pre))
    tail = series * bell
    return jnp.where(pre >= 0, 1.0 - tail, tail), bell


def each_tile(count, step):
    for index in range(count):
        step(index)


def tile_rows(tile):
    start = tile * TILE
    return pl.ds(start if isinstance(start, int) else pl.multiple_of(start, TILE), TILE)


def window_loop(starts_ref, base, tiles, length, step):
    starts = [starts_ref[base + tile] for tile in range(tiles)]
    least = functools.reduce(jnp.minimum, starts)
    window = min(WINDOW, length)

    @pl.when(least >= 0)
    def straight():
        for tile in range(tiles):
            step(tile, pl.multiple_of(starts[tile], 16), window)

    if length > WINDOW:

        @pl.when(least < 0)
        def mixed():
            def one(tile, carry):
                start = starts_ref[base + tile]

                @pl.when(start >= 0)
                def near():
                    step(tile, pl.multiple_of(start, 16), window)

                @pl.when(start < 0)
                def whole():
                    step(tile, 0, length)

                return carry

            lax.fori_loop(0, tiles, one, 0)


def make_marks(segment_row, levels, heads):
    shape = (PAIR, segment_row.shape[1])
    level = lax.broadcasted_iota(jnp.int32, shape, 0)
    same = level == segment_row
    near = jnp.where(same | ((level >= 16) & (level < 16 + 3 * heads)), 1.0, 0.0)
    far = jnp.where(same | (level >= levels), 0.0, FAR)
    return far.T.astype(BF16), near.T.astype(BF16)


def attend(q_ref, k_ref, v_ref, far_ref, near_ref, sides_ref, ctx_ref, lse_ref, tile, start, window):
    pairs = range(q_ref.shape[1] // PAIR)
    lanes = [slice(p * PAIR, (p + 1) * PAIR) for p in pairs]
    rows = tile_rows(tile)
    keys = pl.ds(start, window)
    left, right = sides_ref[0], sides_ref[1]
    query_marks = far_ref[rows, :]
    key_marks = near_ref[keys, :]
    stacked = []
    for p in pairs:
        queries = q_ref[rows, lanes[p]]
        stacked.append(
            jnp.concatenate(
                [
                    jnp.concatenate([queries * left, query_marks], axis=1),
                    jnp.concatenate([queries * right, query_marks], axis=1),
                ],
                axis=0,
            )
        )
    scores = [
        dot_nt(jnp.concatenate([k_ref[keys, lanes[p]], key_marks], axis=1), stacked[p])
        for p in pairs
    ]
    peaks = [jnp.max(s, axis=0, keepdims=True) for s in scores]
    weights = [jnp.exp(s - m) for s, m in zip(scores, peaks)]
    totals = [jnp.sum(w, axis=0, keepdims=True) for w in weights]
    low = [w.astype(BF16) for w in weights]
    turned = [v_ref[keys, lanes[p]].T for p in pairs]
    mixed = [dot_nn(turned[p], low[p]) for p in pairs]
    shares = [pltpu.reciprocal(t, approx=True) for t in totals]
    context = [
        jnp.concatenate(
            [
                mixed[p][:HEAD_DIM, :TILE] * shares[p][:, :TILE],
                mixed[p][HEAD_DIM:, TILE:] * shares[p][:, TILE:],
            ],
            axis=0,
        )
        for p in pairs
    ]
    for p in pairs:
        ctx_ref[rows, lanes[p]] = context[p].T.astype(BF16)
    if lse_ref is not None:
        for p in pairs:
            log_total = peaks[p] + jnp.log(totals[p])
            lse_ref[tile, pl.ds(2 * p, 1), :] = log_total[:, :TILE]
            lse_ref[tile, pl.ds(2 * p + 1, 1), :] = log_total[:, TILE:]


def three_parts(values):
    high = values.astype(BF16).astype(F32)
    rest = values - high
    middle = rest.astype(BF16).astype(F32)
    return high, middle, rest - middle


def attend_back(
    q_ref,
    k_ref,
    v_ref,
    far_ref,
    near_ref,
    sides_ref,
    own_ref,
    spread_ref,
    lse_ref,
    ctx_ref,
    dctx_ref,
    dq_ref,
    dk_ref,
    dv_ref,
    starts_ref,
    base,
):
    length, width = q_ref.shape
    pairs = range(width // PAIR)
    heads = width // HEAD_DIM
    lanes = [slice(p * PAIR, (p + 1) * PAIR) for p in pairs]
    dk_ref[...] = jnp.zeros_like(dk_ref)
    dv_ref[...] = jnp.zeros_like(dv_ref)

    def step(tile, start, window):
        rows = tile_rows(tile)
        keys = pl.ds(start, window)
        left, right = sides_ref[0], sides_ref[1]
        key_marks = near_ref[keys, :]
        high, middle, rest = three_parts(-lse_ref[tile])
        stats = jnp.concatenate(
            [
                jnp.zeros((16, TILE), F32),
                high,
                middle,
                rest,
                jnp.zeros((TILE - 16 - 3 * heads, TILE), F32),
            ],
            axis=0,
        )
        query_marks = far_ref[rows, :] + stats.T.astype(BF16)
        product = dctx_ref[rows, :].astype(F32) * ctx_ref[rows, :].astype(F32)
        product_high = product.astype(BF16)
        product_rest = (product - product_high.astype(F32)).astype(BF16)
        delta = -(dot_nn(product_high, spread_ref[...]) + dot_nn(product_rest, spread_ref[...]))
        high, middle, rest = three_parts(delta)
        lane = lax.broadcasted_iota(jnp.int32, delta.shape, 1)
        grad_marks = jnp.where(
            lane < 16 + heads, high, jnp.where(lane < 16 + 2 * heads, middle, rest)
        ).astype(BF16)
        query_stack, grad_stack, query_side, grad_side, key_rows = [], [], [], [], []
        for p in pairs:
            queries = q_ref[rows, lanes[p]]
            grads = dctx_ref[rows, lanes[p]]
            key_rows.append(k_ref[keys, lanes[p]])
            query_stack.append(jnp.concatenate([queries * left, queries * right], axis=0))
            grad_stack.append(jnp.concatenate([grads * left, grads * right], axis=0))
            one, two = own_ref[2 * p], own_ref[2 * p + 1]
            marks = jnp.concatenate([query_marks * one, query_marks * two], axis=0)
            query_side.append(jnp.concatenate([query_stack[p], marks], axis=1))
            marks = jnp.concatenate([grad_marks * one, grad_marks * two], axis=0)
            grad_side.append(jnp.concatenate([grad_stack[p], marks], axis=1))
        scores = [
            dot_nt(jnp.concatenate([key_rows[p], key_marks], axis=1), query_side[p]) for p in pairs
        ]
        probs_grad = [
            dot_nt(jnp.concatenate([v_ref[keys, lanes[p]], key_marks], axis=1), grad_side[p])
            for p in pairs
        ]
        probs = [jnp.exp(s) for s in scores]
        probs_low = [w.astype(BF16) for w in probs]
        scores_grad = [(probs[p] * probs_grad[p]).astype(BF16) for p in pairs]
        turned_keys = [key_rows[p].T for p in pairs]
        for p in pairs:
            dv_ref[keys, lanes[p]] += dot_nn(probs_low[p], grad_stack[p])
        for p in pairs:
            dk_ref[keys, lanes[p]] += dot_nn(scores_grad[p], query_stack[p])
        turned = [dot_nn(turned_keys[p], scores_grad[p]) for p in pairs]
        for p in pairs:
            both = jnp.concatenate(
                [turned[p][:HEAD_DIM, :TILE], turned[p][HEAD_DIM:, TILE:]], axis=0
            )
            dq_ref[rows, lanes[p]] = (both.T * (HEAD_DIM**-0.5)).astype(BF16)

    window_loop(starts_ref, base, length // TILE, length, step)


def join_positions(target_ref, parts, place):
    share = parts[0].shape[0]
    for j, part in enumerate(parts):
        start = ((place + j) % len(parts)) * share
        target_ref[pl.ds(pl.multiple_of(start, share), share), :] = part[...]


def join_all(pairs):
    for target_ref, parts, axis in pairs:
        share = parts[0].shape[axis]
        for j, part in enumerate(parts):
            where = [slice(None)] * len(target_ref.shape)
            where[axis] = slice(j * share, (j + 1) * share)
            target_ref[tuple(where)] = part[...]


def join_weights(pairs):
    @pl.when(pl.program_id(0) == 0)
    def join():
        join_all(pairs)


def joined(parts):
    return jnp.concatenate([part[...].astype(F32) for part in parts], axis=1)


def window_base(r, tiles, cross):
    rows = pl.num_programs(0)
    row = r.place[0] * rows + pl.program_id(0)
    held = r.starts.shape[0] // (2 * tiles)
    return (row + held * cross) * tiles


def self_start(r, x_ref, segment_row, near_ref, far_ref, q_ref, k_ref, v_ref, levels):
    far, near = make_marks(segment_row, levels, x_ref.shape[1] // HEAD_DIM)
    far_ref[...] = far
    near_ref[...] = near
    bias = joined(r.head_bias)
    inputs = x_ref[...]
    queries = (dot_nn(inputs, r.self_qkv[0]) + bias[0:1, :]).astype(BF16)
    q_ref[...] = queries * jnp.asarray(HEAD_DIM**-0.5, BF16)
    k_ref[...] = dot_nn(inputs, r.self_qkv[1]).astype(BF16)
    v_ref[...] = (dot_nn(inputs, r.self_qkv[2]) + bias[1:2, :]).astype(BF16)


def self_end(r, x_ref, ctx_ref, r1_ref, a1_ref, work_ref):
    work_ref[...] = dot_nn(ctx_ref[...], r.self_out[...])
    out_bias = r.out_bias[0:1, :].astype(F32)
    gain, shift = r.gain[0:1, :].astype(F32), r.shift[0:1, :].astype(F32)

    def step(tile):
        rows = tile_rows(tile)
        sums = x_ref[rows, :].astype(F32) + (work_ref[rows, :] + out_bias)
        if r1_ref is not None:
            r1_ref[rows, :] = sums
        normed = norm_stats(sums)[0] * gain + shift
        work_ref[rows, :] = normed
        a1_ref[rows, :] = normed.astype(BF16)

    each_tile(x_ref.shape[0] // TILE, step)


def cross_start(r, segment_row, near_ref, a1_ref, q2_ref, levels):
    near_ref[...] = make_marks(segment_row, levels, q2_ref.shape[1] // HEAD_DIM)[1]
    bias = joined(r.head_bias)
    queries = (dot_nn(a1_ref[...], r.cross_q[...]) + bias[2:3, :]).astype(BF16)
    q2_ref[...] = queries * jnp.asarray(HEAD_DIM**-0.5, BF16)


def cross_end(r, ctx2_ref, r2_ref, work_ref):
    r2_ref[...] = work_ref[...] + (
        dot_nn(ctx2_ref[...], r.cross_out[...]) + r.out_bias[1:2, :].astype(F32)
    )


def attention_weights(r):
    return [
        (r.self_qkv, r.self_qkv_parts, 2),
        (r.self_out, r.self_out_parts, 0),
        (r.cross_q, r.cross_q_parts, 1),
        (r.cross_out, r.cross_out_parts, 0),
    ]


def attention_kernel(levels, r):
    join_weights(attention_weights(r) + [(r.cross_kv, r.cross_kv_parts, 2)])
    join_positions(r.x, r.x_parts, r.place[0])
    join_positions(r.memory, r.memory_parts, r.place[0])
    length, tiles = r.x.shape[0], r.x.shape[0] // TILE
    self_start(r, r.x, r.tgt[...], r.near, r.far, r.q, r.k, r.v, levels)
    step = functools.partial(attend, r.q, r.k, r.v, r.far, r.near, r.sides, r.ctx, r.lse)
    window_loop(r.starts, window_base(r, tiles, 0), tiles, length, step)
    self_end(r, r.x, r.ctx, r.r1, r.a1, r.work)
    bias = joined(r.head_bias)
    r.k2[...] = dot_nn(r.memory[...], r.cross_kv[0]).astype(BF16)
    r.v2[...] = (dot_nn(r.memory[...], r.cross_kv[1]) + bias[3:4, :]).astype(BF16)
    cross_start(r, r.src[...], r.near, r.a1, r.q2, levels)
    step = functools.partial(attend, r.q2, r.k2, r.v2, r.far, r.near, r.sides, r.ctx2, r.lse2)
    window_loop(r.starts, window_base(r, tiles, 1), tiles, length, step)
    cross_end(r, r.ctx2, r.r2, r.work)


def feed_norm(r, r2_ref, a2_ref, work_ref):
    gain, shift = r.gain[1:2, :].astype(F32), r.shift[1:2, :].astype(F32)

    def step(tile):
        rows = tile_rows(tile)
        normed = norm_stats(r2_ref[rows, :])[0] * gain + shift
        work_ref[rows, :] = normed
        a2_ref[rows, :] = normed.astype(BF16)

    each_tile(r2_ref.shape[0] // TILE, step)


def feed_units(r, j, a2_ref, g_ref, slope_ref):
    units = r.ffn_in[j].shape[1]
    chunk = min(256, units)
    for first in range(0, units, chunk):
        cut = slice(first, first + chunk)
        pre = dot_nn(a2_ref[...], r.ffn_in[j][:, cut]) + r.ffn_bias[j][:, cut].astype(F32)
        phi, bell = gelu_parts(pre)
        cut = slice(j * units + first, j * units + first + chunk)
        g_ref[:, cut] = (pre * phi).astype(BF16)
        if slope_ref is not None:
            slope_ref[:, cut] = (phi + (pre * bell) * 0.3989422804014327).astype(BF16)


def feed_out(r, work_ref, g_ref):
    units = r.ffn_in[0].shape[1]
    fed = r.out_bias[2:3, :].astype(F32)
    for j in range(len(r.ffn_out)):
        fed = fed + dot_nn(g_ref[:, j * units : (j + 1) * units], r.ffn_out[j][...])
    work_ref[...] += fed


def add_grad(total_ref, left, right):
    total_ref[...] += dot_nn(left, right)


def start_totals(refs):
    @pl.when(pl.program_id(0) == 0)
    def clear():
        for ref in refs:
            ref[...] = jnp.zeros_like(ref)


def end_totals(pairs):
    @pl.when(pl.program_id(0) == pl.num_programs(0) - 1)
    def write():
        for total_ref, out_ref in pairs:
            share = out_ref.shape[2]
            for j in range(out_ref.shape[0]):
                out_ref[j] = total_ref[:, j * share : (j + 1) * share].astype(BF16)


def end_feed_totals(r):
    @pl.when(pl.program_id(0) == pl.num_programs(0) - 1)
    def write():
        share = r.own_grads.shape[2]
        for which, total_ref in enumerate((r.in_total, r.out_total)):
            r.own_grads[which] = total_ref[:, 0:share].astype(BF16)
            for j, out_ref in enumerate(r.sent_grads):
                out_ref[which] = total_ref[:, (j + 1) * share : (j + 2) * share].astype(BF16)


def column_total(values):
    return jnp.sum(values.astype(F32), axis=0, keepdims=True)


def add_share(share_ref, row, values):
    share = share_ref.shape[2]
    for j in range(share_ref.shape[0]):
        share_ref[j, row : row + 1, :] += values[:, j * share : (j + 1) * share]


def feed_kernel(levels, r):
    length = r.r2.shape[0]
    units = r.ffn_in[0].shape[1]
    chunk = min(256, units)
    start_totals([r.in_total, r.out_total, r.common, r.shares])
    join_positions(r.cot, r.cot_parts, r.place[0])
    feed_norm(r, r.r2, r.a2, r.work)
    for j in range(len(r.ffn_in)):
        feed_units(r, j, r.a2, r.g, r.slope)
    feed_out(r, r.work, r.g)
    gain, shift = r.gain[...].astype(F32), r.shift[...].astype(F32)

    def last_norm(tile):
        rows = tile_rows(tile)
        normed, inverse = norm_stats(r.work[rows, :])
        r.second[rows, :] = (normed * gain[2:3, :] + shift[2:3, :]).astype(BF16)
        grad, gain_part, shift_part = norm_back(
            normed, inverse, gain[2:3, :], r.cot[rows, :].astype(F32)
        )
        r.work[rows, :] = grad
        low = grad.astype(BF16)
        r.df[rows, :] = low
        r.common[2:3, :] += column_total(low)
        r.common[5:6, :] += gain_part
        r.common[8:9, :] += shift_part

    each_tile(length // TILE, last_norm)
    spots = [(j, first) for j in range(len(r.ffn_in)) for first in range(0, units, chunk)]

    def product(spot):
        j, first = spot
        return dot_nt(r.df[...], r.ffn_out[j][first : first + chunk, :])

    share = r.shares.shape[2]
    following = product(spots[0])
    for index, (j, first) in enumerate(spots):
        hidden_grad = following.astype(BF16)
        if index + 1 < len(spots):
            following = product(spots[index + 1])
        cut = slice(j * units + first, j * units + first + chunk)
        pre_grad = (hidden_grad.astype(F32) * r.slope[:, cut].astype(F32)).astype(BF16)
        r.du[:, cut] = pre_grad
        sums = column_total(pre_grad)
        for piece in range(0, chunk, share):
            row = 4 + (first + piece) // share
            r.shares[j, row : row + 1, :] += sums[:, piece : piece + share]
    back = r.work[...]
    for j in range(len(r.ffn_in)):
        back = back + dot_nt(r.du[:, j * units : (j + 1) * units], r.ffn_in[j][...])
    r.work[...] = back

    def middle_norm(tile):
        rows = tile_rows(tile)
        normed, inverse = norm_stats(r.r2[rows, :])
        grad, gain_part, shift_part = norm_back(normed, inverse, gain[1:2, :], r.work[rows, :])
        r.dr2[rows, :] = grad
        low = grad.astype(BF16)
        r.common[1:2, :] += column_total(low)
        r.common[4:5, :] += gain_part
        r.common[7:8, :] += shift_part

    each_tile(length // TILE, middle_norm)
    turned = r.a2[...].T
    hidden = r.du.shape[1]
    wide = min(512, hidden)
    for first in range(0, hidden, wide):
        cut = slice(first, first + wide)
        r.in_total[:, cut] += dot_nn(turned, r.du[:, cut])
    turned = r.df[...].T
    for first in range(0, hidden, wide):
        cut = slice(first, first + wide)
        r.out_total[:, cut] += dot_nn(turned, r.g[:, cut])
    end_feed_totals(r)


def cross_back_kernel(levels, r):
    tiles, width = r.dr2.shape[0] // TILE, r.dr2.shape[1]
    start_totals([r.total_q, r.total_k, r.total_v, r.total_o, r.common, r.shares])
    join_weights(
        [
            (r.cross_q, r.cross_q_parts, 1),
            (r.cross_kv, r.cross_kv_parts, 2),
            (r.cross_out, r.cross_out_parts, 0),
        ]
    )
    join_positions(r.memory, r.memory_parts, r.place[0])
    far, unused = make_marks(r.tgt[...], levels, width // HEAD_DIM)
    unused, near = make_marks(r.src[...], levels, width // HEAD_DIM)
    r.far[...] = far
    r.near[...] = near
    r.low[...] = r.dr2[...].astype(BF16)
    r.dctx[...] = dot_nt(r.low[...], r.cross_out[...]).astype(BF16)
    base = window_base(r, tiles, 1)
    attend_back(
        r.q2,
        r.k2,
        r.v2,
        r.far,
        r.near,
        r.sides,
        r.own,
        r.spread,
        r.lse2,
        r.ctx2,
        r.dctx,
        r.dq,
        r.dk,
        r.dv,
        r.starts,
        base,
    )
    r.dk_low[...] = r.dk[...].astype(BF16)
    r.dv_low[...] = r.dv[...].astype(BF16)
    r.memory_grad[...] = (
        dot_nt(r.dk_low[...], r.cross_kv[0]) + dot_nt(r.dv_low[...], r.cross_kv[1])
    ).astype(BF16)
    r.work[...] = r.dr2[...] + dot_nt(r.dq[...], r.cross_q[...])
    add_grad(r.total_o, r.low[...].T, r.ctx2[...])
    turned = r.memory[...].T
    add_grad(r.total_k, turned, r.dk_low[...])
    add_grad(r.total_v, turned, r.dv_low[...])
    add_grad(r.total_q, r.a1[...].T, r.dq[...])
    add_share(r.shares, 2, column_total(r.dq[...]))
    add_share(r.shares, 3, column_total(r.dv_low[...]))
    gain = r.gain[0:1, :].astype(F32)

    def first_norm(tile):
        rows = tile_rows(tile)
        normed, inverse = norm_stats(r.r1[rows, :])
        grad, gain_part, shift_part = norm_back(normed, inverse, gain, r.work[rows, :])
        r.dr1[rows, :] = grad
        r.common[0:1, :] += column_total(grad.astype(BF16))
        r.common[3:4, :] += gain_part
        r.common[6:7, :] += shift_part

    each_tile(tiles, first_norm)
    end_totals(
        [
            (r.total_q, r.cross_q_grad),
            (r.total_k, r.cross_k_grad),
            (r.total_v, r.cross_v_grad),
            (r.total_o, r.cross_out_grad),
        ]
    )


def self_back_kernel(levels, r):
    tiles, width = r.dr1.shape[0] // TILE, r.dr1.shape[1]
    start_totals([r.total_q, r.total_k, r.total_v, r.total_o, r.shares])
    join_weights([(r.self_qkv, r.self_qkv_parts, 2), (r.self_out, r.self_out_parts, 0)])
    join_positions(r.x, r.x_parts, r.place[0])
    far, near = make_marks(r.tgt[...], levels, width // HEAD_DIM)
    r.far[...] = far
    r.near[...] = near
    r.low[...] = r.dr1[...].astype(BF16)
    r.dctx[...] = dot_nt(r.low[...], r.self_out[...]).astype(BF16)
    attend_back(
        r.q,
        r.k,
        r.v,
        r.far,
        r.near,
        r.sides,
        r.own,
        r.spread,
        r.lse,
        r.ctx,
        r.dctx,
        r.dq,
        r.dk,
        r.dv,
        r.starts,
        window_base(r, tiles, 0),
    )
    r.dk_low[...] = r.dk[...].astype(BF16)
    r.dv_low[...] = r.dv[...].astype(BF16)
    r.input_grad[...] = (
        r.dr1[...]
        + (dot_nt(r.dq[...], r.self_qkv[0]) + dot_nt(r.dk_low[...], r.self_qkv[1]))
        + dot_nt(r.dv_low[...], r.self_qkv[2])
    ).astype(BF16)
    add_grad(r.total_o, r.low[...].T, r.ctx[...])
    turned = r.x[...].T
    add_grad(r.total_q, turned, r.dq[...])
    add_grad(r.total_k, turned, r.dk_low[...])
    add_grad(r.total_v, turned, r.dv_low[...])
    add_share(r.shares, 0, column_total(r.dq[...]))
    add_share(r.shares, 1, column_total(r.dv_low[...]))
    end_totals(
        [
            (r.total_q, r.self_q_grad),
            (r.total_k, r.self_k_grad),
            (r.total_v, r.self_v_grad),
            (r.total_o, r.self_out_grad),
        ]
    )


class Refs:
    pass


def call_rows(
    kernel, name, rows, levels, scalars, held_args, row_args, fixed_args, row_outs, fixed_outs, scratch
):
    names, args, specs = [], [], []

    def put(key, array, kind):
        names.append(key)
        args.append(array)
        zeros = (0,) * (array.ndim if kind == "fixed" else array.ndim - 1)
        block = (None,) + array.shape[1:]
        if kind == "fixed":
            spec = pl.BlockSpec(array.shape, lambda row, *_: zeros, pipeline_mode=pl.Buffered(1))
        elif kind == "row":
            spec = pl.BlockSpec(block, lambda row, *_: (row,) + zeros)
        else:
            spec = pl.BlockSpec(block, lambda row, place, *_: (place[0] * rows + row,) + zeros)
        specs.append(spec)

    for group, kind in ((held_args, "held"), (row_args, "row"), (fixed_args, "fixed")):
        for key, value in group.items():
            if isinstance(value, tuple):
                for index, array in enumerate(value):
                    put((key, index), array, kind)
            else:
                put(key, value, kind)
    out_names, out_shapes, out_specs = [], [], []
    for key, (shape, kind) in row_outs.items():
        tail = (0,) * (len(shape) - 1)
        out_names.append(key)
        out_shapes.append(jax.ShapeDtypeStruct(shape, kind))
        out_specs.append(
            pl.BlockSpec((None,) + shape[1:], lambda row, *_, tail=tail: (row,) + tail)
        )
    for key, (shape, kind) in fixed_outs.items():
        zeros = (0,) * len(shape)
        out_names.append(key)
        out_shapes.append(jax.ShapeDtypeStruct(shape, kind))
        out_specs.append(pl.BlockSpec(shape, lambda row, *_, zeros=zeros: zeros))
    all_names = list(scalars) + names + out_names + list(scratch)

    def run(*refs):
        found = Refs()
        for key, ref in zip(all_names, refs):
            if isinstance(key, tuple):
                if not hasattr(found, key[0]):
                    setattr(found, key[0], [])
                getattr(found, key[0]).append(ref)
            else:
                setattr(found, key, ref)
        kernel(levels, found)

    outs = pl.pallas_call(
        run,
        grid_spec=pltpu.PrefetchScalarGridSpec(
            num_scalar_prefetch=len(scalars),
            grid=(rows,),
            in_specs=specs,
            out_specs=tuple(out_specs),
            scratch_shapes=[pltpu.VMEM(shape, kind) for shape, kind in scratch.values()],
        ),
        out_shape=tuple(out_shapes),
        compiler_params=pltpu.CompilerParams(
            dimension_semantics=("arbitrary",), vmem_limit_bytes=VMEM_BYTES
        ),
        cost_estimate=pl.CostEstimate(flops=1000, bytes_accessed=1000, transcendentals=0),
        name=name,
    )(*scalars.values(), *args)
    return dict(zip(out_names, outs))


def from_peer(values, size, step):
    return lax.ppermute(values, "head", [((i + step) % size, i) for i in range(size)])


def own_first(values, size):
    return tuple([values] + [from_peer(values, size, step) for step in range(1, size)])


def row_shares(values, rows, me, size):
    shares = []
    for step in range(1, size):
        target = (me - step) % size
        part = lax.dynamic_slice_in_dim(values, target * rows, rows, 0)
        shares.append(from_peer(part, size, step))
    return tuple(shares)


def stage_orders(dp_size):
    bits = [1 << b for b in range(dp_size.bit_length() - 1)]
    return bits, bits[:2][::-1] + bits[2:]


def closing_kernel(dp_size, head_size, count, results, levels, *refs):
    refs = list(refs)

    def take(number):
        taken = refs[:number]
        del refs[:number]
        return taken

    grads = take(count)
    rows_in = take(results)
    source_in, keys_in, feed_in = take(head_size), take(2), take(2 * head_size)
    r = Refs()
    r.out_bias, r.gain, r.shift, r.sides, tgt_ref, src_ref = take(6)
    r.ffn_bias, r.head_bias = take(head_size), take(head_size)
    r.self_qkv_parts, r.self_out_parts = take(head_size), take(head_size)
    r.cross_q_parts, r.cross_out_parts = take(head_size), take(head_size)
    common_one, common_two, share_one, share_two, share_three = take(5)
    out_ref, small_out_ref, first_ref = take(3)
    rows_out = take(results + 1)
    head_land, land, small_land, small_ref, sum_ref = take(5)
    source_ref, k2_ref, v2_ref, ffn_in_ref, ffn_out_ref, low_ref, work_ref, g_ref = take(8)
    x_ref, q_ref, k_ref, v_ref, ctx_ref, sums_ref, far_ref, near_ref = take(8)
    r.self_qkv, r.self_out, r.cross_q, r.cross_out = take(4)
    r.ffn_in = [ffn_in_ref.at[j] for j in range(head_size)]
    r.ffn_out = [ffn_out_ref.at[j] for j in range(head_size)]
    (
        local_sem,
        head_send,
        head_recv,
        fold_send,
        fold_recv,
        grow_send,
        grow_recv,
        small_send,
        small_recv,
        rows_send,
        rows_recv,
        feed_sem,
    ) = refs
    length = out_ref.shape[1]
    me, spot = lax.axis_index("head"), lax.axis_index("dp")
    held, positions = rows_out[0].shape[0] // head_size, rows_out[0].shape[1]
    mine = pl.ds(me * held, held)
    moves = [(part.at[mine], source_ref.at[j]) for j, part in enumerate(source_in)]
    moves += [(keys_in[0], k2_ref), (keys_in[1], v2_ref)]
    moves += list(zip(feed_in, r.ffn_in + r.ffn_out))
    loads = [
        pltpu.make_async_copy(source, target, feed_sem.at[i])
        for i, (source, target) in enumerate(moves)
    ]
    for copy in loads:
        copy.start()
    orders = stage_orders(dp_size)
    depth = len(orders[0])

    def digit(stride):
        return (spot // stride) % 2

    def partner(stride):
        return spot + (1 - 2 * digit(stride)) * stride

    share = out_ref.shape[2]
    for j in range(head_size):
        small_ref[j, 0:16, :] = common_one[...] + common_two[...]
        small_ref[j, 16:24, 0:share] = share_one[j] + share_two[j] + share_three[j]
        if share < small_ref.shape[2]:
            small_ref[j, 16:24, share:] = jnp.zeros((8, small_ref.shape[2] - share), F32)
    peers = [(me + step) % head_size for step in range(1, head_size)]
    barrier = pltpu.get_barrier_semaphore()
    for peer in peers:
        pl.semaphore_signal(
            barrier, inc=1, device_id={"head": peer}, device_id_type=pl.DeviceIdType.MESH
        )
    for stride in orders[0]:
        pl.semaphore_signal(
            barrier, inc=1, device_id={"dp": partner(stride)}, device_id_type=pl.DeviceIdType.MESH
        )

    def remote(source, target, send, recv, where):
        return pltpu.make_async_remote_copy(
            src_ref=source,
            dst_ref=target,
            send_sem=send,
            recv_sem=recv,
            device_id=where,
            device_id_type=pl.DeviceIdType.MESH,
        )

    queue = [i for pair in zip(range(count // 2), range(count // 2, count)) for i in pair]
    small_head = [
        remote(
            small_ref.at[j + 1],
            small_land.at[j],
            small_send.at[j],
            small_recv.at[j],
            {"head": peer},
        )
        for j, peer in enumerate(peers)
    ]
    trades = []

    def trade(source, target, j, i):
        there = pl.ds(pl.multiple_of(peers[j] * positions, positions), positions)
        copy = remote(
            source.at[:, there, :], target, rows_send.at[j, i], rows_recv.at[j, i], {"head": peers[j]}
        )
        copy.start()
        trades.append(copy)

    tiles = x_ref.shape[0] // TILE

    def row_start(row):
        if row == 0:
            join_all(attention_weights(r))
            for copy in loads[:head_size]:
                copy.wait()
        join_positions(x_ref, [source_ref.at[j, row] for j in range(head_size)], me)
        segment_row = tgt_ref[pl.ds(me * held + row, 1), :]
        self_start(r, x_ref, segment_row, near_ref, far_ref, q_ref, k_ref, v_ref, levels)

    def self_tile(tile):
        start, end = max(0, tile - 1) * TILE, min(tiles, tile + 2) * TILE
        attend(
            q_ref, k_ref, v_ref, far_ref, near_ref, r.sides, ctx_ref, None, tile, start, end - start
        )

    def row_middle(row):
        self_end(r, x_ref, ctx_ref, None, low_ref, work_ref)
        segment_row = src_ref[pl.ds(me * held + row, 1), :]
        cross_start(r, segment_row, near_ref, low_ref, q_ref, levels)
        if row == 0:
            for copy in loads[head_size : head_size + 2]:
                copy.wait()

    def cross_tile(row, tile):
        keys, values = k2_ref.at[row], v2_ref.at[row]
        attend(
            q_ref, keys, values, far_ref, near_ref, r.sides, ctx_ref, None, tile, 0, x_ref.shape[0]
        )

    def feed_start(row):
        cross_end(r, ctx_ref, sums_ref, work_ref)
        feed_norm(r, sums_ref, low_ref, work_ref)
        if row == 0:
            for copy in loads[head_size + 2 :]:
                copy.wait()

    def feed_middle(j):
        feed_units(r, j, low_ref, g_ref, None)

    def feed_end(row):
        feed_out(r, work_ref, g_ref)
        gain, shift = r.gain[2:3, :].astype(F32), r.shift[2:3, :].astype(F32)
        for tile in range(work_ref.shape[0] // TILE):
            rows = tile_rows(tile)
            normed = norm_stats(work_ref[rows, :])[0]
            first_ref[row, rows, :] = (normed * gain + shift).astype(BF16)
        for j in range(len(peers)):
            trade(
                first_ref.at[pl.ds(row, 1)],
                rows_out[0].at[pl.ds(me * held + row, 1)],
                j,
                results + row,
            )

    pieces = []
    for row in range(held):
        pieces.append(functools.partial(row_start, row))
        pieces += [functools.partial(self_tile, tile) for tile in range(tiles)]
        pieces.append(functools.partial(row_middle, row))
        pieces += [functools.partial(cross_tile, row, tile) for tile in range(tiles)]
        pieces.append(functools.partial(feed_start, row))
        pieces += [functools.partial(feed_middle, j) for j in range(head_size)]
        pieces.append(functools.partial(feed_end, row))
    early = min(EARLY, len(pieces))
    for piece in pieces[:early]:
        piece()
    pieces = pieces[early:]
    pl.semaphore_wait(barrier, len(peers) + depth)
    for copy in small_head:
        copy.start()
    locals_, heads_ = {}, {}
    for i in queue:
        locals_[i] = pltpu.make_async_copy(grads[i].at[0], sum_ref.at[i], local_sem.at[i])
        locals_[i].start()
        heads_[i] = [
            remote(
                grads[i].at[j + 1],
                head_land.at[j, i],
                head_send.at[j, i],
                head_recv.at[j, i],
                {"head": peer},
            )
            for j, peer in enumerate(peers)
        ]
        for copy in heads_[i]:
            copy.start()

    for i in range(results):
        for j in range(len(peers)):
            trade(rows_in[i], rows_out[i + 1].at[mine], j, i)

    def places(i):
        order = orders[0] if i < count // 2 else orders[1]
        offset, size, result = 0, length, []
        for stride in order:
            size //= 2
            keep = offset + digit(stride) * size
            give = offset + (1 - digit(stride)) * size
            result.append((stride, size, pl.multiple_of(keep, 16), pl.multiple_of(give, 16)))
            offset = keep
        return result

    plan = {i: places(i) for i in range(count)}
    moving = {}

    def fold(i, stage):
        stride, size, keep, give = plan[i][stage]
        base = length - (length >> stage)
        copy = remote(
            sum_ref.at[i, pl.ds(give, size), :],
            land.at[i, pl.ds(base, size), :],
            fold_send.at[stage, i],
            fold_recv.at[stage, i],
            {"dp": partner(stride)},
        )
        copy.start()
        moving[i] = copy

    def grow(i, stage):
        stride, size, keep, give = plan[i][stage]
        rows = out_ref.at[i, pl.ds(keep, size), :]
        copy = remote(
            rows, rows, grow_send.at[stage, i], grow_recv.at[stage, i], {"dp": partner(stride)}
        )
        copy.start()
        moving[i] = copy

    def task(i, number):
        if number == 0:
            locals_[i].wait()
            total = sum_ref[i].astype(F32)
            for j, copy in enumerate(heads_[i]):
                copy.wait()
                total = total + head_land[j, i].astype(F32)
            sum_ref[i] = total.astype(BF16)
            fold(i, 0)
        elif number <= depth:
            moving[i].wait()
            stage = number - 1
            stride, size, keep, give = plan[i][stage]
            base = length - (length >> stage)
            rows = pl.ds(keep, size)
            total = (
                sum_ref[i, rows, :].astype(F32) + land[i, pl.ds(base, size), :].astype(F32)
            ).astype(BF16)
            if number < depth:
                sum_ref[i, rows, :] = total
                fold(i, number)
            else:
                out_ref[i, rows, :] = total
                grow(i, depth - 1)
        else:
            moving[i].wait()
            stage = 2 * depth - number
            if stage > 0:
                grow(i, stage - 1)

    steps = 2 * depth + 1
    small_moving = []

    def small_task(number):
        if number == 0:
            total = small_ref[0]
            for j, copy in enumerate(small_head):
                copy.wait()
                total = total + small_land[j]
            small_out_ref[...] = total
        else:
            small_moving.pop().wait()
            small_out_ref[...] += small_land[len(peers) + number - 1]
        if number < depth:
            slot = len(peers) + number
            copy = remote(
                small_out_ref,
                small_land.at[slot],
                small_send.at[slot],
                small_recv.at[slot],
                {"dp": partner(orders[0][number])},
            )
            copy.start()
            small_moving.append(copy)

    times = steps + count // 2 - 1
    for time in range(times):
        if time <= depth:
            small_task(time)
        for place, i in enumerate(queue):
            if 0 <= time - place // 2 < steps:
                task(i, time - place // 2)
        first, last = (min(n, times - 1) * len(pieces) // (times - 1) for n in (time, time + 1))
        for piece in pieces[first:last]:
            piece()
    for copy in trades:
        copy.wait()


def close(grads, common, shares, arrays, source, keys, segments, weights, levels, dp_size, head_size):
    count, results = len(grads), len(arrays)
    rows, positions, width = arrays[0].shape
    traded = jax.ShapeDtypeStruct((rows * head_size, positions // head_size, width), BF16)
    length, share = grads[0].shape[1:]
    depth = dp_size.bit_length() - 1
    peers = head_size - 1
    small = (24, common[0].shape[1])
    any_spec = pl.BlockSpec(memory_space=pl.ANY)
    vmem = pl.BlockSpec(memory_space=pltpu.VMEM)
    dma = pltpu.SemaphoreType.DMA
    return pl.pallas_call(
        functools.partial(closing_kernel, dp_size, head_size, count, results, levels),
        out_shape=(
            jax.ShapeDtypeStruct((count, length, share), BF16),
            jax.ShapeDtypeStruct(small, F32),
            jax.ShapeDtypeStruct(arrays[0].shape, BF16),
        )
        + (traded,) * (results + 1),
        in_specs=[any_spec] * (count + results + 3 * head_size + 2) + [vmem] * (11 + 6 * head_size),
        out_specs=(vmem, vmem, vmem) + (any_spec,) * (results + 1),
        scratch_shapes=[
            pltpu.VMEM((peers, count, length, share), BF16),
            pltpu.VMEM((count, length, share), BF16),
            pltpu.VMEM((peers + depth,) + small, F32),
            pltpu.VMEM((head_size,) + small, F32),
            pltpu.VMEM((count, length, share), BF16),
            pltpu.VMEM((head_size, rows, positions // head_size, width), BF16),
            pltpu.VMEM((rows, positions, width), BF16),
            pltpu.VMEM((rows, positions, width), BF16),
            pltpu.VMEM((head_size,) + weights["ffn_in"][0].shape, BF16),
            pltpu.VMEM((head_size,) + weights["ffn_out"][0].shape, BF16),
            pltpu.VMEM((positions, width), BF16),
            pltpu.VMEM((positions, width), F32),
            pltpu.VMEM((positions, head_size * weights["ffn_in"][0].shape[1]), BF16),
        ]
        + [pltpu.VMEM((positions, width), BF16)] * 5
        + [
            pltpu.VMEM((positions, width), F32),
            pltpu.VMEM((positions, PAIR), BF16),
            pltpu.VMEM((positions, PAIR), BF16),
            pltpu.VMEM((3, width, width), BF16),
            pltpu.VMEM((width, width), BF16),
            pltpu.VMEM((width, width), BF16),
            pltpu.VMEM((width, width), BF16),
            dma((count,)),
            dma((peers, count)),
            dma((peers, count)),
            dma((depth, count)),
            dma((depth, count)),
            dma((depth, count)),
            dma((depth, count)),
            dma((peers + depth,)),
            dma((peers + depth,)),
            dma((peers, results + rows)),
            dma((peers, results + rows)),
            dma((2 + 3 * head_size,)),
        ],
        compiler_params=pltpu.CompilerParams(
            collective_id=0, has_side_effects=True, vmem_limit_bytes=VMEM_BYTES
        ),
        name="closing",
    )(
        *grads,
        *arrays,
        *source,
        *keys,
        *weights["ffn_in"],
        *weights["ffn_out"],
        weights["out_bias"],
        weights["gain"],
        weights["shift"],
        constants(width, levels)["sides"],
        *segments,
        *weights["ffn_bias"],
        *weights["head_bias"],
        *weights["self_qkv"],
        *weights["self_out"],
        *weights["cross_q"],
        *weights["cross_out"],
        *common,
        *shares,
    )


def finish_kernel(results, *refs):
    place_ref, refs = refs[0], list(refs[1:])

    def take(number):
        taken = refs[:number]
        del refs[:number]
        return taken

    own, arrived = take(results), take(results)
    summed_ref, feed_in_ref, feed_out_ref = take(3)
    rows_out = take(results)
    qkv_ref, kv_ref, self_out_ref, cross_q_ref, cross_out_ref, ffn_in_ref, ffn_out_ref = take(7)
    step = pl.program_id(0)
    rows = pl.num_programs(0) // place_ref[1]
    mine = step // rows == place_ref[0]
    for i in range(results):
        rows_out[i][...] = jnp.where(mine, own[i][...], arrived[i][...])
    ffn_in_ref[...] = feed_in_ref[...].astype(F32)
    ffn_out_ref[...] = feed_out_ref[...].astype(F32).T

    def at(number, target_ref, turned):
        @pl.when(step == number)
        def write():
            values = summed_ref[...].astype(F32)
            target_ref[...] = values.T if turned else values

    for number, (target_ref, turned) in enumerate(
        [(cross_q_ref, False), (kv_ref, False), (kv_ref, False), (cross_out_ref, True)]
        + [(qkv_ref, False)] * 3
        + [(self_out_ref, True)]
    ):
        at(number, target_ref, turned)


def finish(place, arrays, arrived, summed, feed_grads, head_size):
    results = len(arrays)
    rows, length, width = arrays[0].shape
    held, positions = rows * head_size, length // head_size
    share, units = summed.shape[2], feed_grads.shape[2]
    steps = summed.shape[0]
    if held != steps:
        raise ValueError(held)
    pieces = max(1, min(steps, units // 128))
    tall, wide = width // steps, units // pieces

    def clip(step, low, high):
        return jnp.clip(step - low, 0, high)

    def own_row(step, place):
        return (jnp.clip(step - place[0] * rows, 0, rows - 1), place[0], 0)

    def arrived_row(step, place):
        other = ((place[0] + 1) % place[1]) * rows
        return (jnp.where(step // rows == place[0], other, step), 0, 0)

    block = (None, positions, width)
    return pl.pallas_call(
        functools.partial(finish_kernel, results),
        grid_spec=pltpu.PrefetchScalarGridSpec(
            num_scalar_prefetch=1,
            grid=(steps,),
            in_specs=[pl.BlockSpec(block, own_row)] * results
            + [pl.BlockSpec(block, arrived_row)] * results
            + [
                pl.BlockSpec((None, width, share), lambda step, _: (step, 0, 0)),
                pl.BlockSpec((None, tall, units), lambda step, _: (0, step, 0)),
                pl.BlockSpec(
                    (None, width, wide), lambda step, _: (1, 0, clip(step, 0, pieces - 1))
                ),
            ],
            out_specs=(pl.BlockSpec(block, lambda step, _: (step, 0, 0)),) * results
            + (
                pl.BlockSpec((None, width, share), lambda step, _: (clip(step, 4, 2), 0, 0)),
                pl.BlockSpec((None, width, share), lambda step, _: (clip(step, 1, 1), 0, 0)),
                pl.BlockSpec((share, width), lambda step, _: (0, 0)),
                pl.BlockSpec((width, share), lambda step, _: (0, 0)),
                pl.BlockSpec((share, width), lambda step, _: (0, 0)),
                pl.BlockSpec((tall, units), lambda step, _: (step, 0)),
                pl.BlockSpec((wide, width), lambda step, _: (clip(step, 0, pieces - 1), 0)),
            ),
        ),
        out_shape=(jax.ShapeDtypeStruct((held, positions, width), BF16),) * results
        + tuple(
            jax.ShapeDtypeStruct(shape, F32)
            for shape in (
                (3, width, share),
                (2, width, share),
                (share, width),
                (width, share),
                (share, width),
                (width, units),
                (units, width),
            )
        ),
        compiler_params=pltpu.CompilerParams(
            dimension_semantics=("arbitrary",), vmem_limit_bytes=VMEM_BYTES
        ),
        name="finish",
    )(place, *arrays, *arrived, summed, feed_grads, feed_grads)


def window_starts(query_segments, key_segments, window):
    rows, length = query_segments.shape
    tiles = query_segments.reshape(rows, length // TILE, TILE)
    first, last = tiles[:, :, 0], tiles[:, :, -1]
    before = jnp.sum(key_segments[:, None, :] < first[:, :, None], axis=2).astype(jnp.int32)
    after = jnp.sum(key_segments[:, None, :] <= last[:, :, None], axis=2).astype(jnp.int32)
    start = jnp.minimum((before // 16) * 16, key_segments.shape[1] - window)
    return jnp.where(after - start <= window, start, -1).reshape(-1)


def constants(width, levels):
    heads = width // HEAD_DIM
    lane = np.arange(PAIR)
    sides = np.stack([lane < HEAD_DIM, lane >= HEAD_DIM])
    kept = (lane >= 16) & (lane < 16 + 3 * heads)
    own = np.stack([(lane < levels) | (kept & ((lane - 16) % heads == h)) for h in range(heads)])
    spread = kept[None, :] & (
        (lane[None, :] - 16) % heads == np.arange(width)[:, None] // HEAD_DIM
    )

    def tall(rows):
        return jnp.asarray(np.broadcast_to(rows[:, None, :], (rows.shape[0], TILE, PAIR)), BF16)

    return {"sides": tall(sides), "own": tall(own), "spread": jnp.asarray(spread, BF16)}


def local_layer(
    place,
    rows,
    mixed,
    memory,
    cotangent,
    tgt_segments,
    src_segments,
    levels,
    weights,
    feed_total=lambda own, sent: own,
):
    head_size = len(weights["ffn_in"])
    held, length = tgt_segments.shape
    width = mixed[0].shape[2]
    hidden = weights["ffn_in"][0].shape[1] * head_size
    heads = width // HEAD_DIM
    tiles = length // TILE
    window = min(WINDOW, length)
    share = width // head_size
    marks = constants(width, levels)
    sides = {"sides": marks["sides"]}
    alone = {"place": place}
    starts = alone | {
        "starts": jnp.concatenate(
            [
                window_starts(tgt_segments, tgt_segments, window),
                window_starts(tgt_segments, src_segments, window),
            ]
        )
    }
    tgt = {"tgt": tgt_segments[:, None, :]}
    src = {"src": src_segments[:, None, :]}

    def pick(*keys):
        return {key: weights[key] for key in keys}

    def parts_of(*keys):
        return {key + "_parts": weights[key] for key in keys}

    wide_low = ((rows, length, width), BF16)
    wide = ((rows, length, width), F32)
    stats = ((rows, tiles, heads, TILE), F32)
    one_low, one = ((length, width), BF16), ((length, width), F32)
    mark = ((length, PAIR), BF16)
    square, square_low = ((width, width), F32), ((width, width), BF16)
    split = ((head_size, width, share), BF16)
    common, shares = ((16, width), F32), ((head_size, 8, share), F32)
    norms = pick("out_bias", "gain", "shift")
    feed = pick("ffn_in", "ffn_out", "ffn_bias")
    self_qkv = {"self_qkv": ((3, width, width), BF16)}
    cross_kv = {"cross_kv": ((2, width, width), BF16)}
    marks_scratch = {"far": mark, "near": mark}
    half = ((2, width, hidden // head_size), BF16)
    kept = call_rows(
        attention_kernel,
        "attention",
        rows,
        levels,
        starts,
        {"x_parts": mixed[:1], "memory_parts": memory[:1]} | tgt | src,
        {("x_parts", j): part for j, part in enumerate(mixed[1:])}
        | {("memory_parts", j): part for j, part in enumerate(memory[1:])},
        sides
        | parts_of("self_qkv", "self_out", "cross_q", "cross_kv", "cross_out")
        | pick("head_bias")
        | norms,
        {key: wide_low for key in ("q", "k", "v", "ctx", "a1", "q2", "k2", "v2", "ctx2")}
        | {"lse": stats, "lse2": stats, "r1": wide, "r2": wide},
        {},
        {"work": one, "x": one_low, "memory": one_low}
        | {key: square_low for key in ("self_out", "cross_q", "cross_out")}
        | self_qkv
        | cross_kv
        | marks_scratch,
    )
    fed = call_rows(
        feed_kernel,
        "feed",
        rows,
        levels,
        alone,
        {"cot_parts": cotangent},
        {"r2": kept["r2"]},
        feed | norms,
        {"second": wide_low, "dr2": wide},
        {"own_grads": half, "common": common, "shares": shares}
        | {("sent_grads", j): half for j in range(1, head_size)},
        {
            "cot": one_low,
            "a2": one_low,
            "df": one_low,
            "work": one,
            "g": ((length, hidden), BF16),
            "du": ((length, hidden), BF16),
            "slope": ((length, hidden), BF16),
            "in_total": ((width, hidden), F32),
            "out_total": ((width, hidden), F32),
        },
    )
    sent = [fed[("sent_grads", j)] for j in range(1, head_size)]
    dr2, feed_grads = feed_total(fed["dr2"], fed["own_grads"], sent)
    totals = {"total_" + key: square for key in "qkvo"}
    back_scratch = (
        totals
        | marks_scratch
        | {key: one_low for key in ("dctx", "low", "dq", "dk_low", "dv_low")}
        | {"dk": one, "dv": one}
    )
    crossed = call_rows(
        cross_back_kernel,
        "cross_back",
        rows,
        levels,
        starts,
        {"memory_parts": memory[:1]} | tgt | src,
        {key: kept[key] for key in ("q2", "k2", "v2", "ctx2", "lse2", "r1", "a1")}
        | {"dr2": dr2}
        | {("memory_parts", j): part for j, part in enumerate(memory[1:])},
        marks | parts_of("cross_q", "cross_kv", "cross_out") | pick("gain"),
        {"memory_grad": wide_low, "dr1": wide},
        {key: split for key in ("cross_q_grad", "cross_k_grad", "cross_v_grad", "cross_out_grad")}
        | {"common": common, "shares": shares},
        back_scratch
        | cross_kv
        | {"work": one, "memory": one_low, "cross_q": square_low, "cross_out": square_low},
    )
    selfed = call_rows(
        self_back_kernel,
        "self_back",
        rows,
        levels,
        starts,
        {"x_parts": mixed[:1]} | tgt,
        {key: kept[key] for key in ("q", "k", "v", "ctx", "lse")}
        | {"dr1": crossed["dr1"]}
        | {("x_parts", j): part for j, part in enumerate(mixed[1:])},
        marks | parts_of("self_qkv", "self_out"),
        {"input_grad": wide_low},
        {key: split for key in ("self_q_grad", "self_k_grad", "self_v_grad", "self_out_grad")}
        | {"shares": shares},
        back_scratch | self_qkv | {"x": one_low, "self_out": square_low},
    )
    grads = tuple(
        crossed[key] for key in ("cross_q_grad", "cross_k_grad", "cross_v_grad", "cross_out_grad")
    ) + tuple(selfed[key] for key in ("self_q_grad", "self_k_grad", "self_v_grad", "self_out_grad"))
    return (
        (kept["k2"], kept["v2"]),
        (fed["second"], selfed["input_grad"], crossed["memory_grad"]),
        feed_grads,
        grads,
        (fed["common"], crossed["common"]),
        (fed["shares"], crossed["shares"], selfed["shares"]),
    )


def body(
    dp_size,
    head_size,
    source_copy,
    target_embed,
    memory,
    tgt_segments,
    src_segments,
    hamming,
    priority,
    cotangent,
    self_qkv,
    self_out,
    cross_q,
    cross_kv,
    cross_out,
    ffn_in,
    ffn_out,
    head_bias,
    ffn_bias,
    out_bias,
    norm_gain,
    norm_shift,
):
    me = lax.axis_index("head")
    levels = hamming.shape[1]
    held, share, width = source_copy.shape
    rows = held // head_size

    def own_positions(array):
        return lax.dynamic_slice_in_dim(array, me * share, share, 1)

    level = jnp.arange(levels, dtype=jnp.int32)
    chosen = own_positions(tgt_segments)[:, :, None] == level[None, None, :]
    limits = jnp.sum(jnp.where(chosen, hamming[:, None, :], 0), axis=2)
    glanced = own_positions(priority) < limits
    mixed = jnp.where(glanced[:, :, None], target_embed, source_copy)
    weights = {
        "self_qkv": own_first(self_qkv, head_size),
        "self_out": own_first(self_out, head_size),
        "cross_q": own_first(cross_q, head_size),
        "cross_kv": own_first(cross_kv, head_size),
        "cross_out": own_first(cross_out, head_size),
        "head_bias": own_first(head_bias, head_size),
        "out_bias": out_bias,
        "gain": norm_gain,
        "shift": norm_shift,
    }
    memory_shares = row_shares(memory, rows, me, head_size)
    mixed_shares = row_shares(mixed, rows, me, head_size)
    ffn_bias, ffn_in, ffn_out, cotangent, source_copy, mixed_shares = lax.optimization_barrier(
        (ffn_bias, ffn_in, ffn_out, cotangent, source_copy, mixed_shares)
    )
    weights["ffn_bias"] = own_first(ffn_bias[None, :], head_size)
    weights["ffn_in"] = own_first(ffn_in, head_size)
    weights["ffn_out"] = own_first(ffn_out, head_size)

    def feed_total(later, own, sent):
        arrived = [
            lax.ppermute(part, "head", [(i, (i + j + 1) % head_size) for i in range(head_size)])
            for j, part in enumerate(sent)
        ]
        total = own.astype(F32)
        for part in arrived:
            total = total + part.astype(F32)
        later, total = lax.optimization_barrier((later, total.astype(BF16)))
        return later, lax.psum(total, "dp")

    keys, arrays, feed_grads, grads, common, shares = local_layer(
        me.astype(jnp.int32).reshape(1),
        rows,
        (mixed,) + mixed_shares,
        (memory,) + memory_shares,
        own_first(cotangent, head_size),
        tgt_segments,
        src_segments,
        levels,
        weights,
        feed_total,
    )
    summed, sums, first, *arrived = close(
        grads,
        common,
        shares,
        arrays,
        own_first(source_copy, head_size),
        keys,
        (tgt_segments, src_segments),
        weights,
        levels,
        dp_size,
        head_size,
    )
    place = jnp.stack([me.astype(jnp.int32), jnp.int32(head_size)])
    *outs, qkv, kv, self_out, cross_q, cross_out, ffn_in, ffn_out = finish(
        place, (first, *arrays), arrived, summed, feed_grads, head_size
    )
    part = width // head_size

    return (
        *outs,
        qkv,
        self_out,
        cross_q,
        kv,
        cross_out,
        ffn_in,
        ffn_out,
        sums[16:20, :part],
        sums[20:24, :part].reshape(-1),
        sums[0:3],
        sums[3:6],
        sums[6:9],
    )


def solution(mesh):
    split = P("dp", "head", None)
    rows = P("dp", None)
    last, last_two, first = P(None, "head"), P(None, None, "head"), P("head", None)
    return jax.shard_map(
        functools.partial(body, mesh.shape["dp"], mesh.shape["head"]),
        mesh=mesh,
        in_specs=(split, split, split, rows, rows, rows, rows, split)
        + (last_two, first, last, last_two, first, last, first, last, P("head"), P(), P(), P()),
        out_specs=(split, split, split, split)
        + (last_two, first, last, last_two, first, last, first, last, P("head"), P(), P(), P()),
        check_vma=False,
    )
```

```python
import functools

import jax
import jax.numpy as jnp
import numpy as np
from jax import lax
from jax.experimental import pallas as pl
from jax.experimental.pallas import tpu as pltpu
from jax.sharding import PartitionSpec as P

HEAD_DIM = 64
PAIR = 2 * HEAD_DIM
TILE = 128
WINDOW = 256
EARLY = 2
FAR = -1e30
AXIS = "head"
F32 = jnp.float32
BF16 = jnp.bfloat16
VMEM_BYTES = 60 * 1024 * 1024


def dot_nn(left, right):
    return lax.dot_general(left, right, (((1,), (0,)), ((), ())), preferred_element_type=F32)


def dot_nt(left, right):
    return lax.dot_general(left, right, (((1,), (1,)), ((), ())), preferred_element_type=F32)


def norm_stats(sums):
    row_mean = jnp.mean(sums, axis=-1, keepdims=True)
    centred = sums - row_mean
    spread = jnp.mean(centred * centred, axis=-1, keepdims=True)
    inverse = lax.rsqrt(spread + 1e-05)
    return centred * inverse, inverse


def norm_back(normed, inverse, gain_row, incoming):
    scaled = incoming * gain_row
    mean_one = jnp.mean(scaled, axis=-1, keepdims=True)
    mean_two = jnp.mean(scaled * normed, axis=-1, keepdims=True)
    grad = (scaled - mean_one - normed * mean_two) * inverse
    gain_part = jnp.sum(incoming * normed, axis=0, keepdims=True)
    shift_part = jnp.sum(incoming, axis=0, keepdims=True)
    return grad, gain_part, shift_part


def gelu_parts(pre):
    ratio = pltpu.reciprocal(1.0 + 0.23164189015488 * jnp.abs(pre), approx=True)
    series = ratio * (
        0.127414796
        + ratio
        * (-0.142248368 + ratio * (0.7107068705 + ratio * (-0.7265760135 + ratio * 0.5307027145)))
    )
    bell = jnp.exp(-0.5 * (pre * pre))
    tail = series * bell
    return jnp.where(pre >= 0, 1.0 - tail, tail), bell


def each_tile(count, step):
    for index in range(count):
        step(index)


def tile_rows(tile):
    start = tile * TILE
    return pl.ds(start if isinstance(start, int) else pl.multiple_of(start, TILE), TILE)


def window_loop(starts_ref, base, tiles, length, step):
    starts = [starts_ref[base + tile] for tile in range(tiles)]
    least = functools.reduce(jnp.minimum, starts)
    window = min(WINDOW, length)

    @pl.when(least >= 0)
    def straight():
        for tile in range(tiles):
            step(tile, pl.multiple_of(starts[tile], 16), window)

    if length > WINDOW:

        @pl.when(least < 0)
        def mixed():
            def one(tile, carry):
                start = starts_ref[base + tile]

                @pl.when(start >= 0)
                def near():
                    step(tile, pl.multiple_of(start, 16), window)

                @pl.when(start < 0)
                def whole():
                    step(tile, 0, length)

                return carry

            lax.fori_loop(0, tiles, one, 0)


def make_marks(segment_row, levels, heads):
    shape = (PAIR, segment_row.shape[1])
    level = lax.broadcasted_iota(jnp.int32, shape, 0)
    same = level == segment_row
    near = jnp.where(same | ((level >= 16) & (level < 16 + 3 * heads)), 1.0, 0.0)
    far = jnp.where(same | (level >= levels), 0.0, FAR)
    return far.T.astype(BF16), near.T.astype(BF16)


def attend(q_ref, k_ref, v_ref, far_ref, near_ref, sides_ref, ctx_ref, lse_ref, tile, start, window):
    pairs = range(q_ref.shape[1] // PAIR)
    lanes = [slice(p * PAIR, (p + 1) * PAIR) for p in pairs]
    rows = tile_rows(tile)
    keys = pl.ds(start, window)
    left, right = sides_ref[0], sides_ref[1]
    query_marks = far_ref[rows, :]
    key_marks = near_ref[keys, :]
    stacked = []
    for p in pairs:
        queries = q_ref[rows, lanes[p]]
        stacked.append(
            jnp.concatenate(
                [
                    jnp.concatenate([queries * left, query_marks], axis=1),
                    jnp.concatenate([queries * right, query_marks], axis=1),
                ],
                axis=0,
            )
        )
    scores = [
        dot_nt(jnp.concatenate([k_ref[keys, lanes[p]], key_marks], axis=1), stacked[p])
        for p in pairs
    ]
    peaks = [jnp.max(s, axis=0, keepdims=True) for s in scores]
    weights = [jnp.exp(s - m) for s, m in zip(scores, peaks)]
    totals = [jnp.sum(w, axis=0, keepdims=True) for w in weights]
    low = [w.astype(BF16) for w in weights]
    turned = [v_ref[keys, lanes[p]].T for p in pairs]
    mixed = [dot_nn(turned[p], low[p]) for p in pairs]
    shares = [pltpu.reciprocal(t, approx=True) for t in totals]
    context = [
        jnp.concatenate(
            [
                mixed[p][:HEAD_DIM, :TILE] * shares[p][:, :TILE],
                mixed[p][HEAD_DIM:, TILE:] * shares[p][:, TILE:],
            ],
            axis=0,
        )
        for p in pairs
    ]
    for p in pairs:
        ctx_ref[rows, lanes[p]] = context[p].T.astype(BF16)
    if lse_ref is not None:
        for p in pairs:
            log_total = peaks[p] + jnp.log(totals[p])
            lse_ref[tile, pl.ds(2 * p, 1), :] = log_total[:, :TILE]
            lse_ref[tile, pl.ds(2 * p + 1, 1), :] = log_total[:, TILE:]


def three_parts(values):
    high = values.astype(BF16).astype(F32)
    rest = values - high
    middle = rest.astype(BF16).astype(F32)
    return high, middle, rest - middle


def attend_back(
    q_ref,
    k_ref,
    v_ref,
    far_ref,
    near_ref,
    sides_ref,
    own_ref,
    spread_ref,
    lse_ref,
    ctx_ref,
    dctx_ref,
    dq_ref,
    dk_ref,
    dv_ref,
    starts_ref,
    base,
):
    length, width = q_ref.shape
    pairs = range(width // PAIR)
    heads = width // HEAD_DIM
    lanes = [slice(p * PAIR, (p + 1) * PAIR) for p in pairs]
    dk_ref[...] = jnp.zeros_like(dk_ref)
    dv_ref[...] = jnp.zeros_like(dv_ref)

    def step(tile, start, window):
        rows = tile_rows(tile)
        keys = pl.ds(start, window)
        left, right = sides_ref[0], sides_ref[1]
        key_marks = near_ref[keys, :]
        high, middle, rest = three_parts(-lse_ref[tile])
        stats = jnp.concatenate(
            [
                jnp.zeros((16, TILE), F32),
                high,
                middle,
                rest,
                jnp.zeros((TILE - 16 - 3 * heads, TILE), F32),
            ],
            axis=0,
        )
        query_marks = far_ref[rows, :] + stats.T.astype(BF16)
        product = dctx_ref[rows, :].astype(F32) * ctx_ref[rows, :].astype(F32)
        product_high = product.astype(BF16)
        product_rest = (product - product_high.astype(F32)).astype(BF16)
        delta = -(dot_nn(product_high, spread_ref[...]) + dot_nn(product_rest, spread_ref[...]))
        high, middle, rest = three_parts(delta)
        lane = lax.broadcasted_iota(jnp.int32, delta.shape, 1)
        grad_marks = jnp.where(
            lane < 16 + heads, high, jnp.where(lane < 16 + 2 * heads, middle, rest)
        ).astype(BF16)
        query_stack, grad_stack, query_side, grad_side, key_rows = [], [], [], [], []
        for p in pairs:
            queries = q_ref[rows, lanes[p]]
            grads = dctx_ref[rows, lanes[p]]
            key_rows.append(k_ref[keys, lanes[p]])
            query_stack.append(jnp.concatenate([queries * left, queries * right], axis=0))
            grad_stack.append(jnp.concatenate([grads * left, grads * right], axis=0))
            one, two = own_ref[2 * p], own_ref[2 * p + 1]
            marks = jnp.concatenate([query_marks * one, query_marks * two], axis=0)
            query_side.append(jnp.concatenate([query_stack[p], marks], axis=1))
            marks = jnp.concatenate([grad_marks * one, grad_marks * two], axis=0)
            grad_side.append(jnp.concatenate([grad_stack[p], marks], axis=1))
        scores = [
            dot_nt(jnp.concatenate([key_rows[p], key_marks], axis=1), query_side[p]) for p in pairs
        ]
        probs_grad = [
            dot_nt(jnp.concatenate([v_ref[keys, lanes[p]], key_marks], axis=1), grad_side[p])
            for p in pairs
        ]
        probs = [jnp.exp(s) for s in scores]
        probs_low = [w.astype(BF16) for w in probs]
        scores_grad = [(probs[p] * probs_grad[p]).astype(BF16) for p in pairs]
        turned_keys = [key_rows[p].T for p in pairs]
        for p in pairs:
            dv_ref[keys, lanes[p]] += dot_nn(probs_low[p], grad_stack[p])
        for p in pairs:
            dk_ref[keys, lanes[p]] += dot_nn(scores_grad[p], query_stack[p])
        turned = [dot_nn(turned_keys[p], scores_grad[p]) for p in pairs]
        for p in pairs:
            both = jnp.concatenate(
                [turned[p][:HEAD_DIM, :TILE], turned[p][HEAD_DIM:, TILE:]], axis=0
            )
            dq_ref[rows, lanes[p]] = (both.T * (HEAD_DIM**-0.5)).astype(BF16)

    window_loop(starts_ref, base, length // TILE, length, step)


def glance_columns(segment_row, priority_row, counts):
    limits = jnp.zeros(segment_row.shape, jnp.int32)
    for level, count in enumerate(counts):
        limits = jnp.where(segment_row == level, count, limits)
    chosen = jnp.where(priority_row < limits, 1.0, 0.0)
    return jnp.broadcast_to(chosen, (PAIR, segment_row.shape[1])).T


def held_row(r):
    return r.place[0] * pl.num_programs(0) + pl.program_id(0)


def row_of(r, rows_ref):
    return rows_ref[pl.ds(held_row(r), 1), :]


def join_positions(target_ref, parts, place):
    share = parts[0].shape[0]
    for j, part in enumerate(parts):
        start = ((place + j) % len(parts)) * share
        target_ref[pl.ds(pl.multiple_of(start, share), share), :] = part[...]


def join_all(pairs):
    for target_ref, parts, axis in pairs:
        share = parts[0].shape[axis]
        for j, part in enumerate(parts):
            where = [slice(None)] * len(target_ref.shape)
            where[axis] = slice(j * share, (j + 1) * share)
            target_ref[tuple(where)] = part[...]


def join_weights(pairs):
    @pl.when(pl.program_id(0) == 0)
    def join():
        join_all(pairs)


def joined(parts):
    return jnp.concatenate([part[...].astype(F32) for part in parts], axis=1)


def window_base(r, tiles, cross):
    held = r.starts.shape[0] // (2 * tiles)
    return (held_row(r) + held * cross) * tiles


def self_start(r, x_ref, segment_row, near_ref, far_ref, q_ref, k_ref, v_ref, levels):
    far, near = make_marks(segment_row, levels, x_ref.shape[1] // HEAD_DIM)
    far_ref[...] = far
    near_ref[...] = near
    bias = joined(r.head_bias)
    inputs = x_ref[...]
    queries = (dot_nn(inputs, r.self_qkv[0]) + bias[0:1, :]).astype(BF16)
    q_ref[...] = queries * jnp.asarray(HEAD_DIM**-0.5, BF16)
    k_ref[...] = dot_nn(inputs, r.self_qkv[1]).astype(BF16)
    v_ref[...] = (dot_nn(inputs, r.self_qkv[2]) + bias[1:2, :]).astype(BF16)


def self_end(r, x_ref, ctx_ref, r1_ref, a1_ref, work_ref):
    work_ref[...] = dot_nn(ctx_ref[...], r.self_out[...])
    out_bias = r.out_bias[0:1, :].astype(F32)
    gain, shift = r.gain[0:1, :].astype(F32), r.shift[0:1, :].astype(F32)

    def step(tile):
        rows = tile_rows(tile)
        sums = x_ref[rows, :].astype(F32) + (work_ref[rows, :] + out_bias)
        if r1_ref is not None:
            r1_ref[rows, :] = sums
        normed = norm_stats(sums)[0] * gain + shift
        work_ref[rows, :] = normed
        a1_ref[rows, :] = normed.astype(BF16)

    each_tile(x_ref.shape[0] // TILE, step)


def cross_start(r, segment_row, near_ref, a1_ref, q2_ref, levels):
    near_ref[...] = make_marks(segment_row, levels, q2_ref.shape[1] // HEAD_DIM)[1]
    bias = joined(r.head_bias)
    queries = (dot_nn(a1_ref[...], r.cross_q[...]) + bias[2:3, :]).astype(BF16)
    q2_ref[...] = queries * jnp.asarray(HEAD_DIM**-0.5, BF16)


def cross_end(r, ctx2_ref, r2_ref, work_ref):
    r2_ref[...] = work_ref[...] + (
        dot_nn(ctx2_ref[...], r.cross_out[...]) + r.out_bias[1:2, :].astype(F32)
    )


def attention_weights(r):
    return [
        (r.self_qkv, r.self_qkv_parts, 2),
        (r.self_out, r.self_out_parts, 0),
        (r.cross_q, r.cross_q_parts, 1),
        (r.cross_out, r.cross_out_parts, 0),
    ]


def attention_kernel(levels, r):
    join_weights(attention_weights(r) + [(r.cross_kv, r.cross_kv_parts, 2)])
    join_positions(r.source, r.source_parts, r.place[0])
    join_positions(r.target, r.target_parts, r.place[0])
    join_positions(r.memory, r.memory_parts, r.place[0])
    counts = [r.counts[held_row(r), level] for level in range(levels)]
    glanced = glance_columns(row_of(r, r.tgt), row_of(r, r.priority), counts) > 0.5
    for first in range(0, r.x.shape[1], PAIR):
        cut = slice(first, first + PAIR)
        r.x[:, cut] = jnp.where(
            glanced, r.target[:, cut].astype(F32), r.source[:, cut].astype(F32)
        ).astype(BF16)
    length, tiles = r.x.shape[0], r.x.shape[0] // TILE
    self_start(r, r.x, row_of(r, r.tgt), r.near, r.far, r.q, r.k, r.v, levels)
    step = functools.partial(attend, r.q, r.k, r.v, r.far, r.near, r.sides, r.ctx, r.lse)
    window_loop(r.starts, window_base(r, tiles, 0), tiles, length, step)
    self_end(r, r.x, r.ctx, r.r1, r.a1, r.work)
    bias = joined(r.head_bias)
    r.k2[...] = dot_nn(r.memory[...], r.cross_kv[0]).astype(BF16)
    r.v2[...] = (dot_nn(r.memory[...], r.cross_kv[1]) + bias[3:4, :]).astype(BF16)
    cross_start(r, row_of(r, r.src), r.near, r.a1, r.q2, levels)
    step = functools.partial(attend, r.q2, r.k2, r.v2, r.far, r.near, r.sides, r.ctx2, r.lse2)
    window_loop(r.starts, window_base(r, tiles, 1), tiles, length, step)
    cross_end(r, r.ctx2, r.r2, r.work)


def feed_norm(r, r2_ref, a2_ref, work_ref):
    gain, shift = r.gain[1:2, :].astype(F32), r.shift[1:2, :].astype(F32)

    def step(tile):
        rows = tile_rows(tile)
        normed = norm_stats(r2_ref[rows, :])[0] * gain + shift
        work_ref[rows, :] = normed
        a2_ref[rows, :] = normed.astype(BF16)

    each_tile(r2_ref.shape[0] // TILE, step)


def feed_units(r, j, a2_ref, g_ref, slope_ref):
    units = r.ffn_in[j].shape[1]
    chunk = min(256, units)
    for first in range(0, units, chunk):
        cut = slice(first, first + chunk)
        pre = dot_nn(a2_ref[...], r.ffn_in[j][:, cut]) + r.ffn_bias[j][:, cut].astype(F32)
        phi, bell = gelu_parts(pre)
        cut = slice(j * units + first, j * units + first + chunk)
        g_ref[:, cut] = (pre * phi).astype(BF16)
        if slope_ref is not None:
            slope_ref[:, cut] = (phi + (pre * bell) * 0.3989422804014327).astype(BF16)


def feed_out(r, work_ref, g_ref):
    units = r.ffn_in[0].shape[1]
    fed = r.out_bias[2:3, :].astype(F32)
    for j in range(len(r.ffn_out)):
        fed = fed + dot_nn(g_ref[:, j * units : (j + 1) * units], r.ffn_out[j][...])
    work_ref[...] += fed


def add_grad(total_ref, left, right):
    total_ref[...] += dot_nn(left, right)


def start_totals(refs):
    @pl.when(pl.program_id(0) == 0)
    def clear():
        for ref in refs:
            ref[...] = jnp.zeros_like(ref)


def end_totals(pairs):
    @pl.when(pl.program_id(0) == pl.num_programs(0) - 1)
    def write():
        for total_ref, out_ref in pairs:
            share = out_ref.shape[2]
            for j in range(out_ref.shape[0]):
                out_ref[j] = total_ref[:, j * share : (j + 1) * share].astype(BF16)


def end_feed_totals(r):
    share = r.own_grads.shape[2]
    for which, total_ref in enumerate((r.in_total, r.out_total)):
        r.own_grads[which] = total_ref[:, 0:share].astype(BF16)
        for j, out_ref in enumerate(r.sent_grads):
            out_ref[which] = total_ref[:, (j + 1) * share : (j + 2) * share].astype(BF16)


def column_total(values):
    return jnp.sum(values.astype(F32), axis=0, keepdims=True)


def add_share(share_ref, row, values):
    share = share_ref.shape[2]
    for j in range(share_ref.shape[0]):
        share_ref[j, row : row + 1, :] += values[:, j * share : (j + 1) * share]


def feed_kernel(levels, r):
    length = r.r2.shape[0]
    units = r.ffn_in[0].shape[1]
    chunk = min(256, units)
    start_totals([r.in_total, r.out_total, r.common, r.shares])
    join_positions(r.cot, r.cot_parts, r.place[0])
    feed_norm(r, r.r2, r.a2, r.work)
    for j in range(len(r.ffn_in)):
        feed_units(r, j, r.a2, r.g, r.slope)
    feed_out(r, r.work, r.g)
    gain, shift = r.gain[...].astype(F32), r.shift[...].astype(F32)

    def last_norm(tile):
        rows = tile_rows(tile)
        normed, inverse = norm_stats(r.work[rows, :])
        r.second[rows, :] = (normed * gain[2:3, :] + shift[2:3, :]).astype(BF16)
        grad, gain_part, shift_part = norm_back(
            normed, inverse, gain[2:3, :], r.cot[rows, :].astype(F32)
        )
        r.work[rows, :] = grad
        low = grad.astype(BF16)
        r.df[rows, :] = low
        r.common[2:3, :] += column_total(low)
        r.common[5:6, :] += gain_part
        r.common[8:9, :] += shift_part

    each_tile(length // TILE, last_norm)
    spots = [(j, first) for j in range(len(r.ffn_in)) for first in range(0, units, chunk)]

    def product(spot):
        j, first = spot
        return dot_nt(r.df[...], r.ffn_out[j][first : first + chunk, :])

    share = r.shares.shape[2]
    following = product(spots[0])
    for index, (j, first) in enumerate(spots):
        hidden_grad = following.astype(BF16)
        if index + 1 < len(spots):
            following = product(spots[index + 1])
        cut = slice(j * units + first, j * units + first + chunk)
        pre_grad = (hidden_grad.astype(F32) * r.slope[:, cut].astype(F32)).astype(BF16)
        r.du[:, cut] = pre_grad
        sums = column_total(pre_grad)
        for piece in range(0, chunk, share):
            row = 4 + (first + piece) // share
            r.shares[j, row : row + 1, :] += sums[:, piece : piece + share]
    back = r.work[...]
    for j in range(len(r.ffn_in)):
        back = back + dot_nt(r.du[:, j * units : (j + 1) * units], r.ffn_in[j][...])
    r.work[...] = back

    def middle_norm(tile):
        rows = tile_rows(tile)
        normed, inverse = norm_stats(r.r2[rows, :])
        grad, gain_part, shift_part = norm_back(normed, inverse, gain[1:2, :], r.work[rows, :])
        r.dr2[rows, :] = grad
        low = grad.astype(BF16)
        r.common[1:2, :] += column_total(low)
        r.common[4:5, :] += gain_part
        r.common[7:8, :] += shift_part

    each_tile(length // TILE, middle_norm)
    hidden = r.du.shape[1]
    wide = min(512, hidden)

    def add_in():
        turned = r.a2[...].T
        for first in range(0, hidden, wide):
            cut = slice(first, first + wide)
            r.in_total[:, cut] += dot_nn(turned, r.du[:, cut])

    def add_out():
        turned = r.df[...].T
        for first in range(0, hidden, wide):
            cut = slice(first, first + wide)
            r.out_total[:, cut] += dot_nn(turned, r.g[:, cut])

    add_in()
    add_out()

    @pl.when(pl.program_id(0) == pl.num_programs(0) - 1)
    def write():
        end_feed_totals(r)


def cross_back_kernel(levels, r):
    tiles, width = r.dr2.shape[0] // TILE, r.dr2.shape[1]
    start_totals([r.total_q, r.total_k, r.total_v, r.total_o, r.common, r.shares])
    join_weights(
        [
            (r.cross_q, r.cross_q_parts, 1),
            (r.cross_kv, r.cross_kv_parts, 2),
            (r.cross_out, r.cross_out_parts, 0),
        ]
    )
    join_positions(r.memory, r.memory_parts, r.place[0])
    far, unused = make_marks(row_of(r, r.tgt), levels, width // HEAD_DIM)
    unused, near = make_marks(row_of(r, r.src), levels, width // HEAD_DIM)
    r.far[...] = far
    r.near[...] = near
    r.low[...] = r.dr2[...].astype(BF16)
    r.dctx[...] = dot_nt(r.low[...], r.cross_out[...]).astype(BF16)
    base = window_base(r, tiles, 1)
    attend_back(
        r.q2,
        r.k2,
        r.v2,
        r.far,
        r.near,
        r.sides,
        r.own,
        r.spread,
        r.lse2,
        r.ctx2,
        r.dctx,
        r.dq,
        r.dk,
        r.dv,
        r.starts,
        base,
    )
    r.dk_low[...] = r.dk[...].astype(BF16)
    r.dv_low[...] = r.dv[...].astype(BF16)
    r.memory_grad[...] = (
        dot_nt(r.dk_low[...], r.cross_kv[0]) + dot_nt(r.dv_low[...], r.cross_kv[1])
    ).astype(BF16)
    r.work[...] = r.dr2[...] + dot_nt(r.dq[...], r.cross_q[...])
    add_grad(r.total_o, r.low[...].T, r.ctx2[...])
    turned = r.memory[...].T
    add_grad(r.total_k, turned, r.dk_low[...])
    add_grad(r.total_v, turned, r.dv_low[...])
    add_grad(r.total_q, r.a1[...].T, r.dq[...])
    add_share(r.shares, 2, column_total(r.dq[...]))
    add_share(r.shares, 3, column_total(r.dv_low[...]))
    gain = r.gain[0:1, :].astype(F32)

    def first_norm(tile):
        rows = tile_rows(tile)
        normed, inverse = norm_stats(r.r1[rows, :])
        grad, gain_part, shift_part = norm_back(normed, inverse, gain, r.work[rows, :])
        r.dr1[rows, :] = grad
        r.common[0:1, :] += column_total(grad.astype(BF16))
        r.common[3:4, :] += gain_part
        r.common[6:7, :] += shift_part

    each_tile(tiles, first_norm)
    end_totals(
        [
            (r.total_q, r.cross_q_grad),
            (r.total_k, r.cross_k_grad),
            (r.total_v, r.cross_v_grad),
            (r.total_o, r.cross_out_grad),
        ]
    )


def self_back_kernel(levels, r):
    tiles, width = r.dr1.shape[0] // TILE, r.dr1.shape[1]
    start_totals([r.total_q, r.total_k, r.total_v, r.total_o, r.shares])
    join_weights([(r.self_qkv, r.self_qkv_parts, 2), (r.self_out, r.self_out_parts, 0)])
    far, near = make_marks(row_of(r, r.tgt), levels, width // HEAD_DIM)
    r.far[...] = far
    r.near[...] = near
    r.low[...] = r.dr1[...].astype(BF16)
    r.dctx[...] = dot_nt(r.low[...], r.self_out[...]).astype(BF16)
    attend_back(
        r.q,
        r.k,
        r.v,
        r.far,
        r.near,
        r.sides,
        r.own,
        r.spread,
        r.lse,
        r.ctx,
        r.dctx,
        r.dq,
        r.dk,
        r.dv,
        r.starts,
        window_base(r, tiles, 0),
    )
    r.dk_low[...] = r.dk[...].astype(BF16)
    r.dv_low[...] = r.dv[...].astype(BF16)
    r.input_grad[...] = (
        r.dr1[...]
        + (dot_nt(r.dq[...], r.self_qkv[0]) + dot_nt(r.dk_low[...], r.self_qkv[1]))
        + dot_nt(r.dv_low[...], r.self_qkv[2])
    ).astype(BF16)
    add_grad(r.total_o, r.low[...].T, r.ctx[...])
    turned = r.x[...].T
    add_grad(r.total_q, turned, r.dq[...])
    add_grad(r.total_k, turned, r.dk_low[...])
    add_grad(r.total_v, turned, r.dv_low[...])
    add_share(r.shares, 0, column_total(r.dq[...]))
    add_share(r.shares, 1, column_total(r.dv_low[...]))
    end_totals(
        [
            (r.total_q, r.self_q_grad),
            (r.total_k, r.self_k_grad),
            (r.total_v, r.self_v_grad),
            (r.total_o, r.self_out_grad),
        ]
    )


class Refs:
    pass


def call_rows(
    kernel,
    name,
    rows,
    levels,
    scalars,
    held_args,
    row_args,
    fixed_args,
    row_outs,
    fixed_outs,
    scratch,
):
    names, args, specs = [], [], []

    def put(key, array, kind):
        names.append(key)
        args.append(array)
        zeros = (0,) * (array.ndim if kind == "fixed" else array.ndim - 1)
        block = (None,) + array.shape[1:]
        if kind == "fixed":
            spec = pl.BlockSpec(array.shape, lambda row, *_: zeros, pipeline_mode=pl.Buffered(1))
        elif kind == "row":
            spec = pl.BlockSpec(block, lambda row, *_: (row,) + zeros)
        else:
            spec = pl.BlockSpec(block, lambda row, place, *_: (place[0] * rows + row,) + zeros)
        specs.append(spec)

    groups = [(held_args, "held"), (row_args, "row"), (fixed_args, "fixed")]
    for group, kind in groups:
        for key, value in group.items():
            if isinstance(value, tuple):
                for index, array in enumerate(value):
                    put((key, index), array, kind)
            else:
                put(key, value, kind)
    out_names, out_shapes, out_specs = [], [], []
    for key, (shape, kind) in row_outs.items():
        tail = (0,) * (len(shape) - 1)
        out_names.append(key)
        out_shapes.append(jax.ShapeDtypeStruct(shape, kind))
        out_specs.append(
            pl.BlockSpec((None,) + shape[1:], lambda row, *_, tail=tail: (row,) + tail)
        )
    for key, (shape, kind) in fixed_outs.items():
        zeros = (0,) * len(shape)
        out_names.append(key)
        out_shapes.append(jax.ShapeDtypeStruct(shape, kind))
        out_specs.append(pl.BlockSpec(shape, lambda row, *_, zeros=zeros: zeros))
    all_names = list(scalars) + names + out_names + list(scratch)

    def run(*refs):
        found = Refs()
        for key, ref in zip(all_names, refs):
            if isinstance(key, tuple):
                if not hasattr(found, key[0]):
                    setattr(found, key[0], [])
                getattr(found, key[0]).append(ref)
            else:
                setattr(found, key, ref)
        kernel(levels, found)

    outs = pl.pallas_call(
        run,
        grid_spec=pltpu.PrefetchScalarGridSpec(
            num_scalar_prefetch=len(scalars),
            grid=(rows,),
            in_specs=specs,
            out_specs=tuple(out_specs),
            scratch_shapes=[pltpu.VMEM(shape, kind) for shape, kind in scratch.values()],
        ),
        out_shape=tuple(out_shapes),
        compiler_params=pltpu.CompilerParams(
            dimension_semantics=("arbitrary",),
            vmem_limit_bytes=VMEM_BYTES,
        ),
        cost_estimate=pl.CostEstimate(flops=1000, bytes_accessed=1000, transcendentals=0),
        name=name,
    )(*scalars.values(), *args)
    return dict(zip(out_names, outs))


def from_peer(values, size, step):
    return lax.ppermute(values, AXIS, [((i + step) % size, i) for i in range(size)])


def own_first(values, size):
    return tuple([values] + [from_peer(values, size, step) for step in range(1, size)])


def opening_kernel(head_size, count, rows, *refs):
    arrays, refs = refs[:count], refs[count:]
    landing, (send_sem, recv_sem) = refs[:-2], refs[-2:]
    me = lax.axis_index(AXIS)
    barrier = pltpu.get_barrier_semaphore()
    for j in range(1, head_size):
        pl.semaphore_signal(
            barrier,
            inc=1,
            device_id=dict(head=(me + j) % head_size),
            device_id_type=pl.DeviceIdType.MESH,
        )
    pl.semaphore_wait(barrier, head_size - 1)
    copies = []
    for i, array in enumerate(arrays):
        for j in range(1, head_size):
            target = (me + head_size - j) % head_size
            copies.append(
                pltpu.make_async_remote_copy(
                    src_ref=array.at[pl.ds(target * rows, rows)] if i < 3 else array,
                    dst_ref=landing[i * (head_size - 1) + j - 1],
                    send_sem=send_sem.at[j - 1, i],
                    recv_sem=recv_sem.at[j - 1, i],
                    device_id=dict(head=target),
                    device_id_type=pl.DeviceIdType.MESH,
                )
            )
    for copy in copies:
        copy.start()
    for copy in copies:
        copy.wait()


def opening(positions, weights, rows, head_size):
    arrays = positions + weights
    if head_size == 1:
        return [(array,) for array in arrays]
    outs = []
    for i, array in enumerate(arrays):
        shape = ((rows,) + array.shape[1:]) if i < len(positions) else array.shape
        outs += [jax.ShapeDtypeStruct(shape, array.dtype)] * (head_size - 1)
    semaphores = pltpu.SemaphoreType.DMA((head_size - 1, len(arrays)))
    landed = pl.pallas_call(
        functools.partial(opening_kernel, head_size, len(arrays), rows),
        out_shape=tuple(outs),
        in_specs=[pl.BlockSpec(memory_space=pl.ANY)] * len(arrays),
        out_specs=(pl.BlockSpec(memory_space=pl.ANY),) * len(outs),
        scratch_shapes=[semaphores, semaphores],
        compiler_params=pltpu.CompilerParams(collective_id=2, has_side_effects=True),
        name="opening",
    )(*arrays)
    step = head_size - 1
    return [(array, *landed[i * step : (i + 1) * step]) for i, array in enumerate(arrays)]


def stage_orders(dp_size):
    bits = [1 << b for b in range(dp_size.bit_length() - 1)]
    return bits, bits[:2][::-1] + bits[2:]


def closing_kernel(dp_size, head_size, count, results, levels, *refs):
    refs = list(refs)

    def take(number):
        taken = refs[:number]
        del refs[:number]
        return taken

    grads = take(count)
    rows_in = take(results)
    source_in, keys_in, feed_in = take(head_size), take(2), take(2 * head_size)
    r = Refs()
    r.out_bias, r.gain, r.shift, r.sides, tgt_ref, src_ref = take(6)
    r.ffn_bias, r.head_bias = take(head_size), take(head_size)
    r.self_qkv_parts, r.self_out_parts = take(head_size), take(head_size)
    r.cross_q_parts, r.cross_out_parts = take(head_size), take(head_size)
    common_one, common_two, share_one, share_two, share_three = take(5)
    out_ref, small_out_ref, first_ref = take(3)
    rows_out = take(results + 1)
    head_land, land, small_land, small_ref, sum_ref = take(5)
    source_ref, k2_ref, v2_ref, ffn_in_ref, ffn_out_ref, low_ref, work_ref, g_ref = take(8)
    x_ref, q_ref, k_ref, v_ref, ctx_ref, sums_ref, far_ref, near_ref = take(8)
    r.self_qkv, r.self_out, r.cross_q, r.cross_out = take(4)
    r.ffn_in = [ffn_in_ref.at[j] for j in range(head_size)]
    r.ffn_out = [ffn_out_ref.at[j] for j in range(head_size)]
    (
        local_sem,
        head_send,
        head_recv,
        fold_send,
        fold_recv,
        grow_send,
        grow_recv,
        small_send,
        small_recv,
        rows_send,
        rows_recv,
        feed_sem,
    ) = refs
    length = out_ref.shape[1]
    me, spot = lax.axis_index(AXIS), lax.axis_index("dp")
    held, positions = rows_out[0].shape[0] // head_size, rows_out[0].shape[1]
    mine = pl.ds(me * held, held)
    moves = [
        (part if j > 0 else part.at[mine], source_ref.at[j]) for j, part in enumerate(source_in)
    ]
    moves += [(keys_in[0], k2_ref), (keys_in[1], v2_ref)]
    moves += list(zip(feed_in, r.ffn_in + r.ffn_out))
    loads = [
        pltpu.make_async_copy(source, target, feed_sem.at[i])
        for i, (source, target) in enumerate(moves)
    ]
    for copy in loads:
        copy.start()
    orders = stage_orders(dp_size)
    depth = len(orders[0])

    def digit(stride):
        return (spot // stride) % 2

    def partner(stride):
        return spot + (1 - 2 * digit(stride)) * stride

    share = out_ref.shape[2]
    for j in range(head_size):
        small_ref[j, 0:16, :] = common_one[...] + common_two[...]
        small_ref[j, 16:24, 0:share] = share_one[j] + share_two[j] + share_three[j]
        if share < small_ref.shape[2]:
            small_ref[j, 16:24, share:] = jnp.zeros((8, small_ref.shape[2] - share), F32)
    peers = [(me + step) % head_size for step in range(1, head_size)]
    barrier = pltpu.get_barrier_semaphore()
    for peer in peers:
        pl.semaphore_signal(
            barrier, inc=1, device_id=dict(head=peer), device_id_type=pl.DeviceIdType.MESH
        )
    for stride in orders[0]:
        pl.semaphore_signal(
            barrier, inc=1, device_id=dict(dp=partner(stride)), device_id_type=pl.DeviceIdType.MESH
        )

    def remote(source, target, send, recv, where):
        return pltpu.make_async_remote_copy(
            src_ref=source,
            dst_ref=target,
            send_sem=send,
            recv_sem=recv,
            device_id=where,
            device_id_type=pl.DeviceIdType.MESH,
        )

    queue = [i for pair in zip(range(count // 2), range(count // 2, count)) for i in pair]
    small_head = [
        remote(
            small_ref.at[j + 1],
            small_land.at[j],
            small_send.at[j],
            small_recv.at[j],
            dict(head=peer),
        )
        for j, peer in enumerate(peers)
    ]
    trades = []

    def trade(source, target, j, i):
        there = pl.ds(pl.multiple_of(peers[j] * positions, positions), positions)
        copy = remote(
            source.at[:, there, :], target, rows_send.at[j, i], rows_recv.at[j, i], dict(head=peers[j])
        )
        copy.start()
        trades.append(copy)

    tiles = x_ref.shape[0] // TILE

    def row_start(row):
        if row == 0:
            join_all(attention_weights(r))
            for copy in loads[:head_size]:
                copy.wait()
        join_positions(x_ref, [source_ref.at[j, row] for j in range(head_size)], me)
        segment_row = tgt_ref[pl.ds(me * held + row, 1), :]
        self_start(r, x_ref, segment_row, near_ref, far_ref, q_ref, k_ref, v_ref, levels)

    def self_tile(tile):
        start, end = max(0, tile - 1) * TILE, min(tiles, tile + 2) * TILE
        attend(
            q_ref, k_ref, v_ref, far_ref, near_ref, r.sides, ctx_ref, None, tile, start, end - start
        )

    def row_middle(row):
        self_end(r, x_ref, ctx_ref, None, low_ref, work_ref)
        segment_row = src_ref[pl.ds(me * held + row, 1), :]
        cross_start(r, segment_row, near_ref, low_ref, q_ref, levels)
        if row == 0:
            for copy in loads[head_size : head_size + 2]:
                copy.wait()

    def cross_tile(row, tile):
        keys, values = k2_ref.at[row], v2_ref.at[row]
        attend(
            q_ref, keys, values, far_ref, near_ref, r.sides, ctx_ref, None, tile, 0, x_ref.shape[0]
        )

    def feed_start(row):
        cross_end(r, ctx_ref, sums_ref, work_ref)
        feed_norm(r, sums_ref, low_ref, work_ref)
        if row == 0:
            for copy in loads[head_size + 2 :]:
                copy.wait()

    def feed_middle(j):
        feed_units(r, j, low_ref, g_ref, None)

    def feed_end(row):
        feed_out(r, work_ref, g_ref)
        gain, shift = r.gain[2:3, :].astype(F32), r.shift[2:3, :].astype(F32)
        for tile in range(work_ref.shape[0] // TILE):
            rows = tile_rows(tile)
            normed = norm_stats(work_ref[rows, :])[0]
            first_ref[row, rows, :] = (normed * gain + shift).astype(BF16)
        for j in range(len(peers)):
            trade(
                first_ref.at[pl.ds(row, 1)],
                rows_out[0].at[pl.ds(me * held + row, 1)],
                j,
                results + row,
            )

    pieces = []
    for row in range(held):
        pieces.append(functools.partial(row_start, row))
        pieces += [functools.partial(self_tile, tile) for tile in range(tiles)]
        pieces.append(functools.partial(row_middle, row))
        pieces += [functools.partial(cross_tile, row, tile) for tile in range(tiles)]
        pieces.append(functools.partial(feed_start, row))
        pieces += [functools.partial(feed_middle, j) for j in range(head_size)]
        pieces.append(functools.partial(feed_end, row))
    early = min(EARLY, len(pieces))
    for piece in pieces[:early]:
        piece()
    pieces = pieces[early:]
    pl.semaphore_wait(barrier, len(peers) + depth)
    for copy in small_head:
        copy.start()
    locals_, heads_ = {}, {}
    for i in queue:
        locals_[i] = pltpu.make_async_copy(grads[i].at[0], sum_ref.at[i], local_sem.at[i])
        locals_[i].start()
        heads_[i] = [
            remote(
                grads[i].at[j + 1],
                head_land.at[j, i],
                head_send.at[j, i],
                head_recv.at[j, i],
                dict(head=peer),
            )
            for j, peer in enumerate(peers)
        ]
        for copy in heads_[i]:
            copy.start()

    for i in range(results):
        for j in range(len(peers)):
            trade(rows_in[i], rows_out[i + 1].at[mine], j, i)

    def places(i):
        order = orders[0] if i < count // 2 else orders[1]
        offset, size, result = 0, length, []
        for stride in order:
            size //= 2
            keep = offset + digit(stride) * size
            give = offset + (1 - digit(stride)) * size
            result.append((stride, size, pl.multiple_of(keep, 16), pl.multiple_of(give, 16)))
            offset = keep
        return result

    plan = {i: places(i) for i in range(count)}
    moving = {}

    def fold(i, stage):
        stride, size, keep, give = plan[i][stage]
        base = length - (length >> stage)
        copy = remote(
            sum_ref.at[i, pl.ds(give, size), :],
            land.at[i, pl.ds(base, size), :],
            fold_send.at[stage, i],
            fold_recv.at[stage, i],
            dict(dp=partner(stride)),
        )
        copy.start()
        moving[i] = copy

    def grow(i, stage):
        stride, size, keep, give = plan[i][stage]
        rows = out_ref.at[i, pl.ds(keep, size), :]
        copy = remote(
            rows, rows, grow_send.at[stage, i], grow_recv.at[stage, i], dict(dp=partner(stride))
        )
        copy.start()
        moving[i] = copy

    def task(i, number):
        if number == 0:
            locals_[i].wait()
            total = sum_ref[i].astype(F32)
            for j, copy in enumerate(heads_[i]):
                copy.wait()
                total = total + head_land[j, i].astype(F32)
            sum_ref[i] = total.astype(BF16)
            fold(i, 0)
        elif number <= depth:
            moving[i].wait()
            stage = number - 1
            stride, size, keep, give = plan[i][stage]
            base = length - (length >> stage)
            rows = pl.ds(keep, size)
            total = (
                sum_ref[i, rows, :].astype(F32) + land[i, pl.ds(base, size), :].astype(F32)
            ).astype(BF16)
            if number < depth:
                sum_ref[i, rows, :] = total
                fold(i, number)
            else:
                out_ref[i, rows, :] = total
                grow(i, depth - 1)
        else:
            moving[i].wait()
            stage = 2 * depth - number
            if stage > 0:
                grow(i, stage - 1)

    steps = 2 * depth + 1
    small_moving = []

    def small_task(number):
        if number == 0:
            total = small_ref[0]
            for j, copy in enumerate(small_head):
                copy.wait()
                total = total + small_land[j]
            small_out_ref[...] = total
        else:
            small_moving.pop().wait()
            small_out_ref[...] += small_land[len(peers) + number - 1]
        if number < depth:
            slot = len(peers) + number
            copy = remote(
                small_out_ref,
                small_land.at[slot],
                small_send.at[slot],
                small_recv.at[slot],
                dict(dp=partner(orders[0][number])),
            )
            copy.start()
            small_moving.append(copy)

    times = steps + count // 2 - 1
    for time in range(times):
        if time <= depth:
            small_task(time)
        for place, i in enumerate(queue):
            if 0 <= time - place // 2 < steps:
                task(i, time - place // 2)
        first, last = (min(n, times - 1) * len(pieces) // (times - 1) for n in (time, time + 1))
        for piece in pieces[first:last]:
            piece()
    for copy in trades:
        copy.wait()


def close(grads, common, shares, arrays, source, keys, segments, weights, levels, dp_size, head_size):
    count, results = len(grads), len(arrays)
    rows, positions, width = arrays[0].shape
    traded = jax.ShapeDtypeStruct((rows * head_size, positions // head_size, width), BF16)
    length, share = grads[0].shape[1:]
    depth = dp_size.bit_length() - 1
    peers = head_size - 1
    small = (24, common[0].shape[1])
    any_spec = pl.BlockSpec(memory_space=pl.ANY)
    vmem = pl.BlockSpec(memory_space=pltpu.VMEM)
    dma = pltpu.SemaphoreType.DMA
    return pl.pallas_call(
        functools.partial(closing_kernel, dp_size, head_size, count, results, levels),
        out_shape=(
            jax.ShapeDtypeStruct((count, length, share), BF16),
            jax.ShapeDtypeStruct(small, F32),
            jax.ShapeDtypeStruct(arrays[0].shape, BF16),
        )
        + (traded,) * (results + 1),
        in_specs=[any_spec] * (count + results + 3 * head_size + 2) + [vmem] * (11 + 6 * head_size),
        out_specs=(vmem, vmem, vmem) + (any_spec,) * (results + 1),
        scratch_shapes=[
            pltpu.VMEM((peers, count, length, share), BF16),
            pltpu.VMEM((count, length, share), BF16),
            pltpu.VMEM((peers + depth,) + small, F32),
            pltpu.VMEM((head_size,) + small, F32),
            pltpu.VMEM((count, length, share), BF16),
            pltpu.VMEM((head_size, rows, positions // head_size, width), BF16),
            pltpu.VMEM((rows, positions, width), BF16),
            pltpu.VMEM((rows, positions, width), BF16),
            pltpu.VMEM((head_size,) + weights["ffn_in"][0].shape, BF16),
            pltpu.VMEM((head_size,) + weights["ffn_out"][0].shape, BF16),
            pltpu.VMEM((positions, width), BF16),
            pltpu.VMEM((positions, width), F32),
            pltpu.VMEM((positions, head_size * weights["ffn_in"][0].shape[1]), BF16),
        ]
        + [pltpu.VMEM((positions, width), BF16)] * 5
        + [
            pltpu.VMEM((positions, width), F32),
            pltpu.VMEM((positions, PAIR), BF16),
            pltpu.VMEM((positions, PAIR), BF16),
            pltpu.VMEM((3, width, width), BF16),
            pltpu.VMEM((width, width), BF16),
            pltpu.VMEM((width, width), BF16),
            pltpu.VMEM((width, width), BF16),
            dma((count,)),
            dma((peers, count)),
            dma((peers, count)),
            dma((depth, count)),
            dma((depth, count)),
            dma((depth, count)),
            dma((depth, count)),
            dma((peers + depth,)),
            dma((peers + depth,)),
            dma((peers, results + rows)),
            dma((peers, results + rows)),
            dma((2 + 3 * head_size,)),
        ],
        compiler_params=pltpu.CompilerParams(
            collective_id=0, has_side_effects=True, vmem_limit_bytes=VMEM_BYTES
        ),
        name="closing",
    )(
        *grads,
        *arrays,
        *source,
        *keys,
        *weights["ffn_in"],
        *weights["ffn_out"],
        weights["out_bias"],
        weights["gain"],
        weights["shift"],
        constants(width, levels)["sides"],
        *segments,
        *weights["ffn_bias"],
        *weights["head_bias"],
        *weights["self_qkv"],
        *weights["self_out"],
        *weights["cross_q"],
        *weights["cross_out"],
        *common,
        *shares,
    )


def finish_kernel(results, *refs):
    place_ref, refs = refs[0], list(refs[1:])

    def take(number):
        taken = refs[:number]
        del refs[:number]
        return taken

    own, arrived = take(results), take(results)
    summed_ref, feed_in_ref, feed_out_ref, sums_ref = take(4)
    rows_out = take(results)
    qkv_ref, kv_ref, self_out_ref, cross_q_ref, cross_out_ref, ffn_in_ref, ffn_out_ref = take(7)
    head_bias_ref, ffn_bias_ref, out_bias_ref, gain_ref, shift_ref = take(5)
    step = pl.program_id(0)
    rows = pl.num_programs(0) // place_ref[1]
    mine = step // rows == place_ref[0]
    for i in range(results):
        rows_out[i][...] = jnp.where(mine, own[i][...], arrived[i][...])
    ffn_in_ref[...] = feed_in_ref[...].astype(F32)
    ffn_out_ref[...] = feed_out_ref[...].astype(F32).T

    @pl.when(step == 0)
    def small():
        share = head_bias_ref.shape[1]
        head_bias_ref[...] = sums_ref[16:20, 0:share]
        for j in range(4):
            ffn_bias_ref[0:1, j * share : (j + 1) * share] = sums_ref[20 + j : 21 + j, 0:share]
        out_bias_ref[...] = sums_ref[0:3, :]
        gain_ref[...] = sums_ref[3:6, :]
        shift_ref[...] = sums_ref[6:9, :]

    def at(number, target_ref, turned):
        @pl.when(step == number)
        def write():
            values = summed_ref[...].astype(F32)
            target_ref[...] = values.T if turned else values

    for number, (target_ref, turned) in enumerate(
        [(cross_q_ref, False), (kv_ref, False), (kv_ref, False), (cross_out_ref, True)]
        + [(qkv_ref, False)] * 3
        + [(self_out_ref, True)]
    ):
        at(number, target_ref, turned)


def finish(place, arrays, arrived, summed, feed_grads, sums, head_size):
    results = len(arrays)
    rows, length, width = arrays[0].shape
    held, positions = rows * head_size, length // head_size
    share, units = summed.shape[2], feed_grads.shape[2]
    steps = summed.shape[0]
    if held != steps:
        raise ValueError(held)
    pieces = max(1, min(steps, units // 128))
    small = ((4, share), (1, 4 * share), (3, width), (3, width), (3, width))
    tall, wide = width // steps, units // pieces

    def clip(step, low, high):
        return jnp.clip(step - low, 0, high)

    def own_row(step, place):
        return (jnp.clip(step - place[0] * rows, 0, rows - 1), place[0], 0)

    def arrived_row(step, place):
        other = ((place[0] + 1) % place[1]) * rows
        return (jnp.where(step // rows == place[0], other, step), 0, 0)

    block = (None, positions, width)
    return pl.pallas_call(
        functools.partial(finish_kernel, results),
        grid_spec=pltpu.PrefetchScalarGridSpec(
            num_scalar_prefetch=1,
            grid=(steps,),
            in_specs=[pl.BlockSpec(block, own_row)] * results
            + [pl.BlockSpec(block, arrived_row)] * results
            + [
                pl.BlockSpec((None, width, share), lambda step, _: (step, 0, 0)),
                pl.BlockSpec((None, tall, units), lambda step, _: (0, step, 0)),
                pl.BlockSpec(
                    (None, width, wide), lambda step, _: (1, 0, clip(step, 0, pieces - 1))
                ),
                pl.BlockSpec(sums.shape, lambda step, _: (0, 0)),
            ],
            out_specs=(pl.BlockSpec(block, lambda step, _: (step, 0, 0)),) * results
            + (
                pl.BlockSpec((None, width, share), lambda step, _: (clip(step, 4, 2), 0, 0)),
                pl.BlockSpec((None, width, share), lambda step, _: (clip(step, 1, 1), 0, 0)),
                pl.BlockSpec((share, width), lambda step, _: (0, 0)),
                pl.BlockSpec((width, share), lambda step, _: (0, 0)),
                pl.BlockSpec((share, width), lambda step, _: (0, 0)),
                pl.BlockSpec((tall, units), lambda step, _: (step, 0)),
                pl.BlockSpec((wide, width), lambda step, _: (clip(step, 0, pieces - 1), 0)),
            )
            + tuple(pl.BlockSpec(shape, lambda step, _: (0, 0)) for shape in small),
        ),
        out_shape=(jax.ShapeDtypeStruct((held, positions, width), BF16),) * results
        + tuple(
            jax.ShapeDtypeStruct(shape, F32)
            for shape in (
                (3, width, share),
                (2, width, share),
                (share, width),
                (width, share),
                (share, width),
                (width, units),
                (units, width),
            )
            + small
        ),
        compiler_params=pltpu.CompilerParams(
            dimension_semantics=("arbitrary",), vmem_limit_bytes=VMEM_BYTES
        ),
        name="finish",
    )(place, *arrays, *arrived, summed, feed_grads, feed_grads, sums)


def window_starts(query_segments, key_segments, window):
    rows, length = query_segments.shape
    tiles = query_segments.reshape(rows, length // TILE, TILE)
    first, last = tiles[:, :, 0], tiles[:, :, -1]
    before = jnp.sum(key_segments[:, None, :] < first[:, :, None], axis=2).astype(jnp.int32)
    after = jnp.sum(key_segments[:, None, :] <= last[:, :, None], axis=2).astype(jnp.int32)
    start = jnp.minimum((before // 16) * 16, key_segments.shape[1] - window)
    return jnp.where(after - start <= window, start, -1).reshape(-1)


def constants(width, levels):
    heads = width // HEAD_DIM
    lane = np.arange(PAIR)
    sides = np.stack([lane < HEAD_DIM, lane >= HEAD_DIM])
    kept = (lane >= 16) & (lane < 16 + 3 * heads)
    own = np.stack([(lane < levels) | (kept & ((lane - 16) % heads == h)) for h in range(heads)])
    spread = kept[None, :] & (
        (lane[None, :] - 16) % heads == np.arange(width)[:, None] // HEAD_DIM
    )

    def tall(rows):
        return jnp.asarray(np.broadcast_to(rows[:, None, :], (rows.shape[0], TILE, PAIR)), BF16)

    return dict(sides=tall(sides), own=tall(own), spread=jnp.asarray(spread, BF16))


def local_layer(
    place,
    rows,
    source,
    target,
    priority,
    counts,
    memory,
    cotangent,
    tgt_segments,
    src_segments,
    levels,
    weights,
    feed_total,
):
    head_size = len(weights["ffn_in"])
    held, length = tgt_segments.shape
    width = source[0].shape[2]
    hidden = weights["ffn_in"][0].shape[1] * head_size
    heads = width // HEAD_DIM
    tiles = length // TILE
    window = min(WINDOW, length)
    share = width // head_size
    marks = constants(width, levels)
    sides = dict(sides=marks["sides"])
    alone = dict(place=place)
    starts = alone | dict(starts=jnp.concatenate(
            [
                window_starts(tgt_segments, tgt_segments, window),
                window_starts(tgt_segments, src_segments, window),
            ]
        ))
    tgt = dict(tgt=tgt_segments)
    src = dict(src=src_segments)

    def pick(*keys):
        return {key: weights[key] for key in keys}

    def parts_of(*keys):
        return {key + "_parts": weights[key] for key in keys}

    wide_low = ((rows, length, width), BF16)
    wide = ((rows, length, width), F32)
    stats = ((rows, tiles, heads, TILE), F32)
    one_low, one = ((length, width), BF16), ((length, width), F32)
    mark = ((length, PAIR), BF16)
    square, square_low = ((width, width), F32), ((width, width), BF16)
    split = ((head_size, width, share), BF16)
    common, shares = ((16, width), F32), ((head_size, 8, share), F32)
    norms = pick("out_bias", "gain", "shift")
    feed = pick("ffn_in", "ffn_out", "ffn_bias")
    self_qkv = dict(self_qkv=((3, width, width), BF16))
    cross_kv = dict(cross_kv=((2, width, width), BF16))
    marks_scratch = dict(far=mark, near=mark)
    half = ((2, width, hidden // head_size), BF16)
    kept = call_rows(
        attention_kernel,
        "attention",
        rows,
        levels,
        starts | dict(counts=counts),
        dict(source_parts=source[:1], target_parts=target[:1], memory_parts=memory[:1]),
        {("source_parts", j): part for j, part in enumerate(source[1:])}
        | {("target_parts", j): part for j, part in enumerate(target[1:])}
        | {("memory_parts", j): part for j, part in enumerate(memory[1:])},
        sides
        | dict(priority=priority)
        | tgt
        | src
        | parts_of("self_qkv", "self_out", "cross_q", "cross_kv", "cross_out")
        | pick("head_bias")
        | norms,
        {key: wide_low for key in ("x", "q", "k", "v", "ctx", "a1", "q2", "k2", "v2", "ctx2")}
        | dict(lse=stats, lse2=stats, r1=wide, r2=wide),
        {},
        dict(work=one, source=one_low, target=one_low, memory=one_low)
        | {key: square_low for key in ("self_out", "cross_q", "cross_out")}
        | self_qkv
        | cross_kv
        | marks_scratch,
    )
    fed = call_rows(
        feed_kernel,
        "feed",
        rows,
        levels,
        alone,
        dict(cot_parts=cotangent),
        dict(r2=kept["r2"]),
        feed | norms,
        dict(second=wide_low, dr2=wide),
        dict(own_grads=half, common=common, shares=shares)
        | {("sent_grads", j): half for j in range(1, head_size)},
        dict(cot=one_low, a2=one_low, df=one_low, work=one, g=((length, hidden), BF16), du=((length, hidden), BF16), slope=((length, hidden), BF16), in_total=((width, hidden), F32), out_total=((width, hidden), F32)),
    )
    sent = [fed[("sent_grads", j)] for j in range(1, head_size)]
    dr2, feed_grads = feed_total(fed["dr2"], fed["own_grads"], sent)
    totals = {"total_" + key: square for key in "qkvo"}
    back_scratch = (
        totals
        | marks_scratch
        | {key: one_low for key in ("dctx", "low", "dq", "dk_low", "dv_low")}
        | dict(dk=one, dv=one)
    )
    crossed = call_rows(
        cross_back_kernel,
        "cross_back",
        rows,
        levels,
        starts,
        dict(memory_parts=memory[:1]),
        {key: kept[key] for key in ("q2", "k2", "v2", "ctx2", "lse2", "r1", "a1")}
        | dict(dr2=dr2)
        | {("memory_parts", j): part for j, part in enumerate(memory[1:])},
        marks | tgt | src | parts_of("cross_q", "cross_kv", "cross_out") | pick("gain"),
        dict(memory_grad=wide_low, dr1=wide),
        {key: split for key in ("cross_q_grad", "cross_k_grad", "cross_v_grad", "cross_out_grad")}
        | dict(common=common, shares=shares),
        back_scratch
        | cross_kv
        | dict(work=one, memory=one_low, cross_q=square_low, cross_out=square_low),
    )
    selfed = call_rows(
        self_back_kernel,
        "self_back",
        rows,
        levels,
        starts,
        {},
        {key: kept[key] for key in ("x", "q", "k", "v", "ctx", "lse")}
        | dict(dr1=crossed["dr1"]),
        marks | tgt | parts_of("self_qkv", "self_out"),
        dict(input_grad=wide_low),
        {key: split for key in ("self_q_grad", "self_k_grad", "self_v_grad", "self_out_grad")}
        | dict(shares=shares),
        back_scratch | self_qkv | dict(self_out=square_low),
    )
    grads = tuple(
        crossed[key] for key in ("cross_q_grad", "cross_k_grad", "cross_v_grad", "cross_out_grad")
    ) + tuple(selfed[key] for key in ("self_q_grad", "self_k_grad", "self_v_grad", "self_out_grad"))
    return (
        (kept["k2"], kept["v2"]),
        (fed["second"], selfed["input_grad"], crossed["memory_grad"]),
        feed_grads,
        grads,
        (fed["common"], crossed["common"]),
        (fed["shares"], crossed["shares"], selfed["shares"]),
    )


def body(
    dp_size,
    head_size,
    source_copy,
    target_embed,
    memory,
    tgt_segments,
    src_segments,
    hamming,
    priority,
    cotangent,
    self_qkv,
    self_out,
    cross_q,
    cross_kv,
    cross_out,
    ffn_in,
    ffn_out,
    head_bias,
    ffn_bias,
    out_bias,
    norm_gain,
    norm_shift,
):
    me = lax.axis_index(AXIS)
    levels = hamming.shape[1]
    held = source_copy.shape[0]
    rows = held // head_size

    source, target, memory, self_qkv, self_out, cross_q, cross_kv, cross_out = opening(
        [source_copy, target_embed, memory],
        [self_qkv, self_out, cross_q, cross_kv, cross_out],
        rows,
        head_size,
    )
    weights = dict(self_qkv=self_qkv, self_out=self_out, cross_q=cross_q, cross_kv=cross_kv, cross_out=cross_out, head_bias=own_first(head_bias, head_size), out_bias=out_bias, gain=norm_gain, shift=norm_shift)
    ffn_bias, ffn_in, ffn_out, cotangent, memory, weights["head_bias"] = lax.optimization_barrier(
        (ffn_bias, ffn_in, ffn_out, cotangent, memory, weights["head_bias"])
    )
    weights["ffn_bias"] = own_first(ffn_bias[None, :], head_size)
    weights["ffn_in"] = own_first(ffn_in, head_size)
    weights["ffn_out"] = own_first(ffn_out, head_size)

    def feed_total(later, own, sent):
        total = own.astype(F32)
        for j, part in enumerate(sent):
            total = total + from_peer(part, head_size, head_size - 1 - j).astype(F32)
        later, total = lax.optimization_barrier((later, total.astype(BF16)))
        return later, lax.psum(total, "dp")

    keys, arrays, feed_grads, grads, common, shares = local_layer(
        me.astype(jnp.int32).reshape(1),
        rows,
        source,
        target,
        priority,
        hamming,
        memory,
        own_first(cotangent, head_size),
        tgt_segments,
        src_segments,
        levels,
        weights,
        feed_total,
    )
    summed, sums, first, *arrived = close(
        grads,
        common,
        shares,
        arrays,
        source,
        keys,
        (tgt_segments, src_segments),
        weights,
        levels,
        dp_size,
        head_size,
    )
    place = jnp.stack([me.astype(jnp.int32), jnp.int32(head_size)])
    done = finish(place, (first, *arrays), arrived, summed, feed_grads, sums, head_size)
    *outs, qkv, kv, self_out, cross_q, cross_out, ffn_in, ffn_out = done[:-5]
    head_bias, ffn_bias, out_bias, gain, shift = done[-5:]
    return (
        *outs,
        qkv,
        self_out,
        cross_q,
        kv,
        cross_out,
        ffn_in,
        ffn_out,
        head_bias,
        ffn_bias.reshape(-1),
        out_bias,
        gain,
        shift,
    )


def solution(mesh):
    split = P("dp", AXIS, None)
    rows = P("dp", None)
    last, last_two, first = P(None, AXIS), P(None, None, AXIS), P(AXIS, None)
    return jax.shard_map(
        functools.partial(body, mesh.shape["dp"], mesh.shape[AXIS]),
        mesh=mesh,
        in_specs=(split, split, split, rows, rows, rows, rows, split)
        + (last_two, first, last, last_two, first, last, first, last, P(AXIS), P(), P(), P()),
        out_specs=(split, split, split, split)
        + (last_two, first, last, last_two, first, last, first, last, P(AXIS), P(), P(), P()),
        check_vma=False,
    )
```
